128 devices in a mesh: actor: 4 (over z_lo, core), learn: 32 (over z_hi, x, y).
Axes of the slice: x: 4, y: 4, z: 4 (z_hi: 2, z_lo: 2; z = z_hi * 2 + z_lo), core: 2. Of those that a mesh axis runs over, the one named last changes fastest.
Arguments:
- rec_weight: bfloat16 [2048, 4, 2048], P('learn', None, 'actor'), may hold values from -0.4375 to 0.4375
- head_weight: bfloat16 [2048, 128], P('learn'), may hold values from -0.125 to 0.125
- value_head: bfloat16 [2048], P('learn'), may hold values from -0.25 to 0.25
- gate_inputs: bfloat16 [32, 64, 16, 4, 2048], P('learn', None, None, None, 'actor'), may hold values from -3 to 3
- start_state: bfloat16 [32, 64, 2, 2048], P('learn', None, None, 'actor'), may hold values from -3 to 3
- advantages: bfloat16 [32, 64, 16], P('learn'), may hold values from -6 to 6
- returns: bfloat16 [32, 64, 16], P('learn'), may hold values from -6 to 6
- old_logprob: bfloat16 [32, 64, 16], P('learn'), may hold values from -5.375 to -4.28125
- taken_action: int32 [32, 64, 16], P('learn'), may hold values from 0 to 127
- episode_start: int32 [32, 64, 16], P('learn'), may hold values 0 or 1
- segment_counts: int32 [32], replicated, may hold values from 1 to 64, 1024 in all
- assignment: int32 [32, 64], P('learn'), may hold values from 0 to 31, as said below
Outputs:
- grad_rec: float32 [2048, 4, 2048], P('learn', None, 'actor')
- grad_policy: float32 [2048, 128], P('learn')
- grad_value: float32 [2048], P('learn')
- learner_values: float32 [32, 64, 16], P('learn')
The draws below stay inside these ranges and needn't reach their ends.
Inputs may be any that keep to these rules, and one draw needn't show every extreme that they name: `segment_counts`: only slots below a group's count hold live segments; the counts sum to 1024 and the largest equals 64. `assignment`: each group's row names every learner exactly 2 times.
All inputs are finite; a program needn't handle non-finite values. No bound on the sum of `episode_start` on one device may be relied on, other than what follows from the above.
Results may differ from the reference program's by a relative error of at most 0.038.
Values may be sent and summed in bfloat16 or wider, within the bound.
A program may use at most 128 MiB of HBM per device.

```python
import math
import jax
import jax.numpy as jnp
import numpy as np
from jax import lax

UNITS = 2048
CHOICES = 128
STEPS = 16
BATCH = 64
PER_PAIR = 2
N_LEARN = 32


def shuffle_row(row_key):
    return jax.random.permutation(row_key, BATCH)


def draw_assignment(key, part):
    key = jax.random.fold_in(key, 7)
    row_keys = jax.random.split(key, N_LEARN)
    shuffled = jax.vmap(shuffle_row)(row_keys)
    return (shuffled // PER_PAIR).astype(jnp.int32)


def with_ends(result, key, least, high):
    dims = result.shape
    index_at = [jax.random.randint(jax.random.fold_in(key, axis), (), 0, dims[axis]) for axis in range(len(dims))]
    result = result.at[tuple(index_at)].set(least)
    longest = dims.index(max(dims))
    index_at[longest] = (index_at[longest] + 1) % dims[longest]
    return result.at[tuple(index_at)].set(high)


def level_of(own_key, shape, cuts, low, largest):
    gain, own = 1.0, jax.random.fold_in(own_key, 6)
    for dim, blocks in cuts:
        draws = jnp.exp(jax.random.uniform(jax.random.fold_in(own, dim), (blocks,), jnp.float32, low / len(cuts), largest / len(cuts)))
        gain = gain * jnp.repeat(draws, shape[dim] // blocks).reshape([-1 if axis == dim else 1 for axis in range(len(shape))])
    return gain


def length_profile(number_of, total, most, lean):
    portions = [(1 << 20) // math.isqrt(grade ** lean) + 1 for grade in range(2, number_of + 1)]
    surplus, holding = total - most - (number_of - 1), [1] * (number_of - 1)
    while surplus > 0:
        free = [i for i in range(number_of - 1) if holding[i] < most]
        whole, remaining = sum([portions[i] for i in free]), surplus
        for i in free:
            extra = min(most - holding[i], max(1, remaining * portions[i] // whole), surplus)
            holding[i] = holding[i] + extra
            surplus = surplus - extra
    return np.array([most] + holding)


def uneven_parts(stream_key, amount, total, limit, skew):
    if amount == 2:
        one = jax.random.randint(stream_key, (), max(1, total - limit), min(limit, total - 1) + 1)
        return jnp.stack([one, total - one])
    lengths = jnp.asarray(length_profile(amount, total, limit, skew), jnp.int32)
    twos = (amount - 1) // 2
    giver, taker = lengths[1:1 + 2 * twos:2], lengths[2:2 + 2 * twos:2]
    room = jnp.minimum(giver - 1, limit - taker)
    moved = jax.random.randint(jax.random.fold_in(stream_key, 1), (twos,), 0, 1 << 20) % (room + 1)
    lengths = lengths.at[1:1 + 2 * twos:2].set(giver - moved).at[2:2 + 2 * twos:2].set(taker + moved)
    return lengths[jax.random.permutation(jax.random.fold_in(stream_key, 2), amount)]


def centred(rng, extent, spread, bound, pieces=(), kind=jnp.bfloat16):
    factor_of = level_of(rng, extent, pieces, -0.22, 0.18) if pieces else 1.0
    drawn = jax.random.normal(rng, extent, jnp.float32) * spread * factor_of
    return jnp.minimum(jnp.maximum(drawn, -bound), bound).astype(kind)


def setup_inputs(seed: int = 0) -> dict:
    keys = jax.random.split(jax.random.key(seed), 13)
    return {
        "rec_weight": centred(keys[0], (UNITS, 4, UNITS), (UNITS // 10) ** -0.5, 0.4375, ((0, 32), (2, 4))),
        "head_weight": centred(keys[1], (UNITS, CHOICES), UNITS ** -0.5, 0.125, ((0, 32),)),
        "value_head": centred(keys[2], (UNITS,), (UNITS // 4) ** -0.5, 0.25, ((0, 32),)),
        "gate_inputs": centred(keys[3], (N_LEARN, BATCH, STEPS, 4, UNITS), 0.5, 3.0, ((0, 32), (4, 4))),
        "start_state": centred(keys[4], (N_LEARN, BATCH, 2, UNITS), 0.5, 3.0, ((0, 32), (3, 4))),
        "advantages": centred(keys[5], (N_LEARN, BATCH, STEPS), 1.0, 6.0, ((0, 32),)),
        "returns": centred(keys[6], (N_LEARN, BATCH, STEPS), 1.0, 6.0, ((0, 32),)),
        "old_logprob": jnp.clip(-5.375 + 1.09375 * jax.random.uniform(keys[7], (N_LEARN, BATCH, STEPS), jnp.float32) ** level_of(keys[7], (N_LEARN, BATCH, STEPS), ((0, 32),), -0.2, 0.2), -5.375, -4.28125).astype(jnp.bfloat16),
        "taken_action": with_ends(jax.random.randint(keys[8], (N_LEARN, BATCH, STEPS), 0, CHOICES), jax.random.fold_in(keys[8], 1), 0, CHOICES - 1).astype(jnp.int32),
        "episode_start": with_ends((jax.random.randint(keys[9], (N_LEARN, BATCH, STEPS), 0, 64) < 1).astype(jnp.int32), jax.random.fold_in(keys[9], 1), 0, 1),
        "segment_counts": uneven_parts(keys[10], N_LEARN, N_LEARN * BATCH // 2, BATCH, 2).astype(jnp.int32),
        "assignment": draw_assignment(jax.random.fold_in(keys[12], 71), 0),
    }


penalty_weight = 0.5


def cell_gates(preact):
    in_gate = jax.nn.sigmoid(preact[:, 0])
    forget = jax.nn.sigmoid(preact[:, 1])
    candidate = jnp.tanh(preact[:, 2])
    out_gate = jax.nn.sigmoid(preact[:, 3])
    return in_gate, forget, candidate, out_gate


def cell_backward(preact, kept_cell, grad_hidden, grad_cell):
    in_gate, forget, candidate, out_gate = cell_gates(preact)
    squash = jnp.tanh(forget * kept_cell + in_gate * candidate)
    grad_out = grad_hidden * squash
    grad_total = grad_cell + grad_hidden * out_gate * (1.0 - squash * squash)
    grad_pre = jnp.stack([grad_total * candidate * in_gate * (1.0 - in_gate),
                          grad_total * kept_cell * forget * (1.0 - forget),
                          grad_total * in_gate * (1.0 - candidate * candidate),
                          grad_out * out_gate * (1.0 - out_gate)], axis=1).astype(jnp.bfloat16)
    return grad_pre, grad_total * forget


def head_terms(hidden_rows, head_weight, value_head, chosen_action, advantage, target, old_value, weight):
    logits = jnp.dot(hidden_rows, head_weight, preferred_element_type=jnp.float32)
    logsoft = jax.nn.log_softmax(logits, axis=-1)
    onehot = (lax.broadcasted_iota(jnp.int32, logits.shape, 1) == chosen_action[:, None]).astype(jnp.float32)
    chosen = jnp.sum(logsoft * onehot, axis=1)
    ratio = jnp.exp(chosen - old_value)
    estimate = jnp.dot(hidden_rows, value_head, preferred_element_type=jnp.float32)
    grad_ratio = (-ratio * advantage + penalty_weight * (ratio - 1.0)) * weight
    grad_logits = (grad_ratio[:, None] * (onehot - jnp.exp(logsoft))).astype(jnp.bfloat16)
    grad_estimate = ((estimate - target) * weight).astype(jnp.bfloat16)
    return estimate, grad_logits, grad_estimate


def source_pass(rec_matrix, head_weight, value_head, gate_in, state_in, advantage, target, old_value, chosen_action, starts, live):
    inputs = jnp.transpose(gate_in, (1, 0, 2, 3))
    keep_masks = (1 - starts).astype(jnp.float32).T
    step_count = inputs.shape[0]
    batch_size = inputs.shape[1]

    def advance(state_pair, slice_in):
        hidden_prev, cell_prev = state_pair
        step_input, keep_now = slice_in
        kept_hidden = hidden_prev * keep_now.astype(jnp.bfloat16)[:, None]
        kept_cell = cell_prev * keep_now[:, None]
        preact = step_input.astype(jnp.float32) + jnp.dot(kept_hidden, rec_matrix, preferred_element_type=jnp.float32).reshape(step_input.shape)
        in_gate, forget, candidate, out_gate = cell_gates(preact)
        cell_new = forget * kept_cell + in_gate * candidate
        hidden_new = (out_gate * jnp.tanh(cell_new)).astype(jnp.bfloat16)
        return (hidden_new, cell_new), (kept_hidden, kept_cell, preact, hidden_new)

    final_pair, saved = lax.scan(advance, (state_in[:, 0], state_in[:, 1].astype(jnp.float32)), (inputs, keep_masks))
    kept_hidden, kept_cell, preact, hidden = saved
    width_full = hidden.shape[2]
    hidden_rows = hidden.reshape(step_count * batch_size, width_full)
    weight = jnp.broadcast_to(live.astype(jnp.float32)[None, :] / STEPS, (step_count, batch_size)).reshape(-1)
    estimate, grad_logits, grad_estimate = head_terms(
        hidden_rows, head_weight, value_head, chosen_action.T.reshape(-1),
        advantage.T.reshape(-1).astype(jnp.float32), target.T.reshape(-1).astype(jnp.float32),
        old_value.T.reshape(-1).astype(jnp.float32), weight)
    head_hidden = (jnp.dot(grad_logits, head_weight.T, preferred_element_type=jnp.float32)
                   + grad_estimate.astype(jnp.float32)[:, None] * value_head.astype(jnp.float32)[None, :]).reshape(step_count, batch_size, width_full)

    def retreat(state_pair, slice_in):
        grad_hidden, grad_cell = state_pair
        preact_step, kept_step, keep_now, head_step = slice_in
        grad_pre, grad_cell_prev = cell_backward(preact_step, kept_step, head_step + grad_hidden, grad_cell)
        grad_prev = jnp.dot(grad_pre.reshape(batch_size, -1), rec_matrix.T, preferred_element_type=jnp.float32) * keep_now[:, None]
        return (grad_prev, grad_cell_prev * keep_now[:, None]), grad_pre

    blank = jnp.zeros((batch_size, width_full), jnp.float32)
    back_pair, grad_pres = lax.scan(retreat, (blank, blank), (preact, kept_cell, keep_masks, head_hidden), reverse=True)
    rec_grad = jnp.dot(kept_hidden.reshape(step_count * batch_size, width_full).T,
                       grad_pres.reshape(step_count * batch_size, -1), preferred_element_type=jnp.float32)
    head_grad = jnp.dot(hidden_rows.T, grad_logits, preferred_element_type=jnp.float32)
    value_grad = jnp.dot(grad_estimate, hidden_rows, preferred_element_type=jnp.float32)
    estimates = estimate.reshape(step_count, batch_size).T * live.astype(jnp.float32)[:, None]
    return rec_grad, head_grad, value_grad, estimates


def reference(rec_weight, head_weight, value_head, gate_inputs, start_state, advantages, returns, old_logprob, taken_action, episode_start, segment_counts, assignment):
    rec_matrix = rec_weight.reshape(UNITS, 4 * UNITS)
    slot_index = jnp.arange(BATCH, dtype=jnp.int32)

    def visit(totals, group_data):
        gate_in, state_in, advantage, target, old_value, chosen_action, starts, count, assigned = group_data
        live = (slot_index < count).astype(jnp.int32)
        rec_grad, head_grad, value_grad, estimates = source_pass(
            rec_matrix, head_weight, value_head, gate_in, state_in, advantage, target, old_value, chosen_action, starts, live)
        slot_order = jnp.argsort(assigned, stable=True)
        placed = jnp.take(estimates, slot_order, axis=0).reshape(N_LEARN, PER_PAIR, STEPS)
        return (totals[0] + rec_grad, totals[1] + head_grad, totals[2] + value_grad), placed

    start = (jnp.zeros((UNITS, 4 * UNITS), jnp.float32), jnp.zeros((UNITS, CHOICES), jnp.float32), jnp.zeros((UNITS,), jnp.float32))
    totals, placed = lax.scan(visit, start, (gate_inputs, start_state, advantages, returns, old_logprob, taken_action, episode_start, segment_counts, assignment))
    learner_values = jnp.transpose(placed, (1, 0, 2, 3)).reshape(N_LEARN, BATCH, STEPS)
    return totals[0].reshape(UNITS, 4, UNITS), totals[1], totals[2], learner_values
```

```python
import jax
import jax.numpy as jnp
from jax import lax
from jax.experimental import pallas as pl
from jax.experimental.pallas import tpu as pltpu
from jax.sharding import PartitionSpec as P

MESH = pl.DeviceIdType.MESH
BF = jnp.bfloat16
F32 = jnp.float32
UNITS = 2048
QUARTER = 512
BATCH = 64
STEPS = 16
CHOICES = 128
VMEM = pl.BlockSpec(memory_space=pltpu.VMEM)
LIMIT = 60 * 2**20
OFFSETS = (2, -1, 1, 0)


def params(collective):
    return pltpu.CompilerParams(
        collective_id=collective, has_side_effects=True, vmem_limit_bytes=LIMIT
    )


def meet(devices):
    barrier = pltpu.get_barrier_semaphore()
    for device in devices:
        pl.semaphore_signal(barrier, inc=1, device_id=device, device_id_type=MESH)
    pl.semaphore_wait(barrier, len(devices))


class Torus:
    def __init__(self):
        place = lax.axis_index("learn")
        self.z, self.x, self.y = place // 16, lax.rem(place // 4, 4), lax.rem(place, 4)

    def device(self, dz, dx, dy):
        z = lax.rem(self.z + dz, 2)
        x = lax.rem(self.x + dx + 4, 4)
        y = lax.rem(self.y + dy + 4, 4)
        return {"learn": z * 16 + x * 4 + y}

    def first(self, half, d):
        return self.device(0, d, 0) if half == 0 else self.device(0, 0, d)

    def second(self, half, d):
        return self.device(0, 0, d) if half == 0 else self.device(0, d, 0)

    def other(self):
        return self.device(1, 0, 0)

    def neighbours(self):
        return [
            self.device(0, 1, 0),
            self.device(0, -1, 0),
            self.device(0, 0, 1),
            self.device(0, 0, -1),
            self.other(),
        ]

    def rows(self, half, plane, dp, dq, part=None):
        dx, dy = (dp, dq) if half == 0 else (dq, dp)
        block = self.device(plane, dx, dy)["learn"]
        start = block * 64 + 32 * half
        if part is None:
            return pl.ds(pl.multiple_of(start, 32), 32)
        return pl.ds(pl.multiple_of(start + 16 * part, 16), 16)


def gather_keys():
    keys = []
    for half in (0, 1):
        keys += [("p", half, d) for d in (1, -1)]
        keys += [("pf", half, d) for d in (1, -1)]
        keys += [("z", half, dp) for dp in OFFSETS]
        for plane in (0, 1):
            for dp in OFFSETS:
                keys += [("q", half, plane, dp, d) for d in (1, -1)]
                keys += [("qf", half, plane, dp, d) for d in (1, -1)]
    return {key: index for index, key in enumerate(keys)}


KEYS = gather_keys()


def gather_blocks(held, send_sems, recv_sems):
    torus = Torus()
    started = []

    def move(key, rows, device):
        index = KEYS[key]
        return pltpu.make_async_remote_copy(
            src_ref=held.at[rows],
            dst_ref=held.at[rows],
            send_sem=send_sems.at[index],
            recv_sem=recv_sems.at[index],
            device_id=device,
            device_id_type=MESH,
        )

    def send(key, rows, device):
        copy = move(key, rows, device)
        copy.start()
        started.append(copy)

    def arrive(key, rows):
        move(key, rows, torus.other()).wait_recv()

    def spread(half, plane, dp):
        for d in (1, -1):
            send(("q", half, plane, dp, d), torus.rows(half, plane, dp, 0), torus.second(half, d))

    def pass_on(half, plane, dp):
        for d in (1, -1):
            part = 0 if d == 1 else 1
            arrive(("q", half, plane, dp, d), torus.rows(half, plane, dp, -d))
            send(
                ("qf", half, plane, dp, d),
                torus.rows(half, plane, dp, -d, part),
                torus.second(half, d),
            )

    def cross(half, dp):
        send(("z", half, dp), torus.rows(half, 0, dp, 0), torus.other())

    def crossed(half, dp):
        arrive(("z", half, dp), torus.rows(half, 1, dp, 0))
        spread(half, 1, dp)

    for half in (0, 1):
        for d in (1, -1):
            send(("p", half, d), torus.rows(half, 0, 0, 0), torus.first(half, d))
    for half in (0, 1):
        cross(half, 0)
        spread(half, 0, 0)
    for half in (0, 1):
        for d in (1, -1):
            part = 0 if d == 1 else 1
            arrive(("p", half, d), torus.rows(half, 0, -d, 0))
            send(("pf", half, d), torus.rows(half, 0, -d, 0, part), torus.first(half, d))
            cross(half, -d)
    for half in (0, 1):
        for d in (1, -1):
            spread(half, 0, -d)
    for half in (0, 1):
        crossed(half, 0)
        for d in (1, -1):
            part = 0 if d == 1 else 1
            arrive(("pf", half, d), torus.rows(half, 0, -2 * d, 0, part))
        cross(half, 2)
        spread(half, 0, 2)
    for half in (0, 1):
        pass_on(half, 0, 0)
    for half in (0, 1):
        for d in (1, -1):
            crossed(half, -d)
    for half in (0, 1):
        for d in (1, -1):
            pass_on(half, 0, -d)
    for half in (0, 1):
        crossed(half, 2)
    for half in (0, 1):
        pass_on(half, 1, 0)
    for half in (0, 1):
        pass_on(half, 0, 2)
    for half in (0, 1):
        for d in (1, -1):
            pass_on(half, 1, -d)
    for half in (0, 1):
        pass_on(half, 1, 2)
    for half in (0, 1):
        for plane in (0, 1):
            for dp in OFFSETS:
                for d in (1, -1):
                    part = 0 if d == 1 else 1
                    arrive(
                        ("qf", half, plane, dp, d), torus.rows(half, plane, dp, -2 * d, part)
                    )
    for copy in started:
        copy.wait_send()


def gather_kernel(block_ref, held, send_sems, recv_sems):
    torus = Torus()
    meet(torus.neighbours())
    place = lax.axis_index("learn")
    held[pl.ds(pl.multiple_of(place * 64, 64), 64), :] = block_ref[...]
    gather_blocks(held, send_sems, recv_sems)


def gather_weights(block):
    return pl.pallas_call(
        gather_kernel,
        out_shape=jax.ShapeDtypeStruct((UNITS, block.shape[1]), BF),
        in_specs=[VMEM],
        out_specs=VMEM,
        scratch_shapes=[
            pltpu.SemaphoreType.DMA((len(KEYS),)),
            pltpu.SemaphoreType.DMA((len(KEYS),)),
        ],
        compiler_params=params(1),
        name="gather_weights",
    )(block)


def reduce_kernel(own, out_ref, staged, quarters, halves, send_sems, recv_sems):
    torus = Torus()
    meet(torus.neighbours())
    started = []
    slots = {"qf": 0, "q": 0, "pf": 0, "p": 0, "z": 0}
    where = {}
    for key in KEYS:
        small = key[0] in ("qf", "pf")
        kind = "quarter" if small else "half"
        where[key] = slots.setdefault(kind, 0)
        slots[kind] += 1

    def landing(key):
        size = 16 if key[0] in ("qf", "pf") else 32
        buffer = quarters if size == 16 else halves
        return buffer.at[pl.ds(where[key] * size, size)]

    def send(key, source, device):
        index = KEYS[key]
        copy = pltpu.make_async_remote_copy(
            src_ref=source,
            dst_ref=landing(key),
            send_sem=send_sems.at[index],
            recv_sem=recv_sems.at[index],
            device_id=device,
            device_id_type=MESH,
        )
        copy.start()
        started.append(copy)

    def arrived(key):
        index = KEYS[key]
        ref = landing(key)
        pltpu.make_async_remote_copy(
            src_ref=ref,
            dst_ref=ref,
            send_sem=send_sems.at[index],
            recv_sem=recv_sems.at[index],
            device_id=torus.other(),
            device_id_type=MESH,
        ).wait_recv()
        return ref[...].astype(F32)

    stage = {}

    def slot(key):
        if key not in stage:
            stage[key] = len(stage)
        return staged.at[pl.ds(stage[key] * 32, 32)]

    def far(half, plane, dp):
        for d in (1, -1):
            part = 0 if d == 1 else 1
            send(
                ("qf", half, plane, dp, d),
                own.at[torus.rows(half, plane, dp, -2 * d, part)],
                torus.second(half, -d),
            )

    def near(half, plane, dp):
        for d in (1, -1):
            part = 0 if d == 1 else 1
            target = slot(("q", half, plane, dp, d))
            target[...] = own[torus.rows(half, plane, dp, -d), :]
            extra = arrived(("qf", half, plane, dp, d))
            rows = pl.ds(16 * part, 16)
            target[rows, :] = (target[rows, :].astype(F32) + extra).astype(BF)
            send(("q", half, plane, dp, d), target, torus.second(half, -d))

    def line(half, plane, dp):
        total = own[torus.rows(half, plane, dp, 0), :].astype(F32)
        for d in (1, -1):
            total = total + arrived(("q", half, plane, dp, d))
        return total

    def cross(half, dp):
        target = slot(("z", half, dp))
        target[...] = line(half, 1, dp).astype(BF)
        send(("z", half, dp), target, torus.other())

    def plane_sum(half, dp):
        return line(half, 0, dp) + arrived(("z", half, dp))

    for plane in (1, 0):
        for dp in OFFSETS:
            for half in (0, 1):
                far(half, plane, dp)
    for plane in (1, 0):
        for dp in OFFSETS:
            for half in (0, 1):
                near(half, plane, dp)
    for dp in OFFSETS:
        for half in (0, 1):
            cross(half, dp)
    for half in (0, 1):
        target = slot(("pf", half))
        target[...] = plane_sum(half, 2).astype(BF)
        for d in (1, -1):
            part = 0 if d == 1 else 1
            send(("pf", half, d), target.at[pl.ds(16 * part, 16)], torus.first(half, -d))
    for half in (0, 1):
        for d in (1, -1):
            part = 0 if d == 1 else 1
            target = slot(("p", half, d))
            target[...] = plane_sum(half, -d).astype(BF)
            extra = arrived(("pf", half, d))
            rows = pl.ds(16 * part, 16)
            target[rows, :] = (target[rows, :].astype(F32) + extra).astype(BF)
            send(("p", half, d), target, torus.first(half, -d))
    for half in (0, 1):
        total = plane_sum(half, 0)
        for d in (1, -1):
            total = total + arrived(("p", half, d))
        out_ref[pl.ds(32 * half, 32), :] = total
    for copy in started:
        copy.wait_send()


def reduce_gradient(partial):
    width = partial.shape[1]
    quarters = sum(1 for key in KEYS if key[0] in ("qf", "pf"))
    halves = len(KEYS) - quarters
    return pl.pallas_call(
        reduce_kernel,
        out_shape=jax.ShapeDtypeStruct((64, width), F32),
        in_specs=[VMEM],
        out_specs=VMEM,
        scratch_shapes=[
            pltpu.VMEM((46 * 32, width), BF),
            pltpu.VMEM((quarters * 16, width), BF),
            pltpu.VMEM((halves * 32, width), BF),
            pltpu.SemaphoreType.DMA((len(KEYS),)),
            pltpu.SemaphoreType.DMA((len(KEYS),)),
        ],
        compiler_params=params(2),
        name="reduce_gradient",
    )(partial)


def actor_peers():
    me = lax.axis_index("actor")
    core = me + 1 - 2 * lax.rem(me, 2)
    across = lax.rem(me + 2, 4)
    return me, (core, across, 3 - me)


def columns(quarter):
    return pl.ds(pl.multiple_of(quarter * QUARTER, QUARTER), QUARTER)


def sigmoid(value):
    return 0.5 * jnp.tanh(0.5 * value) + 0.5


def forward_kernel(
    weight_ref, gate_ref, keep_ref, state_ref, hidden, factors, preact, cell, send_sems, recv_sems
):
    me, peers = actor_peers()
    meet([{"actor": peer} for peer in peers])

    def copies(t):
        result = []
        for index, peer in enumerate(peers):
            part = hidden.at[t, :, columns(me)]
            result.append(
                pltpu.make_async_remote_copy(
                    src_ref=part,
                    dst_ref=part,
                    send_sem=send_sems.at[t, index],
                    recv_sem=recv_sems.at[t, index],
                    device_id={"actor": peer},
                    device_id_type=MESH,
                )
            )
        return result

    def arrive(t, index):
        part = hidden.at[t, :, columns(peers[index])]
        pltpu.make_async_remote_copy(
            src_ref=part,
            dst_ref=part,
            send_sem=send_sems.at[t, index],
            recv_sem=recv_sems.at[t, index],
            device_id={"actor": peers[index]},
            device_id_type=MESH,
        ).wait_recv()

    def multiply(t, quarter, first):
        part = hidden[t, :, columns(quarter)]
        for k in range(4):
            spot = pl.ds(k * QUARTER, QUARTER)
            product = jnp.dot(
                part, weight_ref[columns(quarter), spot], preferred_element_type=F32
            )
            if first:
                preact[:, spot] = product
            else:
                preact[:, spot] += product

    def start(t):
        sends = copies(t)
        sends[1].start()
        sends[2].start()
        sends[0].start()

    hidden[0, :, columns(me)] = state_ref[:, 0:QUARTER]
    start(0)
    cell[...] = state_ref[:, QUARTER:].astype(F32)

    def step(t, carry):
        multiply(t, me, True)
        for index in range(3):
            arrive(t, index)
            multiply(t, peers[index], False)
        for chunk in range(QUARTER // 128):
            spot = pl.ds(chunk * 128, 128)
            keep = keep_ref[t]
            kept = keep * cell[:, spot]
            gates = []
            for k in range(4):
                wide = pl.ds(k * QUARTER + chunk * 128, 128)
                gates.append(gate_ref[t, :, wide].astype(F32) + keep * preact[:, wide])
            inp = sigmoid(gates[0])
            forget = sigmoid(gates[1])
            cand = jnp.tanh(gates[2])
            outg = sigmoid(gates[3])
            new_cell = forget * kept + inp * cand
            squash = jnp.tanh(new_cell)
            cell[:, spot] = new_cell
            part = pl.ds(pl.multiple_of(me * QUARTER + chunk * 128, 128), 128)
            hidden[t + 1, :, part] = (outg * squash).astype(BF)
            held = (
                outg * (1.0 - squash * squash),
                keep * cand * inp * (1.0 - inp),
                kept * forget * (1.0 - forget),
                keep * inp * (1.0 - cand * cand),
                keep * squash * outg * (1.0 - outg),
                keep * forget,
            )
            for index, value in enumerate(held):
                factors[t, index, :, spot] = value.astype(BF)
        start(t + 1)
        for copy in copies(t):
            copy.wait_send()
        return carry

    lax.fori_loop(0, STEPS, step, 0)
    for index in range(3):
        arrive(STEPS, index)
    for copy in copies(STEPS):
        copy.wait_send()


def forward(weight, gates, keep, state):
    return pl.pallas_call(
        forward_kernel,
        out_shape=(
            jax.ShapeDtypeStruct((STEPS + 1, BATCH, UNITS), BF),
            jax.ShapeDtypeStruct((STEPS, 6, BATCH, QUARTER), BF),
        ),
        in_specs=[VMEM] * 4,
        out_specs=(VMEM, VMEM),
        scratch_shapes=[
            pltpu.VMEM((BATCH, UNITS), F32),
            pltpu.VMEM((BATCH, QUARTER), F32),
            pltpu.SemaphoreType.DMA((STEPS + 1, 3)),
            pltpu.SemaphoreType.DMA((STEPS + 1, 3)),
        ],
        compiler_params=params(3),
        name="forward",
    )(weight, gates, keep, state)


def backward_kernel(
    weight_ref, factors, head_ref, grads, carry_hidden, carry_cell, sent, got, send_sems, recv_sems
):
    me, peers = actor_peers()
    meet([{"actor": peer} for peer in peers])
    carry_hidden[...] = jnp.zeros_like(carry_hidden)
    carry_cell[...] = jnp.zeros_like(carry_cell)

    def copy(t, index):
        return pltpu.make_async_remote_copy(
            src_ref=sent.at[t, index],
            dst_ref=got.at[t, index],
            send_sem=send_sems.at[t, index],
            recv_sem=recv_sems.at[t, index],
            device_id={"actor": peers[index]},
            device_id_type=MESH,
        )

    def cell_step(t):
        for chunk in range(QUARTER // 128):
            spot = pl.ds(chunk * 128, 128)
            factor = [factors[t, index, :, spot].astype(F32) for index in range(6)]
            total = head_ref[t, :, spot] + carry_hidden[:, spot]
            dcell = carry_cell[:, spot] + total * factor[0]
            carry_cell[:, spot] = dcell * factor[5]
            pieces = (dcell * factor[1], dcell * factor[2], dcell * factor[3], total * factor[4])
            for k, piece in enumerate(pieces):
                grads[t, :, pl.ds(k * QUARTER + chunk * 128, 128)] = piece.astype(BF)

    def product(t, quarter):
        return jnp.dot(
            grads[t], weight_ref[:, columns(quarter)], preferred_element_type=F32
        )

    def step(i, carry):
        t = STEPS - 1 - i
        cell_step(t)
        for index in (2, 1, 0):
            sent[t, index] = product(t, peers[index]).astype(BF)
            copy(t, index).start()
        total = product(t, me)
        for index in (0, 1, 2):
            copy(t, index).wait_recv()
            total = total + got[t, index].astype(F32)
        carry_hidden[...] = total
        for index in range(3):
            copy(t, index).wait_send()
        return carry

    lax.fori_loop(0, STEPS - 1, step, 0)
    cell_step(0)


def backward(weight_turned, factors, head_grad):
    return pl.pallas_call(
        backward_kernel,
        out_shape=jax.ShapeDtypeStruct((STEPS, BATCH, UNITS), BF),
        in_specs=[VMEM] * 3,
        out_specs=VMEM,
        scratch_shapes=[
            pltpu.VMEM((BATCH, QUARTER), F32),
            pltpu.VMEM((BATCH, QUARTER), F32),
            pltpu.VMEM((STEPS, 3, BATCH, QUARTER), BF),
            pltpu.VMEM((STEPS, 3, BATCH, QUARTER), BF),
            pltpu.SemaphoreType.DMA((STEPS, 3)),
            pltpu.SemaphoreType.DMA((STEPS, 3)),
        ],
        compiler_params=params(4),
        name="backward",
    )(weight_turned, factors, head_grad)


def flatten(values_in):
    return values_in.T.reshape(-1)


def shards(
    rec_weight,
    head_weight,
    value_head,
    gate_inputs,
    start_state,
    advantages,
    returns,
    old_logprob,
    taken_action,
    episode_start,
    segment_counts,
    assignment,
):
    learners = lax.axis_size("learn")
    place = lax.axis_index("learn")
    offset = lax.axis_index("actor") * QUARTER
    lanes = jnp.arange(learners, dtype=jnp.int32)
    own_count = jnp.sum(jnp.where(lanes == place, segment_counts, 0))
    live = (jnp.arange(BATCH, dtype=jnp.int32) < own_count).astype(F32)

    both = jnp.concatenate(
        [head_weight, value_head[:, None], jnp.zeros((64, CHOICES - 1), BF)], axis=1
    )
    heads = lax.all_gather(both, "learn", axis=0, tiled=True)

    weight = gather_weights(rec_weight.reshape(64, UNITS))
    gates = jnp.transpose(gate_inputs[0].reshape(BATCH, STEPS, UNITS), (1, 0, 2))
    keep = jnp.broadcast_to(
        (1 - episode_start[0]).astype(F32).T[:, :, None], (STEPS, BATCH, 128)
    )
    hidden, factors = forward(weight, gates, keep, start_state[0].reshape(BATCH, 2 * QUARTER))

    rows = hidden[1:].reshape(STEPS * BATCH, UNITS)
    scores = jnp.dot(rows, heads, preferred_element_type=F32)
    logits, estimate = scores[:, :CHOICES], scores[:, CHOICES]
    logsoft = jax.nn.log_softmax(logits, axis=-1)
    onehot = (
        lax.broadcasted_iota(jnp.int32, logits.shape, 1) == flatten(taken_action[0])[:, None]
    ).astype(F32)
    chosen = jnp.sum(logsoft * onehot, axis=1)
    ratio = jnp.exp(chosen - flatten(old_logprob[0]).astype(F32))
    share = jnp.broadcast_to(live[None, :] / STEPS, (STEPS, BATCH)).reshape(-1)
    grad_ratio = (-ratio * flatten(advantages[0]).astype(F32) + 0.5 * (ratio - 1.0)) * share
    grad_logits = (grad_ratio[:, None] * (onehot - jnp.exp(logsoft))).astype(BF)
    grad_estimate = ((estimate - flatten(returns[0]).astype(F32)) * share).astype(BF)
    grad_scores = jnp.concatenate(
        [grad_logits, grad_estimate[:, None], jnp.zeros((STEPS * BATCH, CHOICES - 1), BF)], axis=1
    )
    head_part = lax.dynamic_slice_in_dim(heads, offset, QUARTER, 0)
    head_grad = jnp.dot(grad_scores, head_part.T, preferred_element_type=F32).reshape(
        STEPS, BATCH, QUARTER
    )
    heads_partial = jnp.dot(rows.T, grad_scores, preferred_element_type=F32).astype(BF)
    heads_share = lax.psum_scatter(
        heads_partial, "learn", scatter_dimension=0, tiled=True
    ).astype(F32)

    assigned = assignment[0]
    slots = jnp.arange(BATCH, dtype=jnp.int32)
    earlier = (assigned[None, :] == assigned[:, None]) & (slots[None, :] < slots[:, None])
    target = assigned * 2 + jnp.sum(earlier.astype(jnp.int32), axis=1)
    values = estimate.reshape(STEPS, BATCH) * live[None, :]
    moved = jnp.sum(
        jnp.where((target[:, None] == slots[None, :])[:, :, None], values.T[:, None, :], 0.0), axis=0
    )
    learner_values = lax.all_to_all(
        moved.reshape(learners, 2, STEPS), "learn", split_axis=0, concat_axis=0, tiled=True
    ).reshape(1, BATCH, STEPS)

    grads = backward(weight.T, factors, head_grad)

    partial = jnp.dot(
        hidden[:STEPS].reshape(STEPS * BATCH, UNITS).T,
        grads.reshape(STEPS * BATCH, UNITS),
        preferred_element_type=F32,
    ).astype(BF)
    rec_share = reduce_gradient(partial).reshape(64, 4, QUARTER)
    return (rec_share, heads_share[:, :CHOICES], heads_share[:, CHOICES], learner_values)


def solution(mesh):
    placed = (
        P("learn", None, "actor"),
        P("learn", None),
        P("learn"),
        P("learn", None, None, None, "actor"),
        P("learn", None, None, "actor"),
        P("learn", None, None),
        P("learn", None, None),
        P("learn", None, None),
        P("learn", None, None),
        P("learn", None, None),
        P(),
        P("learn", None),
    )
    return jax.shard_map(
        shards,
        mesh=mesh,
        in_specs=placed,
        out_specs=(P("learn", None, "actor"), P("learn", None), P("learn"), P("learn", None, None)),
        check_vma=False,
    )
```

```python
import jax
import jax.numpy as jnp
from jax import lax
from jax.experimental import pallas as pl
from jax.experimental.pallas import tpu as pltpu
from jax.sharding import PartitionSpec as P

MESH = pl.DeviceIdType.MESH
BF = jnp.bfloat16
F32 = jnp.float32
UNITS = 2048
QUARTER = 512
BATCH = 64
STEPS = 16
CHOICES = 128
WIDE = UNITS + 2 * CHOICES
VMEM = pl.BlockSpec(memory_space=pltpu.VMEM)
LIMIT = 60 * 2**20
OFFSETS = (2, -1, 1, 0)


def params(collective):
    return pltpu.CompilerParams(
        collective_id=collective, has_side_effects=True, vmem_limit_bytes=LIMIT
    )


def meet(devices):
    barrier = pltpu.get_barrier_semaphore()
    for device in devices:
        pl.semaphore_signal(barrier, inc=1, device_id=device, device_id_type=MESH)
    pl.semaphore_wait(barrier, len(devices))


class Torus:
    def __init__(self):
        place = lax.axis_index("learn")
        self.z, self.x, self.y = place // 16, lax.rem(place // 4, 4), lax.rem(place, 4)

    def device(self, dz, dx, dy):
        z = lax.rem(self.z + dz, 2)
        x = lax.rem(self.x + dx + 4, 4)
        y = lax.rem(self.y + dy + 4, 4)
        return {"learn": z * 16 + x * 4 + y}

    def first(self, half, d):
        return self.device(0, d, 0) if half == 0 else self.device(0, 0, d)

    def second(self, half, d):
        return self.device(0, 0, d) if half == 0 else self.device(0, d, 0)

    def other(self):
        return self.device(1, 0, 0)

    def neighbours(self):
        return [
            self.device(0, 1, 0),
            self.device(0, -1, 0),
            self.device(0, 0, 1),
            self.device(0, 0, -1),
            self.other(),
        ]

    def rows(self, half, plane, dp, dq, part=None):
        dx, dy = (dp, dq) if half == 0 else (dq, dp)
        block = self.device(plane, dx, dy)["learn"]
        start = block * 64 + 32 * half
        if part is None:
            return pl.ds(pl.multiple_of(start, 32), 32)
        return pl.ds(pl.multiple_of(start + 16 * part, 16), 16)


def gather_keys():
    keys = []
    for half in (0, 1):
        keys += [("p", half, d) for d in (1, -1)]
        keys += [("pf", half, d) for d in (1, -1)]
        keys += [("z", half, dp) for dp in OFFSETS]
        for plane in (0, 1):
            for dp in OFFSETS:
                keys += [("q", half, plane, dp, d) for d in (1, -1)]
                keys += [("qf", half, plane, dp, d) for d in (1, -1)]
    return {key: index for index, key in enumerate(keys)}


KEYS = gather_keys()


def gather_blocks(held, send_sems, recv_sems):
    torus = Torus()
    started = []

    def move(key, rows, device):
        index = KEYS[key]
        return pltpu.make_async_remote_copy(
            src_ref=held.at[rows],
            dst_ref=held.at[rows],
            send_sem=send_sems.at[index],
            recv_sem=recv_sems.at[index],
            device_id=device,
            device_id_type=MESH,
        )

    def send(key, rows, device):
        copy = move(key, rows, device)
        copy.start()
        started.append(copy)

    def arrive(key, rows):
        move(key, rows, torus.other()).wait_recv()

    def spread(half, plane, dp):
        for d in (1, -1):
            send(("q", half, plane, dp, d), torus.rows(half, plane, dp, 0), torus.second(half, d))

    def pass_on(half, plane, dp):
        for d in (1, -1):
            part = 0 if d == 1 else 1
            arrive(("q", half, plane, dp, d), torus.rows(half, plane, dp, -d))
            send(
                ("qf", half, plane, dp, d),
                torus.rows(half, plane, dp, -d, part),
                torus.second(half, d),
            )

    def cross(half, dp):
        send(("z", half, dp), torus.rows(half, 0, dp, 0), torus.other())

    def crossed(half, dp):
        arrive(("z", half, dp), torus.rows(half, 1, dp, 0))
        spread(half, 1, dp)

    for half in (0, 1):
        for d in (1, -1):
            send(("p", half, d), torus.rows(half, 0, 0, 0), torus.first(half, d))
    for half in (0, 1):
        cross(half, 0)
        spread(half, 0, 0)
    for half in (0, 1):
        for d in (1, -1):
            part = 0 if d == 1 else 1
            arrive(("p", half, d), torus.rows(half, 0, -d, 0))
            send(("pf", half, d), torus.rows(half, 0, -d, 0, part), torus.first(half, d))
            cross(half, -d)
    for half in (0, 1):
        for d in (1, -1):
            spread(half, 0, -d)
    for half in (0, 1):
        crossed(half, 0)
        for d in (1, -1):
            part = 0 if d == 1 else 1
            arrive(("pf", half, d), torus.rows(half, 0, -2 * d, 0, part))
        cross(half, 2)
        spread(half, 0, 2)
    for half in (0, 1):
        pass_on(half, 0, 0)
    for half in (0, 1):
        for d in (1, -1):
            crossed(half, -d)
    for half in (0, 1):
        for d in (1, -1):
            pass_on(half, 0, -d)
    for half in (0, 1):
        crossed(half, 2)
    for half in (0, 1):
        pass_on(half, 1, 0)
    for half in (0, 1):
        pass_on(half, 0, 2)
    for half in (0, 1):
        for d in (1, -1):
            pass_on(half, 1, -d)
    for half in (0, 1):
        pass_on(half, 1, 2)
    for half in (0, 1):
        for plane in (0, 1):
            for dp in OFFSETS:
                for d in (1, -1):
                    part = 0 if d == 1 else 1
                    arrive(
                        ("qf", half, plane, dp, d), torus.rows(half, plane, dp, -2 * d, part)
                    )
    for copy in started:
        copy.wait_send()


def reduce_kernel(
    hidden,
    grads,
    scores,
    out_ref,
    heads_ref,
    own,
    staged,
    quarters,
    halves,
    send_sems,
    recv_sems,
):
    torus = Torus()
    meet(torus.neighbours())
    started = []
    where = {}
    counts = {16: 0, 32: 0}
    for key in KEYS:
        size = 16 if key[0] in ("qf", "pf") else 32
        where[key] = counts[size]
        counts[size] += 1

    def landing(key):
        size = 16 if key[0] in ("qf", "pf") else 32
        buffer = quarters if size == 16 else halves
        return buffer.at[pl.ds(where[key] * size, size)]

    def send(key, source, device):
        index = KEYS[key]
        copy = pltpu.make_async_remote_copy(
            src_ref=source,
            dst_ref=landing(key),
            send_sem=send_sems.at[index],
            recv_sem=recv_sems.at[index],
            device_id=device,
            device_id_type=MESH,
        )
        copy.start()
        started.append(copy)

    def arrived(key):
        index = KEYS[key]
        ref = landing(key)
        pltpu.make_async_remote_copy(
            src_ref=ref,
            dst_ref=ref,
            send_sem=send_sems.at[index],
            recv_sem=recv_sems.at[index],
            device_id=torus.other(),
            device_id_type=MESH,
        ).wait_recv()
        return ref[...].astype(F32)

    stage = {}

    def slot(key):
        if key not in stage:
            stage[key] = len(stage)
        return staged.at[pl.ds(stage[key] * 32, 32)]

    def multiply(plane, dx):
        first = torus.device(plane, dx, 0)["learn"] // 4
        spot = pl.ds(pl.multiple_of(first * 256, 256), 256)
        kept = hidden[0:STEPS, :, spot].reshape(STEPS * BATCH, 256)
        for k in range(4):
            part = pl.ds(k * QUARTER, QUARTER)
            own[spot, part] = lax.dot_general(
                kept,
                grads[:, :, part].reshape(STEPS * BATCH, QUARTER),
                (((0,), (0,)), ((), ())),
                preferred_element_type=F32,
            ).astype(BF)
        own[spot, UNITS:WIDE] = lax.dot_general(
            hidden[1 : STEPS + 1, :, spot].reshape(STEPS * BATCH, 256),
            scores[1 : STEPS + 1].reshape(STEPS * BATCH, 2 * CHOICES),
            (((0,), (0,)), ((), ())),
            preferred_element_type=F32,
        ).astype(BF)

    def far(half, plane, dp):
        for d in (1, -1):
            part = 0 if d == 1 else 1
            send(
                ("qf", half, plane, dp, d),
                own.at[torus.rows(half, plane, dp, -2 * d, part)],
                torus.second(half, -d),
            )

    def near(half, plane, dp, d):
        part = 0 if d == 1 else 1
        target = slot(("q", half, plane, dp, d))
        target[...] = own[torus.rows(half, plane, dp, -d), :]
        extra = arrived(("qf", half, plane, dp, d))
        rows = pl.ds(16 * part, 16)
        target[rows, :] = (target[rows, :].astype(F32) + extra).astype(BF)
        send(("q", half, plane, dp, d), target, torus.second(half, -d))

    def line(half, plane, dp):
        total = own[torus.rows(half, plane, dp, 0), :].astype(F32)
        for d in (1, -1):
            total = total + arrived(("q", half, plane, dp, d))
        return total

    def cross(half, dp):
        target = slot(("z", half, dp))
        target[...] = line(half, 1, dp).astype(BF)
        send(("z", half, dp), target, torus.other())

    def plane_sum(half, dp):
        return line(half, 0, dp) + arrived(("z", half, dp))

    for plane in (1, 0):
        multiply(plane, 2)
        for dp in OFFSETS:
            far(1, plane, dp)
        far(0, plane, 2)
        multiply(plane, -1)
        far(0, plane, -1)
        for d in (1, -1):
            near(0, plane, 2, d)
        for dp in OFFSETS:
            near(1, plane, dp, 1)
        multiply(plane, 1)
        far(0, plane, 1)
        for d in (1, -1):
            near(0, plane, -1, d)
        for dp in OFFSETS:
            near(1, plane, dp, -1)
        multiply(plane, 0)
        far(0, plane, 0)
        for d in (1, -1):
            near(0, plane, 1, d)
        for d in (1, -1):
            near(0, plane, 0, d)
    for dp in OFFSETS:
        for half in (0, 1):
            cross(half, dp)
    for half in (0, 1):
        target = slot(("pf", half))
        target[...] = plane_sum(half, 2).astype(BF)
        for d in (1, -1):
            part = 0 if d == 1 else 1
            send(("pf", half, d), target.at[pl.ds(16 * part, 16)], torus.first(half, -d))
    for half in (0, 1):
        for d in (1, -1):
            part = 0 if d == 1 else 1
            target = slot(("p", half, d))
            target[...] = plane_sum(half, -d).astype(BF)
            extra = arrived(("pf", half, d))
            rows = pl.ds(16 * part, 16)
            target[rows, :] = (target[rows, :].astype(F32) + extra).astype(BF)
            send(("p", half, d), target, torus.first(half, -d))
    for half in (0, 1):
        total = plane_sum(half, 0)
        for d in (1, -1):
            total = total + arrived(("p", half, d))
        rows = pl.ds(32 * half, 32)
        for k in range(4):
            out_ref[rows, k, :] = total[:, k * QUARTER : (k + 1) * QUARTER]
        heads_ref[rows, :] = total[:, UNITS:]
    for copy in started:
        copy.wait_send()


def reduce_gradient(hidden, grads, scores):
    quarters = sum(1 for key in KEYS if key[0] in ("qf", "pf"))
    halves = len(KEYS) - quarters
    return pl.pallas_call(
        reduce_kernel,
        out_shape=(
            jax.ShapeDtypeStruct((64, 4, QUARTER), F32),
            jax.ShapeDtypeStruct((64, 2 * CHOICES), F32),
        ),
        in_specs=[VMEM] * 3,
        out_specs=(VMEM, VMEM),
        scratch_shapes=[
            pltpu.VMEM((UNITS, WIDE), BF),
            pltpu.VMEM((46 * 32, WIDE), BF),
            pltpu.VMEM((quarters * 16, WIDE), BF),
            pltpu.VMEM((halves * 32, WIDE), BF),
            pltpu.SemaphoreType.DMA((len(KEYS),)),
            pltpu.SemaphoreType.DMA((len(KEYS),)),
        ],
        compiler_params=params(2),
        name="reduce_gradient",
    )(hidden, grads, scores)


def actor_peers():
    me = lax.axis_index("actor")
    core = me + 1 - 2 * lax.rem(me, 2)
    across = lax.rem(me + 2, 4)
    return me, (core, across, 3 - me)


def columns(quarter, start=0, size=QUARTER):
    return pl.ds(pl.multiple_of(quarter * QUARTER + start, min(size, 256)), size)


def sigmoid(value):
    return 0.5 * jnp.tanh(0.5 * value) + 0.5


HALF = QUARTER // 2


def train_kernel(
    block_ref,
    head_ref,
    gate_ref,
    state_ref,
    aux_ref,
    hidden,
    grads,
    scores,
    values,
    held,
    turned,
    factors,
    head_grad,
    gates,
    aux,
    preact,
    cell,
    carry_hidden,
    carry_cell,
    sent,
    got,
    sent_core,
    got_core,
    gather_send,
    gather_recv,
    step_send,
    step_recv,
    back_send,
    back_recv,
):
    torus = Torus()
    me, peers = actor_peers()
    core, across, diagonal = peers
    meet(torus.neighbours() + [{"actor": peer} for peer in peers])
    place = lax.axis_index("learn")
    mine = pl.ds(pl.multiple_of(place * 64, 64), 64)
    held[mine, 0:UNITS] = block_ref[...].reshape(64, UNITS)
    held[mine, UNITS:WIDE] = head_ref[...]

    def pieces(t):
        return (
            (hidden.at[t, :, columns(me)], core),
            (hidden.at[t, :, columns(me, 0, HALF)], across),
            (hidden.at[t, :, columns(me, HALF, HALF)], across),
            (hidden.at[t, :, columns(me, HALF, HALF)], diagonal),
            (hidden.at[t, :, columns(across, 0, HALF)], core),
        )

    def landed(t):
        return (
            hidden.at[t, :, columns(core)],
            hidden.at[t, :, columns(across, 0, HALF)],
            hidden.at[t, :, columns(across, HALF, HALF)],
            hidden.at[t, :, columns(diagonal, HALF, HALF)],
            hidden.at[t, :, columns(diagonal, 0, HALF)],
        )

    def step_copy(t, index):
        part, peer = pieces(t)[index]
        return pltpu.make_async_remote_copy(
            src_ref=part,
            dst_ref=part,
            send_sem=step_send.at[t, index],
            recv_sem=step_recv.at[t, index],
            device_id={"actor": peer},
            device_id_type=MESH,
        )

    def arrive(t, index):
        part = landed(t)[index]
        pltpu.make_async_remote_copy(
            src_ref=part,
            dst_ref=part,
            send_sem=step_send.at[t, index],
            recv_sem=step_recv.at[t, index],
            device_id={"actor": core},
            device_id_type=MESH,
        ).wait_recv()

    def multiply(t, spot, first=False):
        part = hidden[t, :, spot]
        for k in range(4):
            wide = pl.ds(k * QUARTER, QUARTER)
            product = jnp.dot(part, held[spot, wide], preferred_element_type=F32)
            if first:
                preact[:, wide] = product
            else:
                preact[:, wide] += product

    def column(t, kind):
        lane = lax.broadcasted_iota(jnp.int32, (BATCH, 128), 1)
        return jnp.sum(jnp.where(lane == t + 16 * kind, aux[...], 0.0), axis=1, keepdims=True)

    def heads(index):
        t = index - 1
        result = jnp.dot(hidden[index], held[:, UNITS:WIDE], preferred_element_type=F32)
        logits = result[:, 0:CHOICES]
        estimate = result[:, CHOICES : CHOICES + 1]
        share = aux[:, 80:81]
        lane = lax.broadcasted_iota(jnp.int32, (BATCH, CHOICES), 1)
        onehot = (lane.astype(F32) == column(t, 4)).astype(F32)
        shifted = logits - jnp.max(logits, axis=1, keepdims=True)
        powers = jnp.exp(shifted)
        total = jnp.sum(powers, axis=1, keepdims=True)
        chosen = jnp.sum(shifted * onehot, axis=1, keepdims=True) - jnp.log(total)
        ratio = jnp.exp(chosen - column(t, 3))
        slope = (0.5 * (ratio - 1.0) - ratio * column(t, 1)) * share
        grad_logits = slope * (onehot - powers / total)
        grad_estimate = (estimate - column(t, 2)) * share
        scores[index, :, 0:CHOICES] = grad_logits.astype(BF)
        scores[index, :, CHOICES : 2 * CHOICES] = jnp.where(lane == 0, grad_estimate, 0.0).astype(BF)
        live = (share > 0.0).astype(F32)
        values[...] = jnp.where(lane == t, estimate * live, values[...])
        head_grad[index] = lax.dot_general(
            scores[index],
            held[columns(me), UNITS:WIDE],
            (((1,), (1,)), ((), ())),
            preferred_element_type=F32,
        )

    def cells(t, half):
        keep = column(t, 0)
        for chunk in range(2 * half, 2 * half + 2):
            spot = pl.ds(chunk * 128, 128)
            kept = keep * cell[:, spot]
            inputs = []
            for k in range(4):
                wide = pl.ds(k * QUARTER + chunk * 128, 128)
                inputs.append(gates[:, wide].astype(F32) + keep * preact[:, wide])
            inp = sigmoid(inputs[0])
            forget = sigmoid(inputs[1])
            cand = jnp.tanh(inputs[2])
            outg = sigmoid(inputs[3])
            new_cell = forget * kept + inp * cand
            squash = jnp.tanh(new_cell)
            cell[:, spot] = new_cell
            part = pl.ds(pl.multiple_of(me * QUARTER + chunk * 128, 128), 128)
            hidden[t + 1, :, part] = (outg * squash).astype(BF)
            kept_factors = (
                outg * (1.0 - squash * squash),
                keep * cand * inp * (1.0 - inp),
                kept * forget * (1.0 - forget),
                keep * inp * (1.0 - cand * cand),
                keep * squash * outg * (1.0 - outg),
                keep * forget,
            )
            for index, value in enumerate(kept_factors):
                factors[t, index, :, spot] = value.astype(BF)

    hidden[0, :, columns(me)] = state_ref[:, 0, :]
    for index in (1, 2, 3, 0):
        step_copy(0, index).start()
    cell[...] = state_ref[:, 1, :].astype(F32)
    aux[...] = aux_ref[...].T[0:BATCH]
    values[...] = jnp.zeros_like(values)
    gather_blocks(held, gather_send, gather_recv)

    def step(t, carry):
        multiply(t, columns(me), True)
        gates[...] = gate_ref[:, t].reshape(BATCH, UNITS)
        arrive(t, 0)
        multiply(t, columns(core))
        stripe = pl.ds(pl.multiple_of(t * 128, 128), 128)
        turned[:, stripe] = held[stripe, 0:UNITS].T
        arrive(t, 1)
        step_copy(t, 4).start()
        multiply(t, columns(across, 0, HALF))

        @pl.when(t >= 2)
        def _():
            heads(t - 1)

        arrive(t, 2)
        multiply(t, columns(across, HALF, HALF))
        arrive(t, 3)
        multiply(t, columns(diagonal, HALF, HALF))
        arrive(t, 4)
        multiply(t, columns(diagonal, 0, HALF))
        cells(t, 0)
        step_copy(t + 1, 1).start()
        cells(t, 1)
        for index in (2, 3, 0):
            step_copy(t + 1, index).start()
        for index in range(5):
            step_copy(t, index).wait_send()
        return carry

    lax.fori_loop(0, STEPS, step, 0)
    heads(STEPS - 1)
    arrive(STEPS, 1)
    step_copy(STEPS, 4).start()
    for index in (0, 2, 3, 4):
        arrive(STEPS, index)
    for index in range(5):
        step_copy(STEPS, index).wait_send()
    heads(STEPS)

    carry_hidden[...] = jnp.zeros_like(carry_hidden)
    carry_cell[...] = jnp.zeros_like(carry_cell)

    targets = (diagonal, across, core, across, core)

    def back_copy(t, index):
        return pltpu.make_async_remote_copy(
            src_ref=sent_core.at[t] if index == 4 else sent.at[t, index],
            dst_ref=got_core.at[t] if index == 4 else got.at[t, index],
            send_sem=back_send.at[t, index],
            recv_sem=back_recv.at[t, index],
            device_id={"actor": targets[index]},
            device_id_type=MESH,
        )

    def cell_back(t):
        for chunk in range(QUARTER // 128):
            spot = pl.ds(chunk * 128, 128)
            factor = [factors[t, index, :, spot].astype(F32) for index in range(6)]
            total = head_grad[t + 1, :, spot] + carry_hidden[:, spot]
            dcell = carry_cell[:, spot] + total * factor[0]
            carry_cell[:, spot] = dcell * factor[5]
            parts = (dcell * factor[1], dcell * factor[2], dcell * factor[3], total * factor[4])
            for k, part in enumerate(parts):
                grads[t, :, pl.ds(k * QUARTER + chunk * 128, 128)] = part.astype(BF)

    def product(t, spot):
        return jnp.dot(grads[t], turned[:, spot], preferred_element_type=F32)

    def back(i, carry):
        t = STEPS - 1 - i
        cell_back(t)
        for index, quarter, start in ((0, diagonal, 0), (1, across, 0), (2, diagonal, HALF)):
            sent[t, index] = product(t, columns(quarter, start, HALF)).astype(BF)
            back_copy(t, index).start()
        part = product(t, columns(across, HALF, HALF))
        sent_core[t] = product(t, columns(core)).astype(BF)
        back_copy(t, 4).start()
        back_copy(t, 2).wait_recv()
        sent[t, 3] = (part + got[t, 2].astype(F32)).astype(BF)
        back_copy(t, 3).start()
        carry_hidden[...] = product(t, columns(me))
        back_copy(t, 4).wait_recv()
        carry_hidden[...] += got_core[t].astype(F32)
        for index in (0, 1):
            back_copy(t, index).wait_recv()
        carry_hidden[:, 0:HALF] += got[t, 0].astype(F32) + got[t, 1].astype(F32)
        back_copy(t, 3).wait_recv()
        carry_hidden[:, HALF:QUARTER] += got[t, 3].astype(F32)
        for index in range(5):
            back_copy(t, index).wait_send()
        return carry

    lax.fori_loop(0, STEPS - 1, back, 0)
    cell_back(0)


def train(block, heads, gates, state, aux):
    return pl.pallas_call(
        train_kernel,
        out_shape=(
            jax.ShapeDtypeStruct((STEPS + 1, BATCH, UNITS), BF),
            jax.ShapeDtypeStruct((STEPS, BATCH, UNITS), BF),
            jax.ShapeDtypeStruct((STEPS + 1, BATCH, 2 * CHOICES), BF),
            jax.ShapeDtypeStruct((BATCH, 128), F32),
        ),
        in_specs=[VMEM] * 5,
        out_specs=(VMEM,) * 4,
        scratch_shapes=[
            pltpu.VMEM((UNITS, WIDE), BF),
            pltpu.VMEM((UNITS, UNITS), BF),
            pltpu.VMEM((STEPS, 6, BATCH, QUARTER), BF),
            pltpu.VMEM((STEPS + 1, BATCH, QUARTER), F32),
            pltpu.VMEM((BATCH, UNITS), BF),
            pltpu.VMEM((BATCH, 128), F32),
            pltpu.VMEM((BATCH, UNITS), F32),
            pltpu.VMEM((BATCH, QUARTER), F32),
            pltpu.VMEM((BATCH, QUARTER), F32),
            pltpu.VMEM((BATCH, QUARTER), F32),
            pltpu.VMEM((STEPS, 4, BATCH, HALF), BF),
            pltpu.VMEM((STEPS, 4, BATCH, HALF), BF),
            pltpu.VMEM((STEPS, BATCH, QUARTER), BF),
            pltpu.VMEM((STEPS, BATCH, QUARTER), BF),
            pltpu.SemaphoreType.DMA((len(KEYS),)),
            pltpu.SemaphoreType.DMA((len(KEYS),)),
            pltpu.SemaphoreType.DMA((STEPS + 1, 5)),
            pltpu.SemaphoreType.DMA((STEPS + 1, 5)),
            pltpu.SemaphoreType.DMA((STEPS, 5)),
            pltpu.SemaphoreType.DMA((STEPS, 5)),
        ],
        compiler_params=params(1),
        name="train",
    )(block, heads, gates, state, aux)


def shards(
    rec_weight,
    head_weight,
    value_head,
    gate_inputs,
    start_state,
    advantages,
    returns,
    old_logprob,
    taken_action,
    episode_start,
    segment_counts,
    assignment,
):
    learners = lax.axis_size("learn")
    place = lax.axis_index("learn")
    lanes = jnp.arange(learners, dtype=jnp.int32)
    own_count = jnp.sum(jnp.where(lanes == place, segment_counts, 0))
    live = (jnp.arange(BATCH, dtype=jnp.int32) < own_count).astype(F32)

    heads = jnp.concatenate(
        [head_weight, value_head[:, None], jnp.zeros((64, CHOICES - 1), BF)], axis=1
    )
    aux = jnp.concatenate(
        [
            (1 - episode_start[0]).astype(F32).T,
            advantages[0].astype(F32).T,
            returns[0].astype(F32).T,
            old_logprob[0].astype(F32).T,
            taken_action[0].astype(F32).T,
            jnp.broadcast_to(live[None, :] / STEPS, (48, BATCH)),
        ],
        axis=0,
    )
    aux = jnp.pad(aux, ((0, 0), (0, 128 - BATCH)))
    hidden, grads, scores, estimates = train(
        rec_weight, heads, gate_inputs[0], start_state[0], aux
    )

    assigned = assignment[0]
    slots = jnp.arange(BATCH, dtype=jnp.int32)
    earlier = (assigned[None, :] == assigned[:, None]) & (slots[None, :] < slots[:, None])
    target = assigned * 2 + jnp.sum(earlier.astype(jnp.int32), axis=1)
    moved = jnp.sum(
        jnp.where(
            (target[:, None] == slots[None, :])[:, :, None], estimates[:, None, :STEPS], 0.0
        ),
        axis=0,
    )
    learner_values = lax.all_to_all(
        moved.reshape(learners, 2, STEPS), "learn", split_axis=0, concat_axis=0, tiled=True
    ).reshape(1, BATCH, STEPS)
    rec_share, heads_share = reduce_gradient(hidden, grads, scores)
    return (rec_share, heads_share[:, :CHOICES], heads_share[:, CHOICES], learner_values)


def solution(mesh):
    placed = (
        P("learn", None, "actor"),
        P("learn", None),
        P("learn"),
        P("learn", None, None, None, "actor"),
        P("learn", None, None, "actor"),
        P("learn", None, None),
        P("learn", None, None),
        P("learn", None, None),
        P("learn", None, None),
        P("learn", None, None),
        P(),
        P("learn", None),
    )
    return jax.shard_map(
        shards,
        mesh=mesh,
        in_specs=placed,
        out_specs=(P("learn", None, "actor"), P("learn", None), P("learn"), P("learn", None, None)),
        check_vma=False,
    )
```

```python
import jax
import jax.numpy as jnp
from jax import lax
from jax.experimental import pallas as pl
from jax.experimental.pallas import tpu as pltpu
from jax.sharding import PartitionSpec as P

MESH = pl.DeviceIdType.MESH
BF = jnp.bfloat16
F32 = jnp.float32
UNITS = 2048
QUARTER = 512
BATCH = 64
STEPS = 16
CHOICES = 128
WIDE = UNITS + 2 * CHOICES
VMEM = pl.BlockSpec(memory_space=pltpu.VMEM)
LIMIT = 60 * 2**20
OFFSETS = (2, -1, 1, 0)


def params(collective):
    return pltpu.CompilerParams(
        collective_id=collective, has_side_effects=True, vmem_limit_bytes=LIMIT
    )


def meet(devices):
    barrier = pltpu.get_barrier_semaphore()
    for device in devices:
        pl.semaphore_signal(barrier, inc=1, device_id=device, device_id_type=MESH)
    pl.semaphore_wait(barrier, len(devices))


class Torus:
    def __init__(self):
        place = lax.axis_index("learn")
        self.z, self.x, self.y = place // 16, lax.rem(place // 4, 4), lax.rem(place, 4)

    def device(self, dz, dx, dy):
        z = lax.rem(self.z + dz, 2)
        x = lax.rem(self.x + dx + 4, 4)
        y = lax.rem(self.y + dy + 4, 4)
        return {"learn": z * 16 + x * 4 + y}

    def first(self, half, d):
        return self.device(0, d, 0) if half == 0 else self.device(0, 0, d)

    def second(self, half, d):
        return self.device(0, 0, d) if half == 0 else self.device(0, d, 0)

    def other(self):
        return self.device(1, 0, 0)

    def neighbours(self):
        return [
            self.device(0, 1, 0),
            self.device(0, -1, 0),
            self.device(0, 0, 1),
            self.device(0, 0, -1),
            self.other(),
        ]

    def rows(self, half, plane, dp, dq, part=None):
        dx, dy = (dp, dq) if half == 0 else (dq, dp)
        block = self.device(plane, dx, dy)["learn"]
        start = block * 64 + 32 * half
        if part is None:
            return pl.ds(pl.multiple_of(start, 32), 32)
        return pl.ds(pl.multiple_of(start + 16 * part, 16), 16)


def gather_keys():
    keys = []
    for half in (0, 1):
        keys += [("p", half, d) for d in (1, -1)]
        keys += [("pf", half, d) for d in (1, -1)]
        keys += [("z", half, dp) for dp in OFFSETS]
        for plane in (0, 1):
            for dp in OFFSETS:
                keys += [("q", half, plane, dp, d) for d in (1, -1)]
                keys += [("qf", half, plane, dp, d) for d in (1, -1)]
    return {key: index for index, key in enumerate(keys)}


KEYS = gather_keys()


def gather_blocks(held, send_sems, recv_sems, work):
    torus = Torus()
    started = []

    def move(key, rows, device):
        index = KEYS[key]
        return pltpu.make_async_remote_copy(
            src_ref=held.at[rows],
            dst_ref=held.at[rows],
            send_sem=send_sems.at[index],
            recv_sem=recv_sems.at[index],
            device_id=device,
            device_id_type=MESH,
        )

    def send(key, rows, device):
        copy = move(key, rows, device)
        copy.start()
        started.append(copy)

    def arrive(key, rows):
        move(key, rows, torus.other()).wait_recv()

    left = list(range(STEPS))

    def spread(half, plane, dp):
        for d in (1, -1):
            send(("q", half, plane, dp, d), torus.rows(half, plane, dp, 0), torus.second(half, d))

    def pass_on(half, plane, dp):
        for d in (1, -1):
            part = 0 if d == 1 else 1
            arrive(("q", half, plane, dp, d), torus.rows(half, plane, dp, -d))
            send(
                ("qf", half, plane, dp, d),
                torus.rows(half, plane, dp, -d, part),
                torus.second(half, d),
            )

    def cross(half, dp):
        send(("z", half, dp), torus.rows(half, 0, dp, 0), torus.other())

    def crossed(half, dp):
        for t in left[:2]:
            work(t)
        del left[:2]
        arrive(("z", half, dp), torus.rows(half, 1, dp, 0))
        spread(half, 1, dp)

    for half in (0, 1):
        for d in (1, -1):
            send(("p", half, d), torus.rows(half, 0, 0, 0), torus.first(half, d))
    for half in (0, 1):
        cross(half, 0)
        spread(half, 0, 0)
    for half in (0, 1):
        for d in (1, -1):
            part = 0 if d == 1 else 1
            arrive(("p", half, d), torus.rows(half, 0, -d, 0))
            send(("pf", half, d), torus.rows(half, 0, -d, 0, part), torus.first(half, d))
            cross(half, -d)
    for half in (0, 1):
        for d in (1, -1):
            spread(half, 0, -d)
    for half in (0, 1):
        crossed(half, 0)
        for d in (1, -1):
            part = 0 if d == 1 else 1
            arrive(("pf", half, d), torus.rows(half, 0, -2 * d, 0, part))
        cross(half, 2)
        spread(half, 0, 2)
    for half in (0, 1):
        pass_on(half, 0, 0)
    for half in (0, 1):
        for d in (1, -1):
            crossed(half, -d)
    for half in (0, 1):
        for d in (1, -1):
            pass_on(half, 0, -d)
    for half in (0, 1):
        crossed(half, 2)
    for half in (0, 1):
        pass_on(half, 1, 0)
    for half in (0, 1):
        pass_on(half, 0, 2)
    for half in (0, 1):
        for d in (1, -1):
            pass_on(half, 1, -d)
    for half in (0, 1):
        pass_on(half, 1, 2)
    for half in (0, 1):
        for plane in (0, 1):
            for dp in OFFSETS:
                for d in (1, -1):
                    part = 0 if d == 1 else 1
                    arrive(
                        ("qf", half, plane, dp, d), torus.rows(half, plane, dp, -2 * d, part)
                    )
    for copy in started:
        copy.wait_send()


def exchange_values(torus, assigned_ref, estimate_ref, moved, send_sems, recv_sems):
    lane = lax.broadcasted_iota(jnp.int32, (STEPS, 128), 1)
    phases = (
        (0, torus.y, 2, 4, lambda d: torus.device(0, 0, d)),
        (4, torus.x, 8, 4, lambda d: torus.device(0, d, 0)),
        (8, torus.z, 32, 2, lambda d: torus.device(d, 0, 0)),
    )

    def copies(phase):
        first, _, _, size, device = phases[phase]
        return [
            pltpu.make_async_remote_copy(
                src_ref=moved.at[first],
                dst_ref=moved.at[first + d],
                send_sem=send_sems.at[first + d],
                recv_sem=recv_sems.at[first + d],
                device_id=device(d),
                device_id_type=MESH,
            )
            for d in range(1, size)
        ]

    def start(phase):
        for copy in copies(phase):
            copy.start()

    def finish(phase):
        first, place, stride, size, _ = phases[phase]
        for copy in copies(phase):
            copy.wait()
        field = lax.rem(lane // stride, size)
        result = jnp.zeros((STEPS, 128), F32)
        for d in range(size):
            source = lax.rem(place - d + size, size)
            shift = lax.rem((source - place) * stride + 128, 128)
            turned = pltpu.roll(moved[first + d], shift, 1)
            result = jnp.where(field == source, turned, result)
        return result

    def run(stage):
        if stage == 0:
            row = jnp.broadcast_to(assigned_ref[...].astype(F32), (BATCH, BATCH))
            row = jnp.concatenate([row, jnp.full((BATCH, 128 - BATCH), -1.0, F32)], axis=1)
            tall = jnp.concatenate([row, row], axis=0).T
            column = tall[0:BATCH, :]
            across = lax.broadcasted_iota(jnp.int32, (BATCH, 128), 1)
            down = lax.broadcasted_iota(jnp.int32, (BATCH, 128), 0)
            earlier = jnp.where((row == column) & (across < down), 1.0, 0.0)
            target = 2.0 * column + jnp.sum(earlier, axis=1, keepdims=True)
            spread = jnp.where(across.astype(F32) == target, 1.0, 0.0)
            moved[0] = jnp.dot(
                estimate_ref[...],
                spread,
                preferred_element_type=F32,
                precision=lax.Precision.HIGHEST,
            )
            start(0)
        elif stage < 3:
            moved[phases[stage][0]] = finish(stage - 1)
            start(stage)
        else:
            moved[6] = finish(2)

    return run


def reduce_kernel(
    hidden,
    grads,
    scores,
    assigned_ref,
    estimate_ref,
    out_ref,
    policy_ref,
    value_ref,
    values_ref,
    value_column,
    moved,
    own,
    staged,
    quarters,
    halves,
    send_sems,
    recv_sems,
    value_send,
    value_recv,
):
    torus = Torus()
    meet(torus.neighbours() + [torus.device(0, 2, 0), torus.device(0, 0, 2)])
    started = []
    where = {}
    counts = {16: 0, 32: 0}
    for key in KEYS:
        size = 16 if key[0] in ("qf", "pf") else 32
        where[key] = counts[size]
        counts[size] += 1

    def landing(key):
        size = 16 if key[0] in ("qf", "pf") else 32
        buffer = quarters if size == 16 else halves
        return buffer.at[pl.ds(where[key] * size, size)]

    def send(key, source, device):
        index = KEYS[key]
        copy = pltpu.make_async_remote_copy(
            src_ref=source,
            dst_ref=landing(key),
            send_sem=send_sems.at[index],
            recv_sem=recv_sems.at[index],
            device_id=device,
            device_id_type=MESH,
        )
        copy.start()
        started.append(copy)

    def arrived(key):
        index = KEYS[key]
        ref = landing(key)
        pltpu.make_async_remote_copy(
            src_ref=ref,
            dst_ref=ref,
            send_sem=send_sems.at[index],
            recv_sem=recv_sems.at[index],
            device_id=torus.other(),
            device_id_type=MESH,
        ).wait_recv()
        return ref[...].astype(F32)

    stage = {}

    def slot(key):
        if key not in stage:
            stage[key] = len(stage)
        return staged.at[pl.ds(stage[key] * 32, 32)]

    def multiply(plane, dx):
        first = torus.device(plane, dx, 0)["learn"] // 4
        spot = pl.ds(pl.multiple_of(first * 256, 256), 256)
        kept = hidden[0:STEPS, :, spot].reshape(STEPS * BATCH, 256)
        for k in range(4):
            part = pl.ds(k * QUARTER, QUARTER)
            own[spot, part] = lax.dot_general(
                kept,
                grads[:, :, part].reshape(STEPS * BATCH, QUARTER),
                (((0,), (0,)), ((), ())),
                preferred_element_type=F32,
            ).astype(BF)
        own[spot, UNITS:WIDE] = lax.dot_general(
            hidden[1 : STEPS + 1, :, spot].reshape(STEPS * BATCH, 256),
            scores[1 : STEPS + 1].reshape(STEPS * BATCH, 2 * CHOICES),
            (((0,), (0,)), ((), ())),
            preferred_element_type=F32,
        ).astype(BF)

    def far(half, plane, dp):
        for d in (1, -1):
            part = 0 if d == 1 else 1
            send(
                ("qf", half, plane, dp, d),
                own.at[torus.rows(half, plane, dp, -2 * d, part)],
                torus.second(half, -d),
            )

    def near(half, plane, dp, d):
        part = 0 if d == 1 else 1
        target = slot(("q", half, plane, dp, d))
        target[...] = own[torus.rows(half, plane, dp, -d), :]
        extra = arrived(("qf", half, plane, dp, d))
        rows = pl.ds(16 * part, 16)
        target[rows, :] = (target[rows, :].astype(F32) + extra).astype(BF)
        send(("q", half, plane, dp, d), target, torus.second(half, -d))

    def line(half, plane, dp):
        total = own[torus.rows(half, plane, dp, 0), :].astype(F32)
        for d in (1, -1):
            total = total + arrived(("q", half, plane, dp, d))
        return total

    def cross(half, dp):
        target = slot(("z", half, dp))
        target[...] = line(half, 1, dp).astype(BF)
        send(("z", half, dp), target, torus.other())

    def plane_sum(half, dp):
        return line(half, 0, dp) + arrived(("z", half, dp))

    exchange = exchange_values(torus, assigned_ref, estimate_ref, moved, value_send, value_recv)
    for plane in (1, 0):
        multiply(plane, 2)
        for dp in OFFSETS:
            far(1, plane, dp)
        far(0, plane, 2)
        for dp in (-1, 1, 0):
            multiply(plane, dp)
            far(0, plane, dp)
            if plane == 1 and dp == -1:
                exchange(0)
        if plane == 1:
            for dp in OFFSETS:
                for half in (0, 1):
                    for d in (1, -1):
                        near(half, 1, dp, d)
            exchange(1)
    for dp in OFFSETS:
        for half in (0, 1):
            cross(half, dp)
    exchange(2)
    for dp in OFFSETS:
        for half in (0, 1):
            for d in (1, -1):
                near(half, 0, dp, d)
    exchange(3)
    for half in (0, 1):
        target = slot(("pf", half))
        target[...] = plane_sum(half, 2).astype(BF)
        for d in (1, -1):
            part = 0 if d == 1 else 1
            send(("pf", half, d), target.at[pl.ds(16 * part, 16)], torus.first(half, -d))
    for half in (0, 1):
        for d in (1, -1):
            part = 0 if d == 1 else 1
            target = slot(("p", half, d))
            target[...] = plane_sum(half, -d).astype(BF)
            extra = arrived(("pf", half, d))
            rows = pl.ds(16 * part, 16)
            target[rows, :] = (target[rows, :].astype(F32) + extra).astype(BF)
            send(("p", half, d), target, torus.first(half, -d))
    for half in (0, 1):
        total = plane_sum(half, 0)
        for d in (1, -1):
            total = total + arrived(("p", half, d))
        rows = pl.ds(32 * half, 32)
        for k in range(4):
            out_ref[rows, k, :] = total[:, k * QUARTER : (k + 1) * QUARTER]
        policy_ref[rows, :] = total[:, UNITS : UNITS + CHOICES]
        value_column[rows, :] = total[:, UNITS + CHOICES :]
    value_ref[...] = value_column[...].T[0:1, 0:64]
    values_ref[...] = moved[6, :, 0:BATCH]
    for copy in started:
        copy.wait_send()


def reduce_gradient(hidden, grads, scores, assigned, estimates):
    quarters = sum(1 for key in KEYS if key[0] in ("qf", "pf"))
    halves = len(KEYS) - quarters
    return pl.pallas_call(
        reduce_kernel,
        out_shape=(
            jax.ShapeDtypeStruct((64, 4, QUARTER), F32),
            jax.ShapeDtypeStruct((64, CHOICES), F32),
            jax.ShapeDtypeStruct((1, 64), F32),
            jax.ShapeDtypeStruct((STEPS, BATCH), F32),
        ),
        in_specs=[VMEM] * 5,
        out_specs=(VMEM,) * 4,
        scratch_shapes=[
            pltpu.VMEM((64, 128), F32),
            pltpu.VMEM((10, STEPS, 128), F32),
            pltpu.VMEM((UNITS, WIDE), BF),
            pltpu.VMEM((46 * 32, WIDE), BF),
            pltpu.VMEM((quarters * 16, WIDE), BF),
            pltpu.VMEM((halves * 32, WIDE), BF),
            pltpu.SemaphoreType.DMA((len(KEYS),)),
            pltpu.SemaphoreType.DMA((len(KEYS),)),
            pltpu.SemaphoreType.DMA((10,)),
            pltpu.SemaphoreType.DMA((10,)),
        ],
        compiler_params=params(2),
        name="reduce_gradient",
    )(hidden, grads, scores, assigned, estimates)


def actor_peers():
    me = lax.axis_index("actor")
    core = me + 1 - 2 * lax.rem(me, 2)
    across = lax.rem(me + 2, 4)
    return me, (core, across, 3 - me)


def columns(quarter, start=0, size=QUARTER):
    return pl.ds(pl.multiple_of(quarter * QUARTER + start, min(size, 256)), size)


def sigmoid(value):
    return 0.5 * jnp.tanh(0.5 * value) + 0.5


HALF = QUARTER // 2


def train_kernel(
    block_ref,
    head_ref,
    value_ref,
    gate_ref,
    state_ref,
    counts_ref,
    start_ref,
    advantage_ref,
    return_ref,
    logprob_ref,
    action_ref,
    hidden,
    grads,
    scores,
    estimates,
    values,
    held,
    turned,
    factors,
    head_grad,
    gates,
    aux,
    preact,
    cell,
    carry_hidden,
    carry_cell,
    sent,
    got,
    sent_core,
    got_core,
    gather_send,
    gather_recv,
    step_send,
    step_recv,
    back_send,
    back_recv,
):
    torus = Torus()
    me, peers = actor_peers()
    core, across, diagonal = peers
    meet(torus.neighbours() + [{"actor": peer} for peer in peers])
    place = lax.axis_index("learn")
    mine = pl.ds(pl.multiple_of(place * 64, 64), 64)
    held[mine, 0:UNITS] = block_ref[...].reshape(64, UNITS)
    held[mine, UNITS : UNITS + CHOICES] = head_ref[...]
    line = jnp.concatenate([value_ref[...].astype(F32), jnp.zeros((1, 64), F32)], axis=1)
    held[mine, UNITS + CHOICES : WIDE] = jnp.broadcast_to(line, (128, 128)).T[0:64].astype(BF)

    def pieces(t):
        return (
            (hidden.at[t, :, columns(me)], core),
            (hidden.at[t, :, columns(me, 0, HALF)], across),
            (hidden.at[t, :, columns(me, HALF, HALF)], across),
            (hidden.at[t, :, columns(me, HALF, HALF)], diagonal),
            (hidden.at[t, :, columns(across, 0, HALF)], core),
        )

    def landed(t):
        return (
            hidden.at[t, :, columns(core)],
            hidden.at[t, :, columns(across, 0, HALF)],
            hidden.at[t, :, columns(across, HALF, HALF)],
            hidden.at[t, :, columns(diagonal, HALF, HALF)],
            hidden.at[t, :, columns(diagonal, 0, HALF)],
        )

    def step_copy(t, index):
        part, peer = pieces(t)[index]
        return pltpu.make_async_remote_copy(
            src_ref=part,
            dst_ref=part,
            send_sem=step_send.at[t, index],
            recv_sem=step_recv.at[t, index],
            device_id={"actor": peer},
            device_id_type=MESH,
        )

    def arrive(t, index):
        part = landed(t)[index]
        pltpu.make_async_remote_copy(
            src_ref=part,
            dst_ref=part,
            send_sem=step_send.at[t, index],
            recv_sem=step_recv.at[t, index],
            device_id={"actor": core},
            device_id_type=MESH,
        ).wait_recv()

    def multiply(t, spot, first=False):
        part = hidden[t, :, spot]
        for k in range(4):
            wide = pl.ds(k * QUARTER, QUARTER)
            product = jnp.dot(part, held[spot, wide], preferred_element_type=F32)
            if first:
                preact[:, wide] = product
            else:
                preact[:, wide] += product

    def column(t, kind):
        lane = lax.broadcasted_iota(jnp.int32, (BATCH, 128), 1)
        return jnp.sum(jnp.where(lane == t + 16 * kind, aux[...], 0.0), axis=1, keepdims=True)

    def heads(index):
        t = index - 1
        result = jnp.dot(hidden[index], held[:, UNITS:WIDE], preferred_element_type=F32)
        logits = result[:, 0:CHOICES]
        estimate = result[:, CHOICES : CHOICES + 1]
        share = aux[:, 80:81]
        lane = lax.broadcasted_iota(jnp.int32, (BATCH, CHOICES), 1)
        onehot = (lane.astype(F32) == column(t, 4)).astype(F32)
        shifted = logits - jnp.max(logits, axis=1, keepdims=True)
        powers = jnp.exp(shifted)
        total = jnp.sum(powers, axis=1, keepdims=True)
        chosen = jnp.sum(shifted * onehot, axis=1, keepdims=True) - jnp.log(total)
        ratio = jnp.exp(chosen - column(t, 3))
        slope = (0.5 * (ratio - 1.0) - ratio * column(t, 1)) * share
        grad_logits = slope * (onehot - powers / total)
        grad_estimate = (estimate - column(t, 2)) * share
        scores[index, :, 0:CHOICES] = grad_logits.astype(BF)
        scores[index, :, CHOICES : 2 * CHOICES] = jnp.where(lane == 0, grad_estimate, 0.0).astype(BF)
        live = (share > 0.0).astype(F32)
        values[...] = jnp.where(lane == t, estimate * live, values[...])
        head_grad[index] = lax.dot_general(
            scores[index],
            held[columns(me), UNITS:WIDE],
            (((1,), (1,)), ((), ())),
            preferred_element_type=F32,
        )

    def cells(t, half):
        keep = column(t, 0)
        for chunk in range(2 * half, 2 * half + 2):
            spot = pl.ds(chunk * 128, 128)
            kept = keep * cell[:, spot]
            inputs = []
            for k in range(4):
                wide = pl.ds(k * QUARTER + chunk * 128, 128)
                inputs.append(gates[t, :, wide].astype(F32) + keep * preact[:, wide])
            inp = sigmoid(inputs[0])
            forget = sigmoid(inputs[1])
            cand = jnp.tanh(inputs[2])
            outg = sigmoid(inputs[3])
            new_cell = forget * kept + inp * cand
            squash = jnp.tanh(new_cell)
            cell[:, spot] = new_cell
            part = pl.ds(pl.multiple_of(me * QUARTER + chunk * 128, 128), 128)
            hidden[t + 1, :, part] = (outg * squash).astype(BF)
            kept_factors = (
                outg * (1.0 - squash * squash),
                keep * cand * inp * (1.0 - inp),
                kept * forget * (1.0 - forget),
                keep * inp * (1.0 - cand * cand),
                keep * squash * outg * (1.0 - outg),
                keep * forget,
            )
            for index, value in enumerate(kept_factors):
                factors[t, index, :, spot] = value.astype(BF)

    hidden[0, :, columns(me)] = state_ref[:, 0, :]
    for index in (1, 2, 3, 0):
        step_copy(0, index).start()
    cell[...] = state_ref[:, 1, :].astype(F32)
    values[...] = jnp.zeros_like(values)
    row = lax.broadcasted_iota(jnp.int32, (BATCH, 128), 0)
    live = jnp.where(row < counts_ref[place], 1.0 / STEPS, 0.0)
    table = jnp.concatenate(
        [
            1.0 - start_ref[...].astype(F32),
            advantage_ref[...].astype(F32),
            return_ref[...].astype(F32),
            logprob_ref[...].astype(F32),
            action_ref[...].astype(F32),
            jnp.zeros((48, BATCH), F32),
        ],
        axis=0,
    )
    table = jnp.concatenate([table, jnp.zeros((128, 128 - BATCH), F32)], axis=1)
    lane = lax.broadcasted_iota(jnp.int32, (BATCH, 128), 1)
    aux[...] = jnp.where(lane < 80, table.T[0:BATCH], live)

    def unpack(t):
        gates[t] = gate_ref[:, t].reshape(BATCH, UNITS)

    gather_blocks(held, gather_send, gather_recv, unpack)

    def step(t, carry):
        multiply(t, columns(me), True)
        stripe = pl.ds(pl.multiple_of(t * 128, 128), 128)
        turned[:, stripe] = held[stripe, 0:UNITS].T
        arrive(t, 0)
        multiply(t, columns(core))

        @pl.when(t >= 2)
        def _():
            heads(t - 1)

        arrive(t, 1)
        step_copy(t, 4).start()
        multiply(t, columns(across, 0, HALF))
        arrive(t, 2)
        multiply(t, columns(across, HALF, HALF))
        arrive(t, 3)
        multiply(t, columns(diagonal, HALF, HALF))
        arrive(t, 4)
        multiply(t, columns(diagonal, 0, HALF))
        cells(t, 0)
        step_copy(t + 1, 1).start()
        cells(t, 1)
        for index in (2, 3, 0):
            step_copy(t + 1, index).start()
        for index in range(5):
            step_copy(t, index).wait_send()
        return carry

    lax.fori_loop(0, STEPS, step, 0)
    heads(STEPS - 1)
    arrive(STEPS, 1)
    step_copy(STEPS, 4).start()
    for index in (0, 2, 3, 4):
        arrive(STEPS, index)
    for index in range(5):
        step_copy(STEPS, index).wait_send()
    heads(STEPS)
    estimates[...] = jnp.concatenate([values[...], values[...]], axis=0).T[0:STEPS, 0:BATCH]

    carry_hidden[...] = jnp.zeros_like(carry_hidden)
    carry_cell[...] = jnp.zeros_like(carry_cell)

    targets = (diagonal, across, core, across, core)

    def back_copy(t, index):
        return pltpu.make_async_remote_copy(
            src_ref=sent_core.at[t] if index == 4 else sent.at[t, index],
            dst_ref=got_core.at[t] if index == 4 else got.at[t, index],
            send_sem=back_send.at[t, index],
            recv_sem=back_recv.at[t, index],
            device_id={"actor": targets[index]},
            device_id_type=MESH,
        )

    def cell_back(t):
        for chunk in range(QUARTER // 128):
            spot = pl.ds(chunk * 128, 128)
            factor = [factors[t, index, :, spot].astype(F32) for index in range(6)]
            total = head_grad[t + 1, :, spot] + carry_hidden[:, spot]
            dcell = carry_cell[:, spot] + total * factor[0]
            carry_cell[:, spot] = dcell * factor[5]
            parts = (dcell * factor[1], dcell * factor[2], dcell * factor[3], total * factor[4])
            for k, part in enumerate(parts):
                grads[t, :, pl.ds(k * QUARTER + chunk * 128, 128)] = part.astype(BF)

    def product(t, spot):
        return jnp.dot(grads[t], turned[:, spot], preferred_element_type=F32)

    def back(i, carry):
        t = STEPS - 1 - i
        cell_back(t)
        for index, quarter, start in ((2, diagonal, HALF), (0, diagonal, 0), (1, across, 0)):
            sent[t, index] = product(t, columns(quarter, start, HALF)).astype(BF)
            back_copy(t, index).start()
        part = product(t, columns(across, HALF, HALF))
        sent_core[t] = product(t, columns(core)).astype(BF)
        back_copy(t, 4).start()
        back_copy(t, 2).wait_recv()
        sent[t, 3] = (part + got[t, 2].astype(F32)).astype(BF)
        back_copy(t, 3).start()
        carry_hidden[...] = product(t, columns(me))
        back_copy(t, 4).wait_recv()
        carry_hidden[...] += got_core[t].astype(F32)
        for index in (0, 1):
            back_copy(t, index).wait_recv()
        carry_hidden[:, 0:HALF] += got[t, 0].astype(F32) + got[t, 1].astype(F32)
        back_copy(t, 3).wait_recv()
        carry_hidden[:, HALF:QUARTER] += got[t, 3].astype(F32)
        for index in range(5):
            back_copy(t, index).wait_send()
        return carry

    lax.fori_loop(0, STEPS - 1, back, 0)
    cell_back(0)


def train(*operands):
    specs = [VMEM] * len(operands)
    specs[5] = pl.BlockSpec(memory_space=pltpu.SMEM)
    return pl.pallas_call(
        train_kernel,
        out_shape=(
            jax.ShapeDtypeStruct((STEPS + 1, BATCH, UNITS), BF),
            jax.ShapeDtypeStruct((STEPS, BATCH, UNITS), BF),
            jax.ShapeDtypeStruct((STEPS + 1, BATCH, 2 * CHOICES), BF),
            jax.ShapeDtypeStruct((STEPS, BATCH), F32),
        ),
        in_specs=specs,
        out_specs=(VMEM,) * 4,
        scratch_shapes=[
            pltpu.VMEM((BATCH, 128), F32),
            pltpu.VMEM((UNITS, WIDE), BF),
            pltpu.VMEM((UNITS, UNITS), BF),
            pltpu.VMEM((STEPS, 6, BATCH, QUARTER), BF),
            pltpu.VMEM((STEPS + 1, BATCH, QUARTER), F32),
            pltpu.VMEM((STEPS, BATCH, UNITS), BF),
            pltpu.VMEM((BATCH, 128), F32),
            pltpu.VMEM((BATCH, UNITS), F32),
            pltpu.VMEM((BATCH, QUARTER), F32),
            pltpu.VMEM((BATCH, QUARTER), F32),
            pltpu.VMEM((BATCH, QUARTER), F32),
            pltpu.VMEM((STEPS, 4, BATCH, HALF), BF),
            pltpu.VMEM((STEPS, 4, BATCH, HALF), BF),
            pltpu.VMEM((STEPS, BATCH, QUARTER), BF),
            pltpu.VMEM((STEPS, BATCH, QUARTER), BF),
            pltpu.SemaphoreType.DMA((len(KEYS),)),
            pltpu.SemaphoreType.DMA((len(KEYS),)),
            pltpu.SemaphoreType.DMA((STEPS + 1, 5)),
            pltpu.SemaphoreType.DMA((STEPS + 1, 5)),
            pltpu.SemaphoreType.DMA((STEPS, 5)),
            pltpu.SemaphoreType.DMA((STEPS, 5)),
        ],
        compiler_params=params(1),
        name="train",
    )(*operands)


def shards(
    rec_weight,
    head_weight,
    value_head,
    gate_inputs,
    start_state,
    advantages,
    returns,
    old_logprob,
    taken_action,
    episode_start,
    segment_counts,
    assignment,
):
    hidden, grads, scores, estimates = train(
        rec_weight,
        head_weight,
        value_head[None],
        gate_inputs[0],
        start_state[0],
        segment_counts,
        episode_start[0].T,
        advantages[0].T,
        returns[0].T,
        old_logprob[0].T,
        taken_action[0].T,
    )
    rec_share, policy_share, value_share, values = reduce_gradient(
        hidden, grads, scores, assignment, estimates
    )
    return (rec_share, policy_share, value_share[0], values.T[None])


def solution(mesh):
    placed = (
        P("learn", None, "actor"),
        P("learn", None),
        P("learn"),
        P("learn", None, None, None, "actor"),
        P("learn", None, None, "actor"),
        P("learn", None, None),
        P("learn", None, None),
        P("learn", None, None),
        P("learn", None, None),
        P("learn", None, None),
        P(),
        P("learn", None),
    )
    return jax.shard_map(
        shards,
        mesh=mesh,
        in_specs=placed,
        out_specs=(P("learn", None, "actor"), P("learn", None), P("learn"), P("learn", None, None)),
        check_vma=False,
    )
```

```python
import jax
import jax.numpy as jnp
from jax import lax
from jax.experimental import pallas as pl
from jax.experimental.pallas import tpu as pltpu
from jax.sharding import PartitionSpec as P

MESH = pl.DeviceIdType.MESH
BF = jnp.bfloat16
F32 = jnp.float32
UNITS = 2048
QUARTER = 512
BATCH = 64
STEPS = 16
CHOICES = 128
WIDE = UNITS + 2 * CHOICES
VMEM = pl.BlockSpec(memory_space=pltpu.VMEM)
LIMIT = 60 * 2**20
OFFSETS = (2, -1, 1, 0)


def params(collective):
    return pltpu.CompilerParams(
        collective_id=collective, has_side_effects=True, vmem_limit_bytes=LIMIT
    )


def meet(devices):
    barrier = pltpu.get_barrier_semaphore()
    for device in devices:
        pl.semaphore_signal(barrier, inc=1, device_id=device, device_id_type=MESH)
    pl.semaphore_wait(barrier, len(devices))


class Torus:
    def __init__(self):
        place = lax.axis_index("learn")
        self.z, self.x, self.y = place // 16, lax.rem(place // 4, 4), lax.rem(place, 4)

    def device(self, dz, dx, dy):
        z = lax.rem(self.z + dz, 2)
        x = lax.rem(self.x + dx + 4, 4)
        y = lax.rem(self.y + dy + 4, 4)
        return {"learn": z * 16 + x * 4 + y}

    def first(self, half, d):
        return self.device(0, d, 0) if half == 0 else self.device(0, 0, d)

    def second(self, half, d):
        return self.device(0, 0, d) if half == 0 else self.device(0, d, 0)

    def other(self):
        return self.device(1, 0, 0)

    def neighbours(self):
        return [
            self.device(0, 1, 0),
            self.device(0, -1, 0),
            self.device(0, 0, 1),
            self.device(0, 0, -1),
            self.other(),
        ]

    def rows(self, half, plane, dp, dq, part=None):
        dx, dy = (dp, dq) if half == 0 else (dq, dp)
        block = self.device(plane, dx, dy)["learn"]
        start = block * 64 + 32 * half
        if part is None:
            return pl.ds(pl.multiple_of(start, 32), 32)
        return pl.ds(pl.multiple_of(start + 16 * part, 16), 16)


def gather_keys():
    keys = []
    for half in (0, 1):
        keys += [("p", half, d) for d in (1, -1)]
        keys += [("pf", half, d) for d in (1, -1)]
        keys += [("z", half, dp) for dp in OFFSETS]
        for plane in (0, 1):
            for dp in OFFSETS:
                keys += [("q", half, plane, dp, d) for d in (1, -1)]
                keys += [("qf", half, plane, dp, d) for d in (1, -1)]
    return {key: index for index, key in enumerate(keys)}


KEYS = gather_keys()


def gather_blocks(held, send_sems, recv_sems, work):
    torus = Torus()
    started = []

    def move(key, rows, device):
        index = KEYS[key]
        return pltpu.make_async_remote_copy(
            src_ref=held.at[rows],
            dst_ref=held.at[rows],
            send_sem=send_sems.at[index],
            recv_sem=recv_sems.at[index],
            device_id=device,
            device_id_type=MESH,
        )

    def send(key, rows, device):
        copy = move(key, rows, device)
        copy.start()
        started.append(copy)

    def arrive(key, rows):
        move(key, rows, torus.other()).wait_recv()

    left = list(range(STEPS))

    def spread(half, plane, dp):
        for d in (1, -1):
            send(("q", half, plane, dp, d), torus.rows(half, plane, dp, 0), torus.second(half, d))

    def pass_on(half, plane, dp):
        for d in (1, -1):
            part = 0 if d == 1 else 1
            arrive(("q", half, plane, dp, d), torus.rows(half, plane, dp, -d))
            send(
                ("qf", half, plane, dp, d),
                torus.rows(half, plane, dp, -d, part),
                torus.second(half, d),
            )

    def cross(half, dp):
        send(("z", half, dp), torus.rows(half, 0, dp, 0), torus.other())

    def crossed(half, dp):
        for t in left[:2]:
            work(t)
        del left[:2]
        arrive(("z", half, dp), torus.rows(half, 1, dp, 0))
        spread(half, 1, dp)

    for half in (0, 1):
        for d in (1, -1):
            send(("p", half, d), torus.rows(half, 0, 0, 0), torus.first(half, d))
    for half in (0, 1):
        cross(half, 0)
        spread(half, 0, 0)
    for half in (0, 1):
        for d in (1, -1):
            part = 0 if d == 1 else 1
            arrive(("p", half, d), torus.rows(half, 0, -d, 0))
            send(("pf", half, d), torus.rows(half, 0, -d, 0, part), torus.first(half, d))
            cross(half, -d)
    for half in (0, 1):
        for d in (1, -1):
            spread(half, 0, -d)
    for half in (0, 1):
        crossed(half, 0)
        for d in (1, -1):
            part = 0 if d == 1 else 1
            arrive(("pf", half, d), torus.rows(half, 0, -2 * d, 0, part))
        cross(half, 2)
        spread(half, 0, 2)
    for half in (0, 1):
        pass_on(half, 0, 0)
    for half in (0, 1):
        for d in (1, -1):
            crossed(half, -d)
    for half in (0, 1):
        for d in (1, -1):
            pass_on(half, 0, -d)
    for half in (0, 1):
        crossed(half, 2)
    for half in (0, 1):
        pass_on(half, 1, 0)
    for half in (0, 1):
        pass_on(half, 0, 2)
    for half in (0, 1):
        for d in (1, -1):
            pass_on(half, 1, -d)
    for half in (0, 1):
        pass_on(half, 1, 2)
    for half in (0, 1):
        for plane in (0, 1):
            for dp in OFFSETS:
                for d in (1, -1):
                    part = 0 if d == 1 else 1
                    arrive(
                        ("qf", half, plane, dp, d), torus.rows(half, plane, dp, -2 * d, part)
                    )
    for copy in started:
        copy.wait_send()


def exchange_values(torus, assigned_ref, estimates, moved, send_sems, recv_sems):
    lane = lax.broadcasted_iota(jnp.int32, (STEPS, 128), 1)
    phases = (
        (0, torus.y, 2, 4, lambda d: torus.device(0, 0, d)),
        (4, torus.x, 8, 4, lambda d: torus.device(0, d, 0)),
        (8, torus.z, 32, 2, lambda d: torus.device(d, 0, 0)),
    )

    def copies(phase):
        first, _, _, size, device = phases[phase]
        return [
            pltpu.make_async_remote_copy(
                src_ref=moved.at[first],
                dst_ref=moved.at[first + d],
                send_sem=send_sems.at[first + d],
                recv_sem=recv_sems.at[first + d],
                device_id=device(d),
                device_id_type=MESH,
            )
            for d in range(1, size)
        ]

    def start(phase):
        for copy in copies(phase):
            copy.start()

    def finish(phase):
        first, place, stride, size, _ = phases[phase]
        for copy in copies(phase):
            copy.wait()
        field = lax.rem(lane // stride, size)
        result = jnp.zeros((STEPS, 128), F32)
        for d in range(size):
            source = lax.rem(place - d + size, size)
            shift = lax.rem((source - place) * stride + 128, 128)
            turned = pltpu.roll(moved[first + d], shift, 1)
            result = jnp.where(field == source, turned, result)
        return result

    def run(stage):
        if stage == 0:
            row = jnp.broadcast_to(assigned_ref[...].astype(F32), (BATCH, BATCH))
            row = jnp.concatenate([row, jnp.full((BATCH, 128 - BATCH), -1.0, F32)], axis=1)
            tall = jnp.concatenate([row, row], axis=0).T
            column = tall[0:BATCH, :]
            across = lax.broadcasted_iota(jnp.int32, (BATCH, 128), 1)
            down = lax.broadcasted_iota(jnp.int32, (BATCH, 128), 0)
            earlier = jnp.where((row == column) & (across < down), 1.0, 0.0)
            target = 2.0 * column + jnp.sum(earlier, axis=1, keepdims=True)
            spread = jnp.where(across.astype(F32) == target, 1.0, 0.0)
            moved[0] = jnp.dot(
                estimates,
                spread,
                preferred_element_type=F32,
                precision=lax.Precision.HIGHEST,
            )
            start(0)
        elif stage < 3:
            moved[phases[stage][0]] = finish(stage - 1)
            start(stage)
        else:
            moved[6] = finish(2)

    return run


def reduce_blocks(
    torus,
    hidden,
    grads,
    scores,
    exchange,
    out_ref,
    policy_ref,
    value_ref,
    value_column,
    own,
    arena,
    send_sems,
    recv_sems,
):
    started = []
    where = {}
    counts = {16: 0, 32: 0}
    for key in KEYS:
        size = 16 if key[0] in ("qf", "pf") else 32
        where[key] = counts[size]
        counts[size] += 1

    def landing(key):
        size = 16 if key[0] in ("qf", "pf") else 32
        base = 0 if size == 32 else counts[32] * 32
        return arena.at[pl.ds(base + where[key] * size, size)]

    def send(key, source, device):
        index = KEYS[key]
        copy = pltpu.make_async_remote_copy(
            src_ref=source,
            dst_ref=landing(key),
            send_sem=send_sems.at[index],
            recv_sem=recv_sems.at[index],
            device_id=device,
            device_id_type=MESH,
        )
        copy.start()
        started.append(copy)

    def arrived(key):
        index = KEYS[key]
        ref = landing(key)
        pltpu.make_async_remote_copy(
            src_ref=ref,
            dst_ref=ref,
            send_sem=send_sems.at[index],
            recv_sem=recv_sems.at[index],
            device_id=torus.other(),
            device_id_type=MESH,
        ).wait_recv()
        return ref[...].astype(F32)

    def multiply(plane, dx):
        first = torus.device(plane, dx, 0)["learn"] // 4
        spot = pl.ds(pl.multiple_of(first * 256, 256), 256)
        kept = hidden[0:STEPS, :, spot].reshape(STEPS * BATCH, 256)
        for k in range(4):
            part = pl.ds(k * QUARTER, QUARTER)
            own[spot, part] = lax.dot_general(
                kept,
                grads[:, :, part].reshape(STEPS * BATCH, QUARTER),
                (((0,), (0,)), ((), ())),
                preferred_element_type=F32,
            ).astype(BF)
        own[spot, UNITS:WIDE] = lax.dot_general(
            hidden[1 : STEPS + 1, :, spot].reshape(STEPS * BATCH, 256),
            scores[1 : STEPS + 1].reshape(STEPS * BATCH, 2 * CHOICES),
            (((0,), (0,)), ((), ())),
            preferred_element_type=F32,
        ).astype(BF)

    def far(half, plane, dp):
        for d in (1, -1):
            part = 0 if d == 1 else 1
            send(
                ("qf", half, plane, dp, d),
                own.at[torus.rows(half, plane, dp, -2 * d, part)],
                torus.second(half, -d),
            )

    def near(half, plane, dp, d):
        part = 0 if d == 1 else 1
        extra = arrived(("qf", half, plane, dp, d))
        rows = torus.rows(half, plane, dp, -d, part)
        own[rows, :] = (own[rows, :].astype(F32) + extra).astype(BF)
        block = own.at[torus.rows(half, plane, dp, -d)]
        send(("q", half, plane, dp, d), block, torus.second(half, -d))

    def line(half, plane, dp):
        total = own[torus.rows(half, plane, dp, 0), :].astype(F32)
        for d in (1, -1):
            total = total + arrived(("q", half, plane, dp, d))
        return total

    def cross(half, dp):
        rows = torus.rows(half, 1, dp, 0)
        own[rows, :] = line(half, 1, dp).astype(BF)
        send(("z", half, dp), own.at[rows], torus.other())

    def plane_sum(half, dp):
        return line(half, 0, dp) + arrived(("z", half, dp))

    def product(plane, dp):
        multiply(plane, dp)
        if dp == 2:
            for other in OFFSETS:
                far(1, plane, other)
        far(0, plane, dp)

    for dp in OFFSETS:
        product(1, dp)
        if dp == 2:
            exchange(0)
    for dp in OFFSETS:
        for half in (0, 1):
            for d in (1, -1):
                near(half, 1, dp, d)
    exchange(1)
    for dp in OFFSETS:
        product(0, dp)
        for half in (0, 1):
            cross(half, dp)
    exchange(2)
    for dp in OFFSETS:
        for half in (0, 1):
            for d in (1, -1):
                near(half, 0, dp, d)
    exchange(3)
    for half in (0, 1):
        own[torus.rows(half, 0, 2, 0), :] = plane_sum(half, 2).astype(BF)
        for d in (1, -1):
            part = 0 if d == 1 else 1
            block = own.at[torus.rows(half, 0, 2, 0, part)]
            send(("pf", half, d), block, torus.first(half, -d))
    for half in (0, 1):
        for d in (1, -1):
            part = 0 if d == 1 else 1
            rows = torus.rows(half, 0, -d, 0)
            own[rows, :] = plane_sum(half, -d).astype(BF)
            extra = arrived(("pf", half, d))
            some = torus.rows(half, 0, -d, 0, part)
            own[some, :] = (own[some, :].astype(F32) + extra).astype(BF)
            send(("p", half, d), own.at[rows], torus.first(half, -d))
    for half in (0, 1):
        total = plane_sum(half, 0)
        for d in (1, -1):
            total = total + arrived(("p", half, d))
        rows = pl.ds(32 * half, 32)
        for k in range(4):
            out_ref[rows, k, :] = total[:, k * QUARTER : (k + 1) * QUARTER]
        policy_ref[rows, :] = total[:, UNITS : UNITS + CHOICES]
        value_column[rows, :] = total[:, UNITS + CHOICES :]
    value_ref[...] = value_column[...].T[0:1, 0:64]
    for copy in started:
        copy.wait_send()


def actor_peers():
    me = lax.axis_index("actor")
    core = me + 1 - 2 * lax.rem(me, 2)
    across = lax.rem(me + 2, 4)
    return me, (core, across, 3 - me)


def columns(quarter, start=0, size=QUARTER):
    return pl.ds(pl.multiple_of(quarter * QUARTER + start, min(size, 256)), size)


def sigmoid(value):
    return 0.5 * jnp.tanh(0.5 * value) + 0.5


HALF = QUARTER // 2


def train_kernel(
    block_ref,
    head_ref,
    value_ref,
    gate_ref,
    state_ref,
    counts_ref,
    start_ref,
    advantage_ref,
    return_ref,
    logprob_ref,
    action_ref,
    assigned_ref,
    out_ref,
    policy_ref,
    value_out_ref,
    values_ref,
    hidden,
    grads,
    scores,
    values,
    value_column,
    moved,
    held,
    arena,
    factors,
    head_grad,
    gates,
    aux,
    preact,
    cell,
    carry_hidden,
    carry_cell,
    sent,
    got,
    sent_core,
    got_core,
    gather_send,
    gather_recv,
    step_send,
    step_recv,
    back_send,
    back_recv,
    reduce_send,
    reduce_recv,
    value_send,
    value_recv,
    ready,
):
    torus = Torus()
    me, peers = actor_peers()
    core, across, diagonal = peers
    far_devices = [torus.device(0, 2, 0), torus.device(0, 0, 2)]
    meet(torus.neighbours() + far_devices + [{"actor": peer} for peer in peers])
    place = lax.axis_index("learn")
    mine = pl.ds(pl.multiple_of(place * 64, 64), 64)
    held[mine, 0:UNITS] = block_ref[...].reshape(64, UNITS)
    held[mine, UNITS : UNITS + CHOICES] = head_ref[...]
    line = jnp.concatenate([value_ref[...].astype(F32), jnp.zeros((1, 64), F32)], axis=1)
    held[mine, UNITS + CHOICES : WIDE] = jnp.broadcast_to(line, (128, 128)).T[0:64].astype(BF)

    def pieces(t):
        return (
            (hidden.at[t, :, columns(me)], core),
            (hidden.at[t, :, columns(me, 0, HALF)], across),
            (hidden.at[t, :, columns(me, HALF, HALF)], across),
            (hidden.at[t, :, columns(me, HALF, HALF)], diagonal),
            (hidden.at[t, :, columns(across, 0, HALF)], core),
        )

    def landed(t):
        return (
            hidden.at[t, :, columns(core)],
            hidden.at[t, :, columns(across, 0, HALF)],
            hidden.at[t, :, columns(across, HALF, HALF)],
            hidden.at[t, :, columns(diagonal, HALF, HALF)],
            hidden.at[t, :, columns(diagonal, 0, HALF)],
        )

    def step_copy(t, index):
        part, peer = pieces(t)[index]
        return pltpu.make_async_remote_copy(
            src_ref=part,
            dst_ref=part,
            send_sem=step_send.at[t, index],
            recv_sem=step_recv.at[t, index],
            device_id={"actor": peer},
            device_id_type=MESH,
        )

    def arrive(t, index):
        part = landed(t)[index]
        pltpu.make_async_remote_copy(
            src_ref=part,
            dst_ref=part,
            send_sem=step_send.at[t, index],
            recv_sem=step_recv.at[t, index],
            device_id={"actor": core},
            device_id_type=MESH,
        ).wait_recv()

    def multiply(t, spot, first=False):
        part = hidden[t, :, spot]
        for k in range(4):
            wide = pl.ds(k * QUARTER, QUARTER)
            product = jnp.dot(part, held[spot, wide], preferred_element_type=F32)
            if first:
                preact[:, wide] = product
            else:
                preact[:, wide] += product

    def column(t, kind):
        lane = lax.broadcasted_iota(jnp.int32, (BATCH, 128), 1)
        return jnp.sum(jnp.where(lane == t + 16 * kind, aux[...], 0.0), axis=1, keepdims=True)

    def heads(index):
        t = index - 1
        result = jnp.dot(hidden[index], held[:, UNITS:WIDE], preferred_element_type=F32)
        logits = result[:, 0:CHOICES]
        estimate = result[:, CHOICES : CHOICES + 1]
        share = aux[:, 80:81]
        lane = lax.broadcasted_iota(jnp.int32, (BATCH, CHOICES), 1)
        onehot = (lane.astype(F32) == column(t, 4)).astype(F32)
        shifted = logits - jnp.max(logits, axis=1, keepdims=True)
        powers = jnp.exp(shifted)
        total = jnp.sum(powers, axis=1, keepdims=True)
        chosen = jnp.sum(shifted * onehot, axis=1, keepdims=True) - jnp.log(total)
        ratio = jnp.exp(chosen - column(t, 3))
        slope = (0.5 * (ratio - 1.0) - ratio * column(t, 1)) * share
        grad_logits = slope * (onehot - powers / total)
        grad_estimate = (estimate - column(t, 2)) * share
        scores[index, :, 0:CHOICES] = grad_logits.astype(BF)
        scores[index, :, CHOICES : 2 * CHOICES] = jnp.where(lane == 0, grad_estimate, 0.0).astype(BF)
        live = (share > 0.0).astype(F32)
        values[...] = jnp.where(lane == t, estimate * live, values[...])
        head_grad[index] = lax.dot_general(
            scores[index],
            held[columns(me), UNITS:WIDE],
            (((1,), (1,)), ((), ())),
            preferred_element_type=F32,
        )

    def cells(t, half):
        keep = column(t, 0)
        for chunk in range(2 * half, 2 * half + 2):
            spot = pl.ds(chunk * 128, 128)
            kept = keep * cell[:, spot]
            inputs = []
            for k in range(4):
                wide = pl.ds(k * QUARTER + chunk * 128, 128)
                inputs.append(gates[t, :, wide].astype(F32) + keep * preact[:, wide])
            inp = sigmoid(inputs[0])
            forget = sigmoid(inputs[1])
            cand = jnp.tanh(inputs[2])
            outg = sigmoid(inputs[3])
            new_cell = forget * kept + inp * cand
            squash = jnp.tanh(new_cell)
            cell[:, spot] = new_cell
            part = pl.ds(pl.multiple_of(me * QUARTER + chunk * 128, 128), 128)
            hidden[t + 1, :, part] = (outg * squash).astype(BF)
            kept_factors = (
                outg * (1.0 - squash * squash),
                keep * cand * inp * (1.0 - inp),
                kept * forget * (1.0 - forget),
                keep * inp * (1.0 - cand * cand),
                keep * squash * outg * (1.0 - outg),
                keep * forget,
            )
            for index, value in enumerate(kept_factors):
                factors[t, index, :, spot] = value.astype(BF)

    hidden[0, :, columns(me)] = state_ref[:, 0, :]
    for index in (1, 2, 3, 0):
        step_copy(0, index).start()
    cell[...] = state_ref[:, 1, :].astype(F32)
    values[...] = jnp.zeros_like(values)
    row = lax.broadcasted_iota(jnp.int32, (BATCH, 128), 0)
    live = jnp.where(row < counts_ref[place], 1.0 / STEPS, 0.0)
    table = jnp.concatenate(
        [
            1.0 - start_ref[...].astype(F32),
            advantage_ref[...].astype(F32),
            return_ref[...].astype(F32),
            logprob_ref[...].astype(F32),
            action_ref[...].astype(F32),
            jnp.zeros((48, BATCH), F32),
        ],
        axis=0,
    )
    table = jnp.concatenate([table, jnp.zeros((128, 128 - BATCH), F32)], axis=1)
    lane = lax.broadcasted_iota(jnp.int32, (BATCH, 128), 1)
    aux[...] = jnp.where(lane < 80, table.T[0:BATCH], live)

    def unpack(t):
        gates[t] = gate_ref[:, t].reshape(BATCH, UNITS)

    gather_blocks(held, gather_send, gather_recv, unpack)

    def step(t, carry):
        multiply(t, columns(me), True)
        stripe = pl.ds(pl.multiple_of(t * 128, 128), 128)
        arena[:, stripe] = held[stripe, 0:UNITS].T
        arrive(t, 0)
        multiply(t, columns(core))

        @pl.when(t >= 2)
        def _():
            heads(t - 1)

        arrive(t, 1)
        step_copy(t, 4).start()
        multiply(t, columns(across, 0, HALF))
        arrive(t, 2)
        multiply(t, columns(across, HALF, HALF))
        arrive(t, 3)
        multiply(t, columns(diagonal, HALF, HALF))
        arrive(t, 4)
        multiply(t, columns(diagonal, 0, HALF))
        cells(t, 0)
        step_copy(t + 1, 1).start()
        cells(t, 1)
        for index in (2, 3, 0):
            step_copy(t + 1, index).start()
        for index in range(5):
            step_copy(t, index).wait_send()
        return carry

    lax.fori_loop(0, STEPS, step, 0)
    heads(STEPS - 1)
    arrive(STEPS, 1)
    step_copy(STEPS, 4).start()
    for index in (0, 2, 3, 4):
        arrive(STEPS, index)
    for index in range(5):
        step_copy(STEPS, index).wait_send()
    heads(STEPS)

    carry_hidden[...] = jnp.zeros_like(carry_hidden)
    carry_cell[...] = jnp.zeros_like(carry_cell)

    targets = (diagonal, across, core, across, core)

    def back_copy(t, index):
        return pltpu.make_async_remote_copy(
            src_ref=sent_core.at[t] if index == 4 else sent.at[t, index],
            dst_ref=got_core.at[t] if index == 4 else got.at[t, index],
            send_sem=back_send.at[t, index],
            recv_sem=back_recv.at[t, index],
            device_id={"actor": targets[index]},
            device_id_type=MESH,
        )

    def cell_back(t):
        for chunk in range(QUARTER // 128):
            spot = pl.ds(chunk * 128, 128)
            factor = [factors[t, index, :, spot].astype(F32) for index in range(6)]
            total = head_grad[t + 1, :, spot] + carry_hidden[:, spot]
            dcell = carry_cell[:, spot] + total * factor[0]
            carry_cell[:, spot] = dcell * factor[5]
            parts = (dcell * factor[1], dcell * factor[2], dcell * factor[3], total * factor[4])
            for k, part in enumerate(parts):
                grads[t, :, pl.ds(k * QUARTER + chunk * 128, 128)] = part.astype(BF)

    def product(t, spot):
        return jnp.dot(grads[t], arena[:, spot], preferred_element_type=F32)

    def back(i, carry):
        t = STEPS - 1 - i
        cell_back(t)
        for index, quarter, start in ((2, diagonal, HALF), (0, diagonal, 0), (1, across, 0)):
            sent[t, index] = product(t, columns(quarter, start, HALF)).astype(BF)
            back_copy(t, index).start()
        part = product(t, columns(across, HALF, HALF))
        sent_core[t] = product(t, columns(core)).astype(BF)
        back_copy(t, 4).start()
        back_copy(t, 2).wait_recv()
        sent[t, 3] = (part + got[t, 2].astype(F32)).astype(BF)
        back_copy(t, 3).start()
        carry_hidden[...] = product(t, columns(me))
        back_copy(t, 4).wait_recv()
        carry_hidden[...] += got_core[t].astype(F32)
        for index in (0, 1):
            back_copy(t, index).wait_recv()
        carry_hidden[:, 0:HALF] += got[t, 0].astype(F32) + got[t, 1].astype(F32)
        back_copy(t, 3).wait_recv()
        carry_hidden[:, HALF:QUARTER] += got[t, 3].astype(F32)
        for index in range(5):
            back_copy(t, index).wait_send()
        return carry

    lax.fori_loop(0, STEPS - 1, back, 0)
    for device in torus.neighbours():
        pl.semaphore_signal(ready, inc=1, device_id=device, device_id_type=MESH)
    cell_back(0)
    pl.semaphore_wait(ready, 5)
    estimates = jnp.concatenate([values[...], values[...]], axis=0).T[0:STEPS, 0:BATCH]
    exchange = exchange_values(torus, assigned_ref, estimates, moved, value_send, value_recv)
    reduce_blocks(
        torus,
        hidden,
        grads,
        scores,
        exchange,
        out_ref,
        policy_ref,
        value_out_ref,
        value_column,
        held,
        arena,
        reduce_send,
        reduce_recv,
    )
    values_ref[...] = moved[6, :, 0:BATCH]


RESULTS = (
    jax.ShapeDtypeStruct((64, 4, QUARTER), F32),
    jax.ShapeDtypeStruct((64, CHOICES), F32),
    jax.ShapeDtypeStruct((1, 64), F32),
    jax.ShapeDtypeStruct((STEPS, BATCH), F32),
)


def hand_on_kernel(*refs):
    for source, target in zip(refs[:4], refs[4:]):
        target[...] = source[...]


def hand_on(*results):
    return pl.pallas_call(
        hand_on_kernel,
        out_shape=RESULTS,
        in_specs=[VMEM] * 4,
        out_specs=(VMEM,) * 4,
        name="hand_on",
    )(*results)


def train(*operands):
    specs = [VMEM] * len(operands)
    specs[5] = pl.BlockSpec(memory_space=pltpu.SMEM)
    return pl.pallas_call(
        train_kernel,
        out_shape=RESULTS,
        in_specs=specs,
        out_specs=(VMEM,) * 4,
        scratch_shapes=[
            pltpu.VMEM((STEPS + 1, BATCH, UNITS), BF),
            pltpu.VMEM((STEPS, BATCH, UNITS), BF),
            pltpu.VMEM((STEPS + 1, BATCH, 2 * CHOICES), BF),
            pltpu.VMEM((BATCH, 128), F32),
            pltpu.VMEM((64, 128), F32),
            pltpu.VMEM((10, STEPS, 128), F32),
            pltpu.VMEM((UNITS, WIDE), BF),
            pltpu.VMEM((UNITS, WIDE), BF),
            pltpu.VMEM((STEPS, 6, BATCH, QUARTER), BF),
            pltpu.VMEM((STEPS + 1, BATCH, QUARTER), F32),
            pltpu.VMEM((STEPS, BATCH, UNITS), BF),
            pltpu.VMEM((BATCH, 128), F32),
            pltpu.VMEM((BATCH, UNITS), F32),
            pltpu.VMEM((BATCH, QUARTER), F32),
            pltpu.VMEM((BATCH, QUARTER), F32),
            pltpu.VMEM((BATCH, QUARTER), F32),
            pltpu.VMEM((STEPS, 4, BATCH, HALF), BF),
            pltpu.VMEM((STEPS, 4, BATCH, HALF), BF),
            pltpu.VMEM((STEPS, BATCH, QUARTER), BF),
            pltpu.VMEM((STEPS, BATCH, QUARTER), BF),
            pltpu.SemaphoreType.DMA((len(KEYS),)),
            pltpu.SemaphoreType.DMA((len(KEYS),)),
            pltpu.SemaphoreType.DMA((STEPS + 1, 5)),
            pltpu.SemaphoreType.DMA((STEPS + 1, 5)),
            pltpu.SemaphoreType.DMA((STEPS, 5)),
            pltpu.SemaphoreType.DMA((STEPS, 5)),
            pltpu.SemaphoreType.DMA((len(KEYS),)),
            pltpu.SemaphoreType.DMA((len(KEYS),)),
            pltpu.SemaphoreType.DMA((10,)),
            pltpu.SemaphoreType.DMA((10,)),
            pltpu.SemaphoreType.REGULAR,
        ],
        compiler_params=params(1),
        name="train",
    )(*operands)


def shards(
    rec_weight,
    head_weight,
    value_head,
    gate_inputs,
    start_state,
    advantages,
    returns,
    old_logprob,
    taken_action,
    episode_start,
    segment_counts,
    assignment,
):
    results = train(
        rec_weight,
        head_weight,
        value_head[None],
        gate_inputs[0],
        start_state[0],
        segment_counts,
        episode_start[0].T,
        advantages[0].T,
        returns[0].T,
        old_logprob[0].T,
        taken_action[0].T,
        assignment,
    )
    rec_share, policy_share, value_share, values = hand_on(*results)
    return (rec_share, policy_share, value_share[0], values.T[None])


def solution(mesh):
    placed = (
        P("learn", None, "actor"),
        P("learn", None),
        P("learn"),
        P("learn", None, None, None, "actor"),
        P("learn", None, None, "actor"),
        P("learn", None, None),
        P("learn", None, None),
        P("learn", None, None),
        P("learn", None, None),
        P("learn", None, None),
        P(),
        P("learn", None),
    )
    return jax.shard_map(
        shards,
        mesh=mesh,
        in_specs=placed,
        out_specs=(P("learn", None, "actor"), P("learn", None), P("learn"), P("learn", None, None)),
        check_vma=False,
    )
```

```python
import jax
import jax.numpy as jnp
from jax import lax
from jax.experimental import pallas as pl
from jax.experimental.pallas import tpu as pltpu
from jax.sharding import PartitionSpec as P

MESH = pl.DeviceIdType.MESH
BF = jnp.bfloat16
F32 = jnp.float32
UNITS = 2048
QUARTER = 512
BATCH = 64
STEPS = 16
CHOICES = 128
PAIR = 2 * CHOICES
VMEM = pl.BlockSpec(memory_space=pltpu.VMEM)
LIMIT = 60 * 2**20
OFFSETS = (2, -1, 1, 0)


def params(collective):
    return pltpu.CompilerParams(
        collective_id=collective, has_side_effects=True, vmem_limit_bytes=LIMIT
    )


def meet(devices):
    barrier = pltpu.get_barrier_semaphore()
    for device in devices:
        pl.semaphore_signal(barrier, inc=1, device_id=device, device_id_type=MESH)
    pl.semaphore_wait(barrier, len(devices))


GATHER_AT = (0, 1, 3, 8)
REDUCE_AT = (8, 11, 13)


class Torus:
    def __init__(self):
        place = lax.axis_index("learn")
        self.z, self.x, self.y = place // 16, lax.rem(place // 4, 4), lax.rem(place, 4)

    def device(self, dz, dx, dy):
        z = lax.rem(self.z + dz, 2)
        x = lax.rem(self.x + dx + 4, 4)
        y = lax.rem(self.y + dy + 4, 4)
        return {"learn": z * 16 + x * 4 + y}

    def first(self, half, d):
        return self.device(0, d, 0) if half == 0 else self.device(0, 0, d)

    def second(self, half, d):
        return self.device(0, 0, d) if half == 0 else self.device(0, d, 0)

    def other(self):
        return self.device(1, 0, 0)

    def neighbours(self):
        return [
            self.device(0, 1, 0),
            self.device(0, -1, 0),
            self.device(0, 0, 1),
            self.device(0, 0, -1),
            self.other(),
        ]

    def rows(self, half, plane, dp, dq, part=None):
        dx, dy = (dp, dq) if half == 0 else (dq, dp)
        block = self.device(plane, dx, dy)["learn"]
        start = block * 64 + 32 * half
        if part is None:
            return pl.ds(pl.multiple_of(start, 32), 32)
        return pl.ds(pl.multiple_of(start + 16 * part, 16), 16)


def gather_keys():
    keys = []
    for half in (0, 1):
        keys += [("p", half, d) for d in (1, -1)]
        keys += [("pf", half, d) for d in (1, -1)]
        keys += [("z", half, dp) for dp in OFFSETS]
        for plane in (0, 1):
            for dp in OFFSETS:
                keys += [("q", half, plane, dp, d) for d in (1, -1)]
                keys += [("qf", half, plane, dp, d) for d in (1, -1)]
    return {key: index for index, key in enumerate(keys)}


KEYS = gather_keys()


def gather_blocks(held, send_sems, recv_sems, work):
    torus = Torus()
    started = []

    def move(key, rows, device):
        index = KEYS[key]
        return pltpu.make_async_remote_copy(
            src_ref=held.at[rows],
            dst_ref=held.at[rows],
            send_sem=send_sems.at[index],
            recv_sem=recv_sems.at[index],
            device_id=device,
            device_id_type=MESH,
        )

    def send(key, rows, device):
        copy = move(key, rows, device)
        copy.start()
        started.append(copy)

    def arrive(key, rows):
        move(key, rows, torus.other()).wait_recv()

    left = list(range(STEPS))

    def spread(half, plane, dp):
        for d in (1, -1):
            send(("q", half, plane, dp, d), torus.rows(half, plane, dp, 0), torus.second(half, d))

    def pass_on(half, plane, dp):
        for d in (1, -1):
            part = 0 if d == 1 else 1
            arrive(("q", half, plane, dp, d), torus.rows(half, plane, dp, -d))
            send(
                ("qf", half, plane, dp, d),
                torus.rows(half, plane, dp, -d, part),
                torus.second(half, d),
            )

    def cross(half, dp):
        send(("z", half, dp), torus.rows(half, 0, dp, 0), torus.other())

    def crossed(half, dp):
        for t in left[:2]:
            work(t)
        del left[:2]
        arrive(("z", half, dp), torus.rows(half, 1, dp, 0))
        spread(half, 1, dp)

    for half in (0, 1):
        for d in (1, -1):
            send(("p", half, d), torus.rows(half, 0, 0, 0), torus.first(half, d))
    for half in (0, 1):
        cross(half, 0)
        spread(half, 0, 0)
    for half in (0, 1):
        for d in (1, -1):
            part = 0 if d == 1 else 1
            arrive(("p", half, d), torus.rows(half, 0, -d, 0))
            send(("pf", half, d), torus.rows(half, 0, -d, 0, part), torus.first(half, d))
            cross(half, -d)
    for half in (0, 1):
        for d in (1, -1):
            spread(half, 0, -d)
    for half in (0, 1):
        crossed(half, 0)
        for d in (1, -1):
            part = 0 if d == 1 else 1
            arrive(("pf", half, d), torus.rows(half, 0, -2 * d, 0, part))
        cross(half, 2)
        spread(half, 0, 2)
    for half in (0, 1):
        pass_on(half, 0, 0)
    for half in (0, 1):
        for d in (1, -1):
            crossed(half, -d)
    for half in (0, 1):
        for d in (1, -1):
            pass_on(half, 0, -d)
    for half in (0, 1):
        crossed(half, 2)
    for half in (0, 1):
        pass_on(half, 1, 0)
    for half in (0, 1):
        pass_on(half, 0, 2)
    for half in (0, 1):
        for d in (1, -1):
            pass_on(half, 1, -d)
    for half in (0, 1):
        pass_on(half, 1, 2)
    for half in (0, 1):
        for plane in (0, 1):
            for dp in OFFSETS:
                for d in (1, -1):
                    part = 0 if d == 1 else 1
                    arrive(
                        ("qf", half, plane, dp, d), torus.rows(half, plane, dp, -2 * d, part)
                    )
    for copy in started:
        copy.wait_send()


def exchange_values(torus, assigned_ref, estimates, moved, send_sems, recv_sems):
    lane = lax.broadcasted_iota(jnp.int32, (STEPS, 128), 1)
    phases = (
        (0, torus.y, 2, 4, lambda d: torus.device(0, 0, d)),
        (4, torus.x, 8, 4, lambda d: torus.device(0, d, 0)),
        (8, torus.z, 32, 2, lambda d: torus.device(d, 0, 0)),
    )

    def copies(phase):
        first, _, _, size, device = phases[phase]
        return [
            pltpu.make_async_remote_copy(
                src_ref=moved.at[first],
                dst_ref=moved.at[first + d],
                send_sem=send_sems.at[first + d],
                recv_sem=recv_sems.at[first + d],
                device_id=device(d),
                device_id_type=MESH,
            )
            for d in range(1, size)
        ]

    def start(phase):
        for copy in copies(phase):
            copy.start()

    def finish(phase):
        first, place, stride, size, _ = phases[phase]
        for copy in copies(phase):
            copy.wait()
        field = lax.rem(lane // stride, size)
        result = jnp.zeros((STEPS, 128), F32)
        for d in range(size):
            source = lax.rem(place - d + size, size)
            shift = lax.rem((source - place) * stride + 128, 128)
            turned = pltpu.roll(moved[first + d], shift, 1)
            result = jnp.where(field == source, turned, result)
        return result

    def run(stage):
        if stage == 0:
            row = jnp.broadcast_to(assigned_ref[...].astype(F32), (BATCH, BATCH))
            row = jnp.concatenate([row, jnp.full((BATCH, 128 - BATCH), -1.0, F32)], axis=1)
            tall = jnp.concatenate([row, row], axis=0).T
            column = tall[0:BATCH, :]
            across = lax.broadcasted_iota(jnp.int32, (BATCH, 128), 1)
            down = lax.broadcasted_iota(jnp.int32, (BATCH, 128), 0)
            earlier = jnp.where((row == column) & (across < down), 1.0, 0.0)
            target = 2.0 * column + jnp.sum(earlier, axis=1, keepdims=True)
            spread = jnp.where(across.astype(F32) == target, 1.0, 0.0)
            moved[0] = jnp.dot(
                estimates,
                spread,
                preferred_element_type=F32,
                precision=lax.Precision.HIGHEST,
            )
            start(0)
        elif stage < 3:
            moved[phases[stage][0]] = finish(stage - 1)
            start(stage)
        else:
            moved[6] = finish(2)

    return run


def reduce_blocks(
    torus,
    hidden,
    grads,
    exchange,
    out_ref,
    own,
    arena,
    send_sems,
    recv_sems,
):
    started = []
    where = {}
    counts = {16: 0, 32: 0}
    for key in KEYS:
        size = 16 if key[0] in ("qf", "pf") else 32
        where[key] = counts[size]
        counts[size] += 1

    def landing(key):
        size = 16 if key[0] in ("qf", "pf") else 32
        base = 0 if size == 32 else counts[32] * 32
        return arena.at[pl.ds(base + where[key] * size, size)]

    def send(key, source, device):
        index = KEYS[key]
        copy = pltpu.make_async_remote_copy(
            src_ref=source,
            dst_ref=landing(key),
            send_sem=send_sems.at[index],
            recv_sem=recv_sems.at[index],
            device_id=device,
            device_id_type=MESH,
        )
        copy.start()
        started.append(copy)

    def arrived(key):
        index = KEYS[key]
        ref = landing(key)
        pltpu.make_async_remote_copy(
            src_ref=ref,
            dst_ref=ref,
            send_sem=send_sems.at[index],
            recv_sem=recv_sems.at[index],
            device_id=torus.other(),
            device_id_type=MESH,
        ).wait_recv()
        return ref[...].astype(F32)

    def multiply(plane, dx):
        first = torus.device(plane, dx, 0)["learn"] // 4
        spot = pl.ds(pl.multiple_of(first * 256, 256), 256)
        kept = hidden[0:STEPS, :, spot].reshape(STEPS * BATCH, 256)
        for k in range(4):
            part = pl.ds(k * QUARTER, QUARTER)
            own[spot, part] = lax.dot_general(
                kept,
                grads[:, :, part].reshape(STEPS * BATCH, QUARTER),
                (((0,), (0,)), ((), ())),
                preferred_element_type=F32,
            ).astype(BF)

    def far(half, plane, dp):
        for d in (1, -1):
            part = 0 if d == 1 else 1
            send(
                ("qf", half, plane, dp, d),
                own.at[torus.rows(half, plane, dp, -2 * d, part)],
                torus.second(half, -d),
            )

    def near(half, plane, dp, d):
        part = 0 if d == 1 else 1
        extra = arrived(("qf", half, plane, dp, d))
        rows = torus.rows(half, plane, dp, -d, part)
        own[rows, :] = (own[rows, :].astype(F32) + extra).astype(BF)
        block = own.at[torus.rows(half, plane, dp, -d)]
        send(("q", half, plane, dp, d), block, torus.second(half, -d))

    def line(half, plane, dp):
        total = own[torus.rows(half, plane, dp, 0), :].astype(F32)
        for d in (1, -1):
            total = total + arrived(("q", half, plane, dp, d))
        return total

    def cross(half, dp):
        rows = torus.rows(half, 1, dp, 0)
        own[rows, :] = line(half, 1, dp).astype(BF)
        send(("z", half, dp), own.at[rows], torus.other())

    def plane_sum(half, dp):
        return line(half, 0, dp) + arrived(("z", half, dp))

    def product(plane, dp):
        multiply(plane, dp)
        if dp == 2:
            for other in OFFSETS:
                far(1, plane, other)
        far(0, plane, dp)

    for dp in OFFSETS:
        product(1, dp)
        if dp == 2:
            exchange(0)
    for dp in OFFSETS:
        for half in (0, 1):
            for d in (1, -1):
                near(half, 1, dp, d)
    exchange(1)
    for dp in OFFSETS:
        product(0, dp)
        for half in (0, 1):
            cross(half, dp)
    exchange(2)
    for dp in OFFSETS:
        for half in (0, 1):
            for d in (1, -1):
                near(half, 0, dp, d)
    exchange(3)
    for half in (0, 1):
        own[torus.rows(half, 0, 2, 0), :] = plane_sum(half, 2).astype(BF)
        for d in (1, -1):
            part = 0 if d == 1 else 1
            block = own.at[torus.rows(half, 0, 2, 0, part)]
            send(("pf", half, d), block, torus.first(half, -d))
    for half in (0, 1):
        for d in (1, -1):
            part = 0 if d == 1 else 1
            rows = torus.rows(half, 0, -d, 0)
            own[rows, :] = plane_sum(half, -d).astype(BF)
            extra = arrived(("pf", half, d))
            some = torus.rows(half, 0, -d, 0, part)
            own[some, :] = (own[some, :].astype(F32) + extra).astype(BF)
            send(("p", half, d), own.at[rows], torus.first(half, -d))
    for half in (0, 1):
        total = plane_sum(half, 0)
        for d in (1, -1):
            total = total + arrived(("p", half, d))
        rows = pl.ds(32 * half, 32)
        for k in range(4):
            out_ref[rows, k, :] = total[:, k * QUARTER : (k + 1) * QUARTER]
    for copy in started:
        copy.wait_send()


class Heads:
    def __init__(self, torus, held, partial, along_x, along_y, along_z, sems):
        self.torus, self.held, self.partial = torus, held, partial
        self.along = (along_z, along_y, along_x)
        self.sems = sems

    def group(self, plane, dx):
        first = self.torus.device(plane, dx, 0)["learn"] // 4
        return pl.ds(pl.multiple_of(first * 256, 256), 256)

    def block(self, plane, dx, dy):
        return pl.ds(pl.multiple_of(self.torus.device(plane, dx, dy)["learn"] * 64, 64), 64)

    def copy(self, way, index, source, target, device):
        return pltpu.make_async_remote_copy(
            src_ref=source,
            dst_ref=target,
            send_sem=self.sems[2 * way].at[index],
            recv_sem=self.sems[2 * way + 1].at[index],
            device_id=device,
            device_id_type=MESH,
        )

    def gather_copies(self, stage, arrivals):
        held, torus, result = self.held, self.torus, []
        if stage == 0:
            rows = self.block(1 if arrivals else 0, 0, 0)
            result.append(self.copy(0, 0, held.at[rows], held.at[rows], torus.other()))
        for d in (1, 2, 3):
            for plane in (0, 1):
                index = 1 + (stage - 1) * 6 + (d - 1) * 2 + plane
                shift = 4 - d if arrivals else 0
                if stage == 1:
                    rows = self.block(plane, 0, shift)
                    device = torus.device(0, 0, d)
                elif stage == 2:
                    rows = self.group(plane, shift)
                    device = torus.device(0, d, 0)
                else:
                    continue
                result.append(self.copy(0, index, held.at[rows], held.at[rows], device))
        return result

    def gather(self, stage):
        if stage > 0:
            for copy in self.gather_copies(stage - 1, True):
                copy.wait_recv()
            for copy in self.gather_copies(stage - 1, False):
                copy.wait_send()
        if stage < 3:
            for copy in self.gather_copies(stage, False):
                copy.start()

    def reduce_copies(self, stage):
        partial, torus, result = self.partial, self.torus, []
        along_z, along_y, along_x = self.along
        if stage == 2:
            rows = self.block(1, 0, 0)
            result.append(self.copy(1, 12, partial.at[rows], along_z, torus.other()))
        for d in (1, 2, 3):
            for plane in (0, 1):
                slot = (d - 1) * 2 + plane
                if stage == 0:
                    rows, target = self.group(plane, d), along_x.at[slot]
                    device = torus.device(0, d, 0)
                elif stage == 1:
                    rows, target = self.block(plane, 0, d), along_y.at[slot]
                    device = torus.device(0, 0, d)
                else:
                    continue
                result.append(self.copy(1, stage * 6 + slot, partial.at[rows], target, device))
        return result

    def reduce(self, stage):
        along_z, along_y, along_x = self.along
        if stage > 0:
            for copy in self.reduce_copies(stage - 1):
                copy.wait()
        if stage in (1, 2):
            for plane in (0, 1):
                rows = self.group(plane, 0) if stage == 1 else self.block(plane, 0, 0)
                arrived = along_x if stage == 1 else along_y
                total = self.partial[rows, :].astype(F32)
                for d in (1, 2, 3):
                    total = total + arrived[(d - 1) * 2 + plane].astype(F32)
                self.partial[rows, :] = total.astype(BF)
        if stage < 3:
            for copy in self.reduce_copies(stage):
                copy.start()
            return None
        return self.partial[self.block(0, 0, 0), :].astype(F32) + along_z[...].astype(F32)


def actor_peers():
    me = lax.axis_index("actor")
    core = me + 1 - 2 * lax.rem(me, 2)
    across = lax.rem(me + 2, 4)
    return me, (core, across, 3 - me)


def columns(quarter, start=0, size=QUARTER):
    return pl.ds(pl.multiple_of(quarter * QUARTER + start, 128), size)


def sigmoid(value):
    return 0.5 * jnp.tanh(0.5 * value) + 0.5


HALF = QUARTER // 2
DIRECT = 384
SUMMED = QUARTER - DIRECT
WIDTHS = (DIRECT, DIRECT, SUMMED, SUMMED)


def train_kernel(
    block_ref,
    head_ref,
    value_ref,
    gate_ref,
    state_ref,
    counts_ref,
    start_ref,
    advantage_ref,
    return_ref,
    logprob_ref,
    action_ref,
    assigned_ref,
    out_ref,
    policy_ref,
    value_out_ref,
    values_ref,
    hidden,
    grads,
    scores,
    values,
    heads_held,
    heads_partial,
    heads_x,
    heads_y,
    heads_z,
    moved,
    held,
    arena,
    factors,
    head_grad,
    gates,
    aux,
    preact,
    cell,
    carry_hidden,
    carry_cell,
    sent,
    got,
    sent_core,
    got_core,
    gather_send,
    gather_recv,
    step_send,
    step_recv,
    back_send,
    back_recv,
    reduce_send,
    reduce_recv,
    value_send,
    value_recv,
    ready,
    *heads_sems,
):
    torus = Torus()
    me, peers = actor_peers()
    core, across, diagonal = peers
    far_devices = [torus.device(0, 2, 0), torus.device(0, 0, 2)]
    meet(torus.neighbours() + far_devices + [{"actor": peer} for peer in peers])
    place = lax.axis_index("learn")
    mine = pl.ds(pl.multiple_of(place * 64, 64), 64)
    held[mine, :] = block_ref[...].reshape(64, UNITS)
    heads_held[mine, 0:CHOICES] = head_ref[...]
    line = jnp.concatenate([value_ref[...].astype(F32), jnp.zeros((1, 64), F32)], axis=1)
    heads_held[mine, CHOICES:PAIR] = jnp.broadcast_to(line, (128, 128)).T[0:64].astype(BF)
    heads_moves = Heads(torus, heads_held, heads_partial, heads_x, heads_y, heads_z, heads_sems)

    def pieces(t):
        return (
            (hidden.at[t, :, columns(me)], core),
            (hidden.at[t, :, columns(me, 0, HALF)], across),
            (hidden.at[t, :, columns(me, HALF, HALF)], across),
            (hidden.at[t, :, columns(me, HALF, HALF)], diagonal),
            (hidden.at[t, :, columns(across, 0, HALF)], core),
        )

    def landed(t):
        return (
            hidden.at[t, :, columns(core)],
            hidden.at[t, :, columns(across, 0, HALF)],
            hidden.at[t, :, columns(across, HALF, HALF)],
            hidden.at[t, :, columns(diagonal, HALF, HALF)],
            hidden.at[t, :, columns(diagonal, 0, HALF)],
        )

    def step_copy(t, index):
        part, peer = pieces(t)[index]
        return pltpu.make_async_remote_copy(
            src_ref=part,
            dst_ref=part,
            send_sem=step_send.at[t, index],
            recv_sem=step_recv.at[t, index],
            device_id={"actor": peer},
            device_id_type=MESH,
        )

    def arrive(t, index):
        part = landed(t)[index]
        pltpu.make_async_remote_copy(
            src_ref=part,
            dst_ref=part,
            send_sem=step_send.at[t, index],
            recv_sem=step_recv.at[t, index],
            device_id={"actor": core},
            device_id_type=MESH,
        ).wait_recv()

    def multiply(t, spot, first=False):
        part = hidden[t, :, spot]
        for k in range(4):
            wide = pl.ds(k * QUARTER, QUARTER)
            product = jnp.dot(part, held[spot, wide], preferred_element_type=F32)
            if first:
                preact[:, wide] = product
            else:
                preact[:, wide] += product

    def column(t, kind):
        lane = lax.broadcasted_iota(jnp.int32, (BATCH, 128), 1)
        return jnp.sum(jnp.where(lane == t + 16 * kind, aux[...], 0.0), axis=1, keepdims=True)

    def heads(index):
        t = index - 1
        result = jnp.dot(hidden[index], heads_held[...], preferred_element_type=F32)
        logits = result[:, 0:CHOICES]
        estimate = result[:, CHOICES : CHOICES + 1]
        share = aux[:, 80:81]
        lane = lax.broadcasted_iota(jnp.int32, (BATCH, CHOICES), 1)
        onehot = (lane.astype(F32) == column(t, 4)).astype(F32)
        shifted = logits - jnp.max(logits, axis=1, keepdims=True)
        powers = jnp.exp(shifted)
        total = jnp.sum(powers, axis=1, keepdims=True)
        chosen = jnp.sum(shifted * onehot, axis=1, keepdims=True) - jnp.log(total)
        ratio = jnp.exp(chosen - column(t, 3))
        slope = (0.5 * (ratio - 1.0) - ratio * column(t, 1)) * share
        grad_logits = slope * (onehot - powers / total)
        grad_estimate = (estimate - column(t, 2)) * share
        scores[index, :, 0:CHOICES] = grad_logits.astype(BF)
        scores[index, :, CHOICES : 2 * CHOICES] = jnp.where(lane == 0, grad_estimate, 0.0).astype(BF)
        live = (share > 0.0).astype(F32)
        values[...] = jnp.where(lane == t, estimate * live, values[...])
        head_grad[index] = lax.dot_general(
            scores[index],
            heads_held[columns(me), :],
            (((1,), (1,)), ((), ())),
            preferred_element_type=F32,
        )

    def cells(t, half):
        keep = column(t, 0)
        for chunk in range(2 * half, 2 * half + 2):
            spot = pl.ds(chunk * 128, 128)
            kept = keep * cell[:, spot]
            inputs = []
            for k in range(4):
                wide = pl.ds(k * QUARTER + chunk * 128, 128)
                inputs.append(gates[t, :, wide].astype(F32) + keep * preact[:, wide])
            inp = sigmoid(inputs[0])
            forget = sigmoid(inputs[1])
            cand = jnp.tanh(inputs[2])
            outg = sigmoid(inputs[3])
            new_cell = forget * kept + inp * cand
            squash = jnp.tanh(new_cell)
            cell[:, spot] = new_cell
            part = pl.ds(pl.multiple_of(me * QUARTER + chunk * 128, 128), 128)
            hidden[t + 1, :, part] = (outg * squash).astype(BF)
            kept_factors = (
                outg * (1.0 - squash * squash),
                keep * cand * inp * (1.0 - inp),
                kept * forget * (1.0 - forget),
                keep * inp * (1.0 - cand * cand),
                keep * squash * outg * (1.0 - outg),
                keep * forget,
            )
            for index, value in enumerate(kept_factors):
                factors[t, index, :, spot] = value.astype(BF)

    hidden[0, :, columns(me)] = state_ref[:, 0, :]
    for index in (1, 2, 3, 0):
        step_copy(0, index).start()
    cell[...] = state_ref[:, 1, :].astype(F32)
    values[...] = jnp.zeros_like(values)
    row = lax.broadcasted_iota(jnp.int32, (BATCH, 128), 0)
    live = jnp.where(row < counts_ref[place], 1.0 / STEPS, 0.0)
    table = jnp.concatenate(
        [
            1.0 - start_ref[...].astype(F32),
            advantage_ref[...].astype(F32),
            return_ref[...].astype(F32),
            logprob_ref[...].astype(F32),
            action_ref[...].astype(F32),
            jnp.zeros((48, BATCH), F32),
        ],
        axis=0,
    )
    table = jnp.concatenate([table, jnp.zeros((128, 128 - BATCH), F32)], axis=1)
    lane = lax.broadcasted_iota(jnp.int32, (BATCH, 128), 1)
    aux[...] = jnp.where(lane < 80, table.T[0:BATCH], live)

    def unpack(t):
        gates[t] = gate_ref[:, t].reshape(BATCH, UNITS)

    gather_blocks(held, gather_send, gather_recv, unpack)

    def step(t, carry):
        multiply(t, columns(me), True)
        stripe = pl.ds(pl.multiple_of(t * 128, 128), 128)
        arena[:, stripe] = held[stripe, :].T
        arrive(t, 0)
        multiply(t, columns(core))

        for stage, when in enumerate(GATHER_AT):

            @pl.when(t == when)
            def _(stage=stage):
                heads_moves.gather(stage)

        @pl.when(t > GATHER_AT[3])
        def _():
            heads(2 * (t - GATHER_AT[3]) - 1)
            heads(2 * (t - GATHER_AT[3]))

        arrive(t, 1)
        step_copy(t, 4).start()
        multiply(t, columns(across, 0, HALF))
        arrive(t, 2)
        multiply(t, columns(across, HALF, HALF))
        arrive(t, 3)
        multiply(t, columns(diagonal, HALF, HALF))
        arrive(t, 4)
        multiply(t, columns(diagonal, 0, HALF))
        cells(t, 0)
        step_copy(t + 1, 1).start()
        cells(t, 1)
        for index in (2, 3, 0):
            step_copy(t + 1, index).start()
        for index in range(5):
            step_copy(t, index).wait_send()
        return carry

    lax.fori_loop(0, STEPS, step, 0)
    heads(STEPS - 1)
    arrive(STEPS, 1)
    step_copy(STEPS, 4).start()
    for index in (0, 2, 3, 4):
        arrive(STEPS, index)
    for index in range(5):
        step_copy(STEPS, index).wait_send()
    heads(STEPS)

    carry_hidden[...] = jnp.zeros_like(carry_hidden)
    carry_cell[...] = jnp.zeros_like(carry_cell)

    targets = (diagonal, across, core, across, core)

    def back_copy(t, index):
        return pltpu.make_async_remote_copy(
            src_ref=sent_core.at[t] if index == 4 else sent.at[t, index, :, pl.ds(0, WIDTHS[index])],
            dst_ref=got_core.at[t] if index == 4 else got.at[t, index, :, pl.ds(0, WIDTHS[index])],
            send_sem=back_send.at[t, index],
            recv_sem=back_recv.at[t, index],
            device_id={"actor": targets[index]},
            device_id_type=MESH,
        )

    def cell_back(t):
        for chunk in range(QUARTER // 128):
            spot = pl.ds(chunk * 128, 128)
            factor = [factors[t, index, :, spot].astype(F32) for index in range(6)]
            total = head_grad[t + 1, :, spot] + carry_hidden[:, spot]
            dcell = carry_cell[:, spot] + total * factor[0]
            carry_cell[:, spot] = dcell * factor[5]
            parts = (dcell * factor[1], dcell * factor[2], dcell * factor[3], total * factor[4])
            for k, part in enumerate(parts):
                grads[t, :, pl.ds(k * QUARTER + chunk * 128, 128)] = part.astype(BF)

    def product(t, spot):
        return jnp.dot(grads[t], arena[:, spot], preferred_element_type=F32)

    def back(i, carry):
        t = STEPS - 1 - i
        cell_back(t)
        for index, quarter, start in ((2, diagonal, DIRECT), (0, diagonal, 0), (1, across, 0)):
            width = WIDTHS[index]
            sent[t, index, :, 0:width] = product(t, columns(quarter, start, width)).astype(BF)
            back_copy(t, index).start()
        part = product(t, columns(across, DIRECT, SUMMED))
        sent_core[t] = product(t, columns(core)).astype(BF)
        back_copy(t, 4).start()
        back_copy(t, 2).wait_recv()
        sent[t, 3, :, 0:SUMMED] = (part + got[t, 2, :, 0:SUMMED].astype(F32)).astype(BF)
        back_copy(t, 3).start()
        carry_hidden[...] = product(t, columns(me))

        @pl.when(i < 8)
        def _():
            spot = pl.ds(pl.multiple_of(i * 256, 256), 256)
            heads_partial[spot, :] = lax.dot_general(
                hidden[1 : STEPS + 1, :, spot].reshape(STEPS * BATCH, 256),
                scores[1 : STEPS + 1].reshape(STEPS * BATCH, PAIR),
                (((0,), (0,)), ((), ())),
                preferred_element_type=F32,
            ).astype(BF)

        for stage, when in enumerate(REDUCE_AT):

            @pl.when(i == when)
            def _(stage=stage):
                heads_moves.reduce(stage)

        back_copy(t, 4).wait_recv()
        carry_hidden[...] += got_core[t].astype(F32)
        for index in (0, 1):
            back_copy(t, index).wait_recv()
        carry_hidden[:, 0:DIRECT] += got[t, 0, :, 0:DIRECT].astype(F32) + got[t, 1, :, 0:DIRECT].astype(F32)
        back_copy(t, 3).wait_recv()
        carry_hidden[:, DIRECT:QUARTER] += got[t, 3, :, 0:SUMMED].astype(F32)
        for index in range(5):
            back_copy(t, index).wait_send()
        return carry

    lax.fori_loop(0, STEPS - 1, back, 0)
    for device in torus.neighbours():
        pl.semaphore_signal(ready, inc=1, device_id=device, device_id_type=MESH)
    cell_back(0)
    heads_total = heads_moves.reduce(3)
    policy_ref[...] = heads_total[:, 0:CHOICES]
    value_out_ref[...] = heads_total[:, CHOICES:PAIR].T[0:1, 0:64]
    pl.semaphore_wait(ready, 5)
    estimates = jnp.concatenate([values[...], values[...]], axis=0).T[0:STEPS, 0:BATCH]
    exchange = exchange_values(torus, assigned_ref, estimates, moved, value_send, value_recv)
    reduce_blocks(
        torus,
        hidden,
        grads,
        exchange,
        out_ref,
        held,
        arena,
        reduce_send,
        reduce_recv,
    )
    values_ref[...] = moved[6, :, 0:BATCH]


RESULTS = (
    jax.ShapeDtypeStruct((64, 4, QUARTER), F32),
    jax.ShapeDtypeStruct((64, CHOICES), F32),
    jax.ShapeDtypeStruct((1, 64), F32),
    jax.ShapeDtypeStruct((STEPS, BATCH), F32),
)


def hand_on_kernel(*refs):
    for source, target in zip(refs[:4], refs[4:]):
        target[...] = source[...]


def hand_on(*results):
    return pl.pallas_call(
        hand_on_kernel,
        out_shape=RESULTS,
        in_specs=[VMEM] * 4,
        out_specs=(VMEM,) * 4,
        name="hand_on",
    )(*results)


def train(*operands):
    specs = [VMEM] * len(operands)
    specs[5] = pl.BlockSpec(memory_space=pltpu.SMEM)
    return pl.pallas_call(
        train_kernel,
        out_shape=RESULTS,
        in_specs=specs,
        out_specs=(VMEM,) * 4,
        scratch_shapes=[
            pltpu.VMEM((STEPS + 1, BATCH, UNITS), BF),
            pltpu.VMEM((STEPS, BATCH, UNITS), BF),
            pltpu.VMEM((STEPS + 1, BATCH, 2 * CHOICES), BF),
            pltpu.VMEM((BATCH, 128), F32),
            pltpu.VMEM((UNITS, PAIR), BF),
            pltpu.VMEM((UNITS, PAIR), BF),
            pltpu.VMEM((6, 256, PAIR), BF),
            pltpu.VMEM((6, 64, PAIR), BF),
            pltpu.VMEM((64, PAIR), BF),
            pltpu.VMEM((10, STEPS, 128), F32),
            pltpu.VMEM((UNITS, UNITS), BF),
            pltpu.VMEM((UNITS, UNITS), BF),
            pltpu.VMEM((STEPS, 6, BATCH, QUARTER), BF),
            pltpu.VMEM((STEPS + 1, BATCH, QUARTER), F32),
            pltpu.VMEM((STEPS, BATCH, UNITS), BF),
            pltpu.VMEM((BATCH, 128), F32),
            pltpu.VMEM((BATCH, UNITS), F32),
            pltpu.VMEM((BATCH, QUARTER), F32),
            pltpu.VMEM((BATCH, QUARTER), F32),
            pltpu.VMEM((BATCH, QUARTER), F32),
            pltpu.VMEM((STEPS, 4, BATCH, max(DIRECT, SUMMED)), BF),
            pltpu.VMEM((STEPS, 4, BATCH, max(DIRECT, SUMMED)), BF),
            pltpu.VMEM((STEPS, BATCH, QUARTER), BF),
            pltpu.VMEM((STEPS, BATCH, QUARTER), BF),
            pltpu.SemaphoreType.DMA((len(KEYS),)),
            pltpu.SemaphoreType.DMA((len(KEYS),)),
            pltpu.SemaphoreType.DMA((STEPS + 1, 5)),
            pltpu.SemaphoreType.DMA((STEPS + 1, 5)),
            pltpu.SemaphoreType.DMA((STEPS, 5)),
            pltpu.SemaphoreType.DMA((STEPS, 5)),
            pltpu.SemaphoreType.DMA((len(KEYS),)),
            pltpu.SemaphoreType.DMA((len(KEYS),)),
            pltpu.SemaphoreType.DMA((10,)),
            pltpu.SemaphoreType.DMA((10,)),
            pltpu.SemaphoreType.REGULAR,
            pltpu.SemaphoreType.DMA((13,)),
            pltpu.SemaphoreType.DMA((13,)),
            pltpu.SemaphoreType.DMA((13,)),
            pltpu.SemaphoreType.DMA((13,)),
        ],
        compiler_params=params(1),
        name="train",
    )(*operands)


def shards(
    rec_weight,
    head_weight,
    value_head,
    gate_inputs,
    start_state,
    advantages,
    returns,
    old_logprob,
    taken_action,
    episode_start,
    segment_counts,
    assignment,
):
    results = train(
        rec_weight,
        head_weight,
        value_head[None],
        gate_inputs[0],
        start_state[0],
        segment_counts,
        episode_start[0].T,
        advantages[0].T,
        returns[0].T,
        old_logprob[0].T,
        taken_action[0].T,
        assignment,
    )
    rec_share, policy_share, value_share, values = hand_on(*results)
    return (rec_share, policy_share, value_share[0], values.T[None])


def solution(mesh):
    placed = (
        P("learn", None, "actor"),
        P("learn", None),
        P("learn"),
        P("learn", None, None, None, "actor"),
        P("learn", None, None, "actor"),
        P("learn", None, None),
        P("learn", None, None),
        P("learn", None, None),
        P("learn", None, None),
        P("learn", None, None),
        P(),
        P("learn", None),
    )
    return jax.shard_map(
        shards,
        mesh=mesh,
        in_specs=placed,
        out_specs=(P("learn", None, "actor"), P("learn", None), P("learn"), P("learn", None, None)),
        check_vma=False,
    )
```

```python
import jax
import jax.numpy as jnp
from jax import lax
from jax.experimental import pallas as pl
from jax.experimental.pallas import tpu as pltpu
from jax.sharding import PartitionSpec as P

MESH = pl.DeviceIdType.MESH
BF = jnp.bfloat16
F32 = jnp.float32
UNITS = 2048
QUARTER = 512
BATCH = 64
STEPS = 16
CHOICES = 128
PAIR = 2 * CHOICES
VMEM = pl.BlockSpec(memory_space=pltpu.VMEM)
LIMIT = 60 * 2**20
OFFSETS = (2, -1, 1, 0)


def params(collective):
    return pltpu.CompilerParams(
        collective_id=collective, has_side_effects=True, vmem_limit_bytes=LIMIT
    )


def meet(devices):
    barrier = pltpu.get_barrier_semaphore()
    for device in devices:
        pl.semaphore_signal(barrier, inc=1, device_id=device, device_id_type=MESH)
    pl.semaphore_wait(barrier, len(devices))


GATHER_AT = (0, 1, 3, 8)
REDUCE_AT = (8, 11, 13)


class Torus:
    def __init__(self):
        place = lax.axis_index("learn")
        self.z, self.x, self.y = place // 16, lax.rem(place // 4, 4), lax.rem(place, 4)

    def device(self, dz, dx, dy):
        z = lax.rem(self.z + dz, 2)
        x = lax.rem(self.x + dx + 4, 4)
        y = lax.rem(self.y + dy + 4, 4)
        return {"learn": z * 16 + x * 4 + y}

    def first(self, half, d):
        return self.device(0, d, 0) if half == 0 else self.device(0, 0, d)

    def second(self, half, d):
        return self.device(0, 0, d) if half == 0 else self.device(0, d, 0)

    def other(self):
        return self.device(1, 0, 0)

    def neighbours(self):
        return [
            self.device(0, 1, 0),
            self.device(0, -1, 0),
            self.device(0, 0, 1),
            self.device(0, 0, -1),
            self.other(),
        ]

    def rows(self, half, plane, dp, dq, part=None):
        dx, dy = (dp, dq) if half == 0 else (dq, dp)
        block = self.device(plane, dx, dy)["learn"]
        start = block * 64 + 32 * half
        if part is None:
            return pl.ds(pl.multiple_of(start, 32), 32)
        return pl.ds(pl.multiple_of(start + 16 * part, 16), 16)


def gather_keys():
    keys = []
    for half in (0, 1):
        keys += [("p", half, d) for d in (1, -1)]
        keys += [("pf", half, d) for d in (1, -1)]
        keys += [("z", half, dp) for dp in OFFSETS]
        for plane in (0, 1):
            for dp in OFFSETS:
                keys += [("q", half, plane, dp, d) for d in (1, -1)]
                keys += [("qf", half, plane, dp, d) for d in (1, -1)]
    return {key: index for index, key in enumerate(keys)}


KEYS = gather_keys()


def gather_blocks(held, send_sems, recv_sems, work):
    torus = Torus()
    started = []

    def move(key, rows, device):
        index = KEYS[key]
        return pltpu.make_async_remote_copy(
            src_ref=held.at[rows],
            dst_ref=held.at[rows],
            send_sem=send_sems.at[index],
            recv_sem=recv_sems.at[index],
            device_id=device,
            device_id_type=MESH,
        )

    def send(key, rows, device):
        copy = move(key, rows, device)
        copy.start()
        started.append(copy)

    def arrive(key, rows):
        move(key, rows, torus.other()).wait_recv()

    left = list(range(STEPS))

    def spread(half, plane, dp):
        for d in (1, -1):
            send(("q", half, plane, dp, d), torus.rows(half, plane, dp, 0), torus.second(half, d))

    def pass_on(half, plane, dp):
        for d in (1, -1):
            part = 0 if d == 1 else 1
            arrive(("q", half, plane, dp, d), torus.rows(half, plane, dp, -d))
            send(
                ("qf", half, plane, dp, d),
                torus.rows(half, plane, dp, -d, part),
                torus.second(half, d),
            )

    def cross(half, dp):
        send(("z", half, dp), torus.rows(half, 0, dp, 0), torus.other())

    def crossed(half, dp):
        for t in left[:2]:
            work(t)
        del left[:2]
        arrive(("z", half, dp), torus.rows(half, 1, dp, 0))
        spread(half, 1, dp)

    for half in (0, 1):
        for d in (1, -1):
            send(("p", half, d), torus.rows(half, 0, 0, 0), torus.first(half, d))
    for half in (0, 1):
        cross(half, 0)
        spread(half, 0, 0)
    for half in (0, 1):
        for d in (1, -1):
            part = 0 if d == 1 else 1
            arrive(("p", half, d), torus.rows(half, 0, -d, 0))
            send(("pf", half, d), torus.rows(half, 0, -d, 0, part), torus.first(half, d))
            cross(half, -d)
    for half in (0, 1):
        for d in (1, -1):
            spread(half, 0, -d)
    for half in (0, 1):
        crossed(half, 0)
        for d in (1, -1):
            part = 0 if d == 1 else 1
            arrive(("pf", half, d), torus.rows(half, 0, -2 * d, 0, part))
        cross(half, 2)
        spread(half, 0, 2)
    for half in (0, 1):
        pass_on(half, 0, 0)
    for half in (0, 1):
        for d in (1, -1):
            crossed(half, -d)
    for half in (0, 1):
        for d in (1, -1):
            pass_on(half, 0, -d)
    for half in (0, 1):
        crossed(half, 2)
    for half in (0, 1):
        pass_on(half, 1, 0)
    for half in (0, 1):
        pass_on(half, 0, 2)
    for half in (0, 1):
        for d in (1, -1):
            pass_on(half, 1, -d)
    for half in (0, 1):
        pass_on(half, 1, 2)
    for half in (0, 1):
        for plane in (0, 1):
            for dp in OFFSETS:
                for d in (1, -1):
                    part = 0 if d == 1 else 1
                    arrive(
                        ("qf", half, plane, dp, d), torus.rows(half, plane, dp, -2 * d, part)
                    )
    for copy in started:
        copy.wait_send()


def exchange_values(torus, assigned_ref, estimates, moved, send_sems, recv_sems):
    lane = lax.broadcasted_iota(jnp.int32, (STEPS, 128), 1)
    phases = (
        (0, torus.y, 2, 4, lambda d: torus.device(0, 0, d)),
        (4, torus.x, 8, 4, lambda d: torus.device(0, d, 0)),
        (8, torus.z, 32, 2, lambda d: torus.device(d, 0, 0)),
    )

    def copies(phase):
        first, _, _, size, device = phases[phase]
        return [
            pltpu.make_async_remote_copy(
                src_ref=moved.at[first],
                dst_ref=moved.at[first + d],
                send_sem=send_sems.at[first + d],
                recv_sem=recv_sems.at[first + d],
                device_id=device(d),
                device_id_type=MESH,
            )
            for d in range(1, size)
        ]

    def start(phase):
        for copy in copies(phase):
            copy.start()

    def finish(phase):
        first, place, stride, size, _ = phases[phase]
        for copy in copies(phase):
            copy.wait()
        field = lax.rem(lane // stride, size)
        result = jnp.zeros((STEPS, 128), F32)
        for d in range(size):
            source = lax.rem(place - d + size, size)
            shift = lax.rem((source - place) * stride + 128, 128)
            turned = pltpu.roll(moved[first + d], shift, 1)
            result = jnp.where(field == source, turned, result)
        return result

    def run(stage):
        if stage == 0:
            row = jnp.broadcast_to(assigned_ref[...].astype(F32), (BATCH, BATCH))
            row = jnp.concatenate([row, jnp.full((BATCH, 128 - BATCH), -1.0, F32)], axis=1)
            tall = jnp.concatenate([row, row], axis=0).T
            column = tall[0:BATCH, :]
            across = lax.broadcasted_iota(jnp.int32, (BATCH, 128), 1)
            down = lax.broadcasted_iota(jnp.int32, (BATCH, 128), 0)
            earlier = jnp.where((row == column) & (across < down), 1.0, 0.0)
            target = 2.0 * column + jnp.sum(earlier, axis=1, keepdims=True)
            spread = jnp.where(across.astype(F32) == target, 1.0, 0.0)
            moved[0] = jnp.dot(
                estimates,
                spread,
                preferred_element_type=F32,
                precision=lax.Precision.HIGHEST,
            )
            start(0)
        elif stage < 3:
            moved[phases[stage][0]] = finish(stage - 1)
            start(stage)
        else:
            moved[6] = finish(2)

    return run


def reduce_blocks(
    torus,
    hidden,
    grads,
    exchange,
    out_ref,
    own,
    arena,
    send_sems,
    recv_sems,
):
    started = []
    where = {}
    counts = {16: 0, 32: 0}
    for key in KEYS:
        size = 16 if key[0] in ("qf", "pf") else 32
        where[key] = counts[size]
        counts[size] += 1

    def landing(key):
        size = 16 if key[0] in ("qf", "pf") else 32
        base = 0 if size == 32 else counts[32] * 32
        return arena.at[pl.ds(base + where[key] * size, size)]

    def send(key, source, device):
        index = KEYS[key]
        copy = pltpu.make_async_remote_copy(
            src_ref=source,
            dst_ref=landing(key),
            send_sem=send_sems.at[index],
            recv_sem=recv_sems.at[index],
            device_id=device,
            device_id_type=MESH,
        )
        copy.start()
        started.append(copy)

    def arrived(key):
        index = KEYS[key]
        ref = landing(key)
        pltpu.make_async_remote_copy(
            src_ref=ref,
            dst_ref=ref,
            send_sem=send_sems.at[index],
            recv_sem=recv_sems.at[index],
            device_id=torus.other(),
            device_id_type=MESH,
        ).wait_recv()
        return ref[...].astype(F32)

    def multiply(plane, dx):
        first = torus.device(plane, dx, 0)["learn"] // 4
        spot = pl.ds(pl.multiple_of(first * 256, 256), 256)
        kept = hidden[0:STEPS, :, spot].reshape(STEPS * BATCH, 256)
        for k in range(4):
            part = pl.ds(k * QUARTER, QUARTER)
            own[spot, part] = lax.dot_general(
                kept,
                grads[:, :, part].reshape(STEPS * BATCH, QUARTER),
                (((0,), (0,)), ((), ())),
                preferred_element_type=F32,
            ).astype(BF)

    def far(half, plane, dp):
        for d in (1, -1):
            part = 0 if d == 1 else 1
            send(
                ("qf", half, plane, dp, d),
                own.at[torus.rows(half, plane, dp, -2 * d, part)],
                torus.second(half, -d),
            )

    def near(half, plane, dp, d):
        part = 0 if d == 1 else 1
        extra = arrived(("qf", half, plane, dp, d))
        rows = torus.rows(half, plane, dp, -d, part)
        own[rows, :] = (own[rows, :].astype(F32) + extra).astype(BF)
        block = own.at[torus.rows(half, plane, dp, -d)]
        send(("q", half, plane, dp, d), block, torus.second(half, -d))

    def line(half, plane, dp):
        total = own[torus.rows(half, plane, dp, 0), :].astype(F32)
        for d in (1, -1):
            total = total + arrived(("q", half, plane, dp, d))
        return total

    def cross(half, dp):
        rows = torus.rows(half, 1, dp, 0)
        own[rows, :] = line(half, 1, dp).astype(BF)
        send(("z", half, dp), own.at[rows], torus.other())

    def plane_sum(half, dp):
        return line(half, 0, dp) + arrived(("z", half, dp))

    def product(plane, dp):
        multiply(plane, dp)
        if dp == 2:
            for other in OFFSETS:
                far(1, plane, other)
        far(0, plane, dp)

    for dp in OFFSETS:
        product(1, dp)
        if dp == 2:
            exchange(0)
    for dp in OFFSETS:
        for half in (0, 1):
            for d in (1, -1):
                near(half, 1, dp, d)
    exchange(1)
    for dp in OFFSETS:
        product(0, dp)
        for half in (0, 1):
            cross(half, dp)
    exchange(2)
    for dp in OFFSETS:
        for half in (0, 1):
            for d in (1, -1):
                near(half, 0, dp, d)
    exchange(3)
    for half in (0, 1):
        own[torus.rows(half, 0, 2, 0), :] = plane_sum(half, 2).astype(BF)
        for d in (1, -1):
            part = 0 if d == 1 else 1
            block = own.at[torus.rows(half, 0, 2, 0, part)]
            send(("pf", half, d), block, torus.first(half, -d))
    for half in (0, 1):
        for d in (1, -1):
            part = 0 if d == 1 else 1
            rows = torus.rows(half, 0, -d, 0)
            own[rows, :] = plane_sum(half, -d).astype(BF)
            extra = arrived(("pf", half, d))
            some = torus.rows(half, 0, -d, 0, part)
            own[some, :] = (own[some, :].astype(F32) + extra).astype(BF)
            send(("p", half, d), own.at[rows], torus.first(half, -d))
    for half in (0, 1):
        total = plane_sum(half, 0)
        for d in (1, -1):
            total = total + arrived(("p", half, d))
        rows = pl.ds(32 * half, 32)
        for k in range(4):
            out_ref[rows, k, :] = total[:, k * QUARTER : (k + 1) * QUARTER]
    for copy in started:
        copy.wait_send()


class Heads:
    def __init__(self, torus, held, partial, along_x, along_y, along_z, sems):
        self.torus, self.held, self.partial = torus, held, partial
        self.along = (along_z, along_y, along_x)
        self.sems = sems

    def group(self, plane, dx):
        first = self.torus.device(plane, dx, 0)["learn"] // 4
        return pl.ds(pl.multiple_of(first * 256, 256), 256)

    def block(self, plane, dx, dy):
        return pl.ds(pl.multiple_of(self.torus.device(plane, dx, dy)["learn"] * 64, 64), 64)

    def copy(self, way, index, source, target, device):
        return pltpu.make_async_remote_copy(
            src_ref=source,
            dst_ref=target,
            send_sem=self.sems[2 * way].at[index],
            recv_sem=self.sems[2 * way + 1].at[index],
            device_id=device,
            device_id_type=MESH,
        )

    def gather_copies(self, stage, arrivals):
        held, torus, result = self.held, self.torus, []
        if stage == 0:
            rows = self.block(1 if arrivals else 0, 0, 0)
            result.append(self.copy(0, 0, held.at[rows], held.at[rows], torus.other()))
        for d in (1, 2, 3):
            for plane in (0, 1):
                index = 1 + (stage - 1) * 6 + (d - 1) * 2 + plane
                shift = 4 - d if arrivals else 0
                if stage == 1:
                    rows = self.block(plane, 0, shift)
                    device = torus.device(0, 0, d)
                elif stage == 2:
                    rows = self.group(plane, shift)
                    device = torus.device(0, d, 0)
                else:
                    continue
                result.append(self.copy(0, index, held.at[rows], held.at[rows], device))
        return result

    def gather(self, stage):
        if stage > 0:
            for copy in self.gather_copies(stage - 1, True):
                copy.wait_recv()
            for copy in self.gather_copies(stage - 1, False):
                copy.wait_send()
        if stage < 3:
            for copy in self.gather_copies(stage, False):
                copy.start()

    def reduce_copies(self, stage):
        partial, torus, result = self.partial, self.torus, []
        along_z, along_y, along_x = self.along
        if stage == 2:
            rows = self.block(1, 0, 0)
            result.append(self.copy(1, 12, partial.at[rows], along_z, torus.other()))
        for d in (1, 2, 3):
            for plane in (0, 1):
                slot = (d - 1) * 2 + plane
                if stage == 0:
                    rows, target = self.group(plane, d), along_x.at[slot]
                    device = torus.device(0, d, 0)
                elif stage == 1:
                    rows, target = self.block(plane, 0, d), along_y.at[slot]
                    device = torus.device(0, 0, d)
                else:
                    continue
                result.append(self.copy(1, stage * 6 + slot, partial.at[rows], target, device))
        return result

    def reduce(self, stage):
        along_z, along_y, along_x = self.along
        if stage > 0:
            for copy in self.reduce_copies(stage - 1):
                copy.wait()
        if stage in (1, 2):
            for plane in (0, 1):
                rows = self.group(plane, 0) if stage == 1 else self.block(plane, 0, 0)
                arrived = along_x if stage == 1 else along_y
                total = self.partial[rows, :].astype(F32)
                for d in (1, 2, 3):
                    total = total + arrived[(d - 1) * 2 + plane].astype(F32)
                self.partial[rows, :] = total.astype(BF)
        if stage < 3:
            for copy in self.reduce_copies(stage):
                copy.start()
            return None
        return self.partial[self.block(0, 0, 0), :].astype(F32) + along_z[...].astype(F32)


def actor_peers():
    me = lax.axis_index("actor")
    core = me + 1 - 2 * lax.rem(me, 2)
    across = lax.rem(me + 2, 4)
    return me, (core, across, 3 - me)


def columns(quarter, start=0, size=QUARTER):
    return pl.ds(pl.multiple_of(quarter * QUARTER + start, 128), size)


def sigmoid(value):
    return 0.5 * jnp.tanh(0.5 * value) + 0.5


HALF = QUARTER // 2


def train_kernel(
    block_ref,
    head_ref,
    value_ref,
    gate_source,
    state_ref,
    counts_ref,
    start_ref,
    advantage_ref,
    return_ref,
    logprob_ref,
    action_ref,
    assigned_ref,
    out_ref,
    policy_ref,
    value_out_ref,
    values_ref,
    hidden,
    grads,
    scores,
    values,
    heads_held,
    heads_partial,
    heads_x,
    heads_y,
    heads_z,
    moved,
    held,
    arena,
    factors,
    head_grad,
    gates,
    aux,
    preact,
    cell,
    carry_hidden,
    carry_cell,
    sent,
    got,
    gather_send,
    gather_recv,
    step_send,
    step_recv,
    back_send,
    back_recv,
    reduce_send,
    reduce_recv,
    value_send,
    value_recv,
    ready,
    gate_ref,
    gate_sem,
    *heads_sems,
):
    gate_copy = pltpu.make_async_copy(gate_source, gate_ref, gate_sem)
    gate_copy.start()
    torus = Torus()
    me, peers = actor_peers()
    core, across, diagonal = peers
    far_devices = [torus.device(0, 2, 0), torus.device(0, 0, 2)]
    meet(torus.neighbours() + far_devices + [{"actor": peer} for peer in peers])
    place = lax.axis_index("learn")
    mine = pl.ds(pl.multiple_of(place * 64, 64), 64)
    held[mine, :] = block_ref[...].reshape(64, UNITS)
    heads_held[mine, 0:CHOICES] = head_ref[...]
    line = jnp.concatenate([value_ref[...].astype(F32), jnp.zeros((1, 64), F32)], axis=1)
    heads_held[mine, CHOICES:PAIR] = jnp.broadcast_to(line, (128, 128)).T[0:64].astype(BF)
    heads_moves = Heads(torus, heads_held, heads_partial, heads_x, heads_y, heads_z, heads_sems)

    def pieces(t):
        return (
            (hidden.at[t, :, columns(me)], core),
            (hidden.at[t, :, columns(me, 0, HALF)], across),
            (hidden.at[t, :, columns(me, HALF, HALF)], across),
            (hidden.at[t, :, columns(me, HALF, HALF)], diagonal),
            (hidden.at[t, :, columns(across, 0, HALF)], core),
        )

    def landed(t):
        return (
            hidden.at[t, :, columns(core)],
            hidden.at[t, :, columns(across, 0, HALF)],
            hidden.at[t, :, columns(across, HALF, HALF)],
            hidden.at[t, :, columns(diagonal, HALF, HALF)],
            hidden.at[t, :, columns(diagonal, 0, HALF)],
        )

    def step_copy(t, index):
        part, peer = pieces(t)[index]
        return pltpu.make_async_remote_copy(
            src_ref=part,
            dst_ref=part,
            send_sem=step_send.at[t, index],
            recv_sem=step_recv.at[t, index],
            device_id={"actor": peer},
            device_id_type=MESH,
        )

    def arrive(t, index):
        part = landed(t)[index]
        pltpu.make_async_remote_copy(
            src_ref=part,
            dst_ref=part,
            send_sem=step_send.at[t, index],
            recv_sem=step_recv.at[t, index],
            device_id={"actor": core},
            device_id_type=MESH,
        ).wait_recv()

    def multiply(t, spot, first=False):
        part = hidden[t, :, spot]
        for k in range(4):
            wide = pl.ds(k * QUARTER, QUARTER)
            product = jnp.dot(part, held[spot, wide], preferred_element_type=F32)
            if first:
                preact[:, wide] = product
            else:
                preact[:, wide] += product

    def column(t, kind):
        lane = lax.broadcasted_iota(jnp.int32, (BATCH, 128), 1)
        return jnp.sum(jnp.where(lane == t + 16 * kind, aux[...], 0.0), axis=1, keepdims=True)

    def heads(index):
        t = index - 1
        result = jnp.dot(hidden[index], heads_held[...], preferred_element_type=F32)
        logits = result[:, 0:CHOICES]
        estimate = result[:, CHOICES : CHOICES + 1]
        share = aux[:, 80:81]
        lane = lax.broadcasted_iota(jnp.int32, (BATCH, CHOICES), 1)
        onehot = (lane.astype(F32) == column(t, 4)).astype(F32)
        shifted = logits - jnp.max(logits, axis=1, keepdims=True)
        powers = jnp.exp(shifted)
        total = jnp.sum(powers, axis=1, keepdims=True)
        chosen = jnp.sum(shifted * onehot, axis=1, keepdims=True) - jnp.log(total)
        ratio = jnp.exp(chosen - column(t, 3))
        slope = (0.5 * (ratio - 1.0) - ratio * column(t, 1)) * share
        grad_logits = slope * (onehot - powers / total)
        grad_estimate = (estimate - column(t, 2)) * share
        scores[index, :, 0:CHOICES] = grad_logits.astype(BF)
        scores[index, :, CHOICES : 2 * CHOICES] = jnp.where(lane == 0, grad_estimate, 0.0).astype(BF)
        live = (share > 0.0).astype(F32)
        values[...] = jnp.where(lane == t, estimate * live, values[...])
        head_grad[index] = lax.dot_general(
            scores[index],
            heads_held[columns(me), :],
            (((1,), (1,)), ((), ())),
            preferred_element_type=F32,
        )

    def cells(t, half):
        keep = column(t, 0)
        for chunk in range(2 * half, 2 * half + 2):
            spot = pl.ds(chunk * 128, 128)
            kept = keep * cell[:, spot]
            inputs = []
            for k in range(4):
                wide = pl.ds(k * QUARTER + chunk * 128, 128)
                inputs.append(gates[t, :, wide].astype(F32) + keep * preact[:, wide])
            inp = sigmoid(inputs[0])
            forget = sigmoid(inputs[1])
            cand = jnp.tanh(inputs[2])
            outg = sigmoid(inputs[3])
            new_cell = forget * kept + inp * cand
            squash = jnp.tanh(new_cell)
            cell[:, spot] = new_cell
            part = pl.ds(pl.multiple_of(me * QUARTER + chunk * 128, 128), 128)
            hidden[t + 1, :, part] = (outg * squash).astype(BF)
            kept_factors = (
                outg * (1.0 - squash * squash),
                keep * cand * inp * (1.0 - inp),
                kept * forget * (1.0 - forget),
                keep * inp * (1.0 - cand * cand),
                keep * squash * outg * (1.0 - outg),
                keep * forget,
            )
            for index, value in enumerate(kept_factors):
                factors[t, index, :, spot] = value.astype(BF)

    hidden[0, :, columns(me)] = state_ref[:, 0, :]
    for index in (1, 2, 3, 0):
        step_copy(0, index).start()
    cell[...] = state_ref[:, 1, :].astype(F32)
    values[...] = jnp.zeros_like(values)
    row = lax.broadcasted_iota(jnp.int32, (BATCH, 128), 0)
    live = jnp.where(row < counts_ref[place], 1.0 / STEPS, 0.0)
    table = jnp.concatenate(
        [
            1.0 - start_ref[...].astype(F32),
            advantage_ref[...].astype(F32),
            return_ref[...].astype(F32),
            logprob_ref[...].astype(F32),
            action_ref[...].astype(F32),
            jnp.zeros((48, BATCH), F32),
        ],
        axis=0,
    )
    table = jnp.concatenate([table, jnp.zeros((128, 128 - BATCH), F32)], axis=1)
    lane = lax.broadcasted_iota(jnp.int32, (BATCH, 128), 1)
    aux[...] = jnp.where(lane < 80, table.T[0:BATCH], live)

    def unpack(t):
        if t == 0:
            gate_copy.wait()
        gates[t] = gate_ref[:, t].reshape(BATCH, UNITS)

    gather_blocks(held, gather_send, gather_recv, unpack)

    def step(t, carry):
        multiply(t, columns(me), True)
        stripe = pl.ds(pl.multiple_of(t * 128, 128), 128)
        arena[:, stripe] = held[stripe, :].T
        arrive(t, 0)
        multiply(t, columns(core))

        for stage, when in enumerate(GATHER_AT):

            @pl.when(t == when)
            def _(stage=stage):
                heads_moves.gather(stage)

        @pl.when(t > GATHER_AT[3])
        def _():
            heads(2 * (t - GATHER_AT[3]) - 1)
            heads(2 * (t - GATHER_AT[3]))

        arrive(t, 1)
        step_copy(t, 4).start()
        multiply(t, columns(across, 0, HALF))
        arrive(t, 2)
        multiply(t, columns(across, HALF, HALF))
        arrive(t, 3)
        multiply(t, columns(diagonal, HALF, HALF))
        arrive(t, 4)
        multiply(t, columns(diagonal, 0, HALF))
        cells(t, 0)
        step_copy(t + 1, 1).start()
        cells(t, 1)
        for index in (2, 3, 0):
            step_copy(t + 1, index).start()
        for index in range(5):
            step_copy(t, index).wait_send()
        return carry

    lax.fori_loop(0, STEPS, step, 0)
    heads(STEPS - 1)
    arrive(STEPS, 1)
    step_copy(STEPS, 4).start()
    for index in (0, 2, 3, 4):
        arrive(STEPS, index)
    for index in range(5):
        step_copy(STEPS, index).wait_send()
    heads(STEPS)

    carry_hidden[...] = jnp.zeros_like(carry_hidden)
    carry_cell[...] = jnp.zeros_like(carry_cell)

    targets = (diagonal, across, core)

    def back_copy(t, index):
        return pltpu.make_async_remote_copy(
            src_ref=sent.at[t, index],
            dst_ref=got.at[t, index],
            send_sem=back_send.at[t, index],
            recv_sem=back_recv.at[t, index],
            device_id={"actor": targets[index]},
            device_id_type=MESH,
        )

    def cell_back(t):
        for chunk in range(QUARTER // 128):
            spot = pl.ds(chunk * 128, 128)
            factor = [factors[t, index, :, spot].astype(F32) for index in range(6)]
            total = head_grad[t + 1, :, spot] + carry_hidden[:, spot]
            dcell = carry_cell[:, spot] + total * factor[0]
            carry_cell[:, spot] = dcell * factor[5]
            parts = (dcell * factor[1], dcell * factor[2], dcell * factor[3], total * factor[4])
            for k, part in enumerate(parts):
                grads[t, :, pl.ds(k * QUARTER + chunk * 128, 128)] = part.astype(BF)

    def product(t, spot):
        return jnp.dot(grads[t], arena[:, spot], preferred_element_type=F32)

    def back(i, carry):
        t = STEPS - 1 - i
        cell_back(t)
        for index in range(3):
            sent[t, index] = product(t, columns(targets[index])).astype(BF)
            back_copy(t, index).start()
        carry_hidden[...] = product(t, columns(me))

        @pl.when(i < 8)
        def _():
            spot = pl.ds(pl.multiple_of(i * 256, 256), 256)
            heads_partial[spot, :] = lax.dot_general(
                hidden[1 : STEPS + 1, :, spot].reshape(STEPS * BATCH, 256),
                scores[1 : STEPS + 1].reshape(STEPS * BATCH, PAIR),
                (((0,), (0,)), ((), ())),
                preferred_element_type=F32,
            ).astype(BF)

        for stage, when in enumerate(REDUCE_AT):

            @pl.when(i == when)
            def _(stage=stage):
                heads_moves.reduce(stage)

        for index in (2, 0, 1):
            back_copy(t, index).wait_recv()
            carry_hidden[...] += got[t, index].astype(F32)
        for index in range(3):
            back_copy(t, index).wait_send()
        return carry

    lax.fori_loop(0, STEPS - 1, back, 0)
    for device in torus.neighbours():
        pl.semaphore_signal(ready, inc=1, device_id=device, device_id_type=MESH)
    cell_back(0)
    heads_total = heads_moves.reduce(3)
    policy_ref[...] = heads_total[:, 0:CHOICES]
    value_out_ref[...] = heads_total[:, CHOICES:PAIR].T[0:1, 0:64]
    pl.semaphore_wait(ready, 5)
    estimates = jnp.concatenate([values[...], values[...]], axis=0).T[0:STEPS, 0:BATCH]
    exchange = exchange_values(torus, assigned_ref, estimates, moved, value_send, value_recv)
    reduce_blocks(
        torus,
        hidden,
        grads,
        exchange,
        out_ref,
        held,
        arena,
        reduce_send,
        reduce_recv,
    )
    values_ref[...] = moved[6, :, 0:BATCH]


RESULTS = (
    jax.ShapeDtypeStruct((64, 4, QUARTER), F32),
    jax.ShapeDtypeStruct((64, CHOICES), F32),
    jax.ShapeDtypeStruct((1, 64), F32),
    jax.ShapeDtypeStruct((STEPS, BATCH), F32),
)


def hand_on_kernel(*refs):
    for source, target in zip(refs[:4], refs[4:]):
        target[...] = source[...]


def hand_on(*results):
    return pl.pallas_call(
        hand_on_kernel,
        out_shape=RESULTS,
        in_specs=[VMEM] * 4,
        out_specs=(VMEM,) * 4,
        name="hand_on",
    )(*results)


def train(*operands):
    specs = [VMEM] * len(operands)
    specs[5] = pl.BlockSpec(memory_space=pltpu.SMEM)
    specs[3] = pl.BlockSpec(memory_space=pl.ANY)
    return pl.pallas_call(
        train_kernel,
        out_shape=RESULTS,
        in_specs=specs,
        out_specs=(VMEM,) * 4,
        scratch_shapes=[
            pltpu.VMEM((STEPS + 1, BATCH, UNITS), BF),
            pltpu.VMEM((STEPS, BATCH, UNITS), BF),
            pltpu.VMEM((STEPS + 1, BATCH, 2 * CHOICES), BF),
            pltpu.VMEM((BATCH, 128), F32),
            pltpu.VMEM((UNITS, PAIR), BF),
            pltpu.VMEM((UNITS, PAIR), BF),
            pltpu.VMEM((6, 256, PAIR), BF),
            pltpu.VMEM((6, 64, PAIR), BF),
            pltpu.VMEM((64, PAIR), BF),
            pltpu.VMEM((10, STEPS, 128), F32),
            pltpu.VMEM((UNITS, UNITS), BF),
            pltpu.VMEM((UNITS, UNITS), BF),
            pltpu.VMEM((STEPS, 6, BATCH, QUARTER), BF),
            pltpu.VMEM((STEPS + 1, BATCH, QUARTER), F32),
            pltpu.VMEM((STEPS, BATCH, UNITS), BF),
            pltpu.VMEM((BATCH, 128), F32),
            pltpu.VMEM((BATCH, UNITS), F32),
            pltpu.VMEM((BATCH, QUARTER), F32),
            pltpu.VMEM((BATCH, QUARTER), F32),
            pltpu.VMEM((BATCH, QUARTER), F32),
            pltpu.VMEM((STEPS, 3, BATCH, QUARTER), BF),
            pltpu.VMEM((STEPS, 3, BATCH, QUARTER), BF),
            pltpu.SemaphoreType.DMA((len(KEYS),)),
            pltpu.SemaphoreType.DMA((len(KEYS),)),
            pltpu.SemaphoreType.DMA((STEPS + 1, 5)),
            pltpu.SemaphoreType.DMA((STEPS + 1, 5)),
            pltpu.SemaphoreType.DMA((STEPS, 3)),
            pltpu.SemaphoreType.DMA((STEPS, 3)),
            pltpu.SemaphoreType.DMA((len(KEYS),)),
            pltpu.SemaphoreType.DMA((len(KEYS),)),
            pltpu.SemaphoreType.DMA((10,)),
            pltpu.SemaphoreType.DMA((10,)),
            pltpu.SemaphoreType.REGULAR,
            pltpu.VMEM((BATCH, STEPS, 4, QUARTER), BF),
            pltpu.SemaphoreType.DMA(()),
            pltpu.SemaphoreType.DMA((13,)),
            pltpu.SemaphoreType.DMA((13,)),
            pltpu.SemaphoreType.DMA((13,)),
            pltpu.SemaphoreType.DMA((13,)),
        ],
        compiler_params=params(1),
        name="train",
    )(*operands)


def shards(
    rec_weight,
    head_weight,
    value_head,
    gate_inputs,
    start_state,
    advantages,
    returns,
    old_logprob,
    taken_action,
    episode_start,
    segment_counts,
    assignment,
):
    results = train(
        rec_weight,
        head_weight,
        value_head[None],
        gate_inputs[0],
        start_state[0],
        segment_counts,
        episode_start[0].T,
        advantages[0].T,
        returns[0].T,
        old_logprob[0].T,
        taken_action[0].T,
        assignment,
    )
    rec_share, policy_share, value_share, values = hand_on(*results)
    return (rec_share, policy_share, value_share[0], values.T[None])


def solution(mesh):
    placed = (
        P("learn", None, "actor"),
        P("learn", None),
        P("learn"),
        P("learn", None, None, None, "actor"),
        P("learn", None, None, "actor"),
        P("learn", None, None),
        P("learn", None, None),
        P("learn", None, None),
        P("learn", None, None),
        P("learn", None, None),
        P(),
        P("learn", None),
    )
    return jax.shard_map(
        shards,
        mesh=mesh,
        in_specs=placed,
        out_specs=(P("learn", None, "actor"), P("learn", None), P("learn"), P("learn", None, None)),
        check_vma=False,
    )
```

```python
import jax
import jax.numpy as jnp
from jax import lax
from jax.experimental import pallas as pl
from jax.experimental.pallas import tpu as pltpu
from jax.sharding import PartitionSpec as P

MESH = pl.DeviceIdType.MESH
BF = jnp.bfloat16
F32 = jnp.float32
UNITS = 2048
QUARTER = 512
BATCH = 64
STEPS = 16
CHOICES = 128
PAIR = 2 * CHOICES
VMEM = pl.BlockSpec(memory_space=pltpu.VMEM)
LIMIT = 60 * 2**20
OFFSETS = (2, -1, 1, 0)


def params(collective):
    return pltpu.CompilerParams(
        collective_id=collective, has_side_effects=True, vmem_limit_bytes=LIMIT
    )


def meet(devices):
    barrier = pltpu.get_barrier_semaphore()
    for device in devices:
        pl.semaphore_signal(barrier, inc=1, device_id=device, device_id_type=MESH)
    pl.semaphore_wait(barrier, len(devices))


GATHER_AT = (0, 1, 3, 8)
REDUCE_AT = (8, 11, 13)


class Torus:
    def __init__(self):
        place = lax.axis_index("learn")
        self.z, self.x, self.y = place // 16, lax.rem(place // 4, 4), lax.rem(place, 4)

    def device(self, dz, dx, dy):
        z = lax.rem(self.z + dz, 2)
        x = lax.rem(self.x + dx + 4, 4)
        y = lax.rem(self.y + dy + 4, 4)
        return {"learn": z * 16 + x * 4 + y}

    def first(self, half, d):
        return self.device(0, d, 0) if half == 0 else self.device(0, 0, d)

    def second(self, half, d):
        return self.device(0, 0, d) if half == 0 else self.device(0, d, 0)

    def other(self):
        return self.device(1, 0, 0)

    def neighbours(self):
        return [
            self.device(0, 1, 0),
            self.device(0, -1, 0),
            self.device(0, 0, 1),
            self.device(0, 0, -1),
            self.other(),
        ]

    def rows(self, half, plane, dp, dq, part=None):
        dx, dy = (dp, dq) if half == 0 else (dq, dp)
        block = self.device(plane, dx, dy)["learn"]
        start = block * 64 + 32 * half
        if part is None:
            return pl.ds(pl.multiple_of(start, 32), 32)
        return pl.ds(pl.multiple_of(start + 16 * part, 16), 16)


def gather_keys():
    keys = []
    for half in (0, 1):
        keys += [("p", half, d) for d in (1, -1)]
        keys += [("pf", half, d) for d in (1, -1)]
        keys += [("z", half, dp) for dp in OFFSETS]
        keys += [("zq", half)]
        for plane in (0, 1):
            for dp in OFFSETS:
                keys += [("q", half, plane, dp, d) for d in (1, -1)]
                keys += [("qf", half, plane, dp, d) for d in (1, -1)]
    return {key: index for index, key in enumerate(keys)}


KEYS = gather_keys()


def gather_blocks(held, send_sems, recv_sems, work):
    torus = Torus()
    started = []

    def move(key, rows, device):
        index = KEYS[key]
        return pltpu.make_async_remote_copy(
            src_ref=held.at[rows],
            dst_ref=held.at[rows],
            send_sem=send_sems.at[index],
            recv_sem=recv_sems.at[index],
            device_id=device,
            device_id_type=MESH,
        )

    def send(key, rows, device):
        copy = move(key, rows, device)
        copy.start()
        started.append(copy)

    def arrive(key, rows):
        move(key, rows, torus.other()).wait_recv()

    left = list(range(STEPS))

    def spread(half, plane, dp):
        for d in (1, -1):
            send(("q", half, plane, dp, d), torus.rows(half, plane, dp, 0), torus.second(half, d))

    def pass_on(half, plane, dp):
        for d in (1, -1):
            part = 0 if d == 1 else 1
            arrive(("q", half, plane, dp, d), torus.rows(half, plane, dp, -d))
            if (plane, dp) != (1, 0):
                send(
                    ("qf", half, plane, dp, d),
                    torus.rows(half, plane, dp, -d, part),
                    torus.second(half, d),
                )

    def cross(half, dp):
        send(("z", half, dp), torus.rows(half, 0, dp, 0), torus.other())

    def crossed(half, dp):
        for t in left[:2]:
            work(t)
        del left[:2]
        arrive(("z", half, dp), torus.rows(half, 1, dp, 0))
        spread(half, 1, dp)

    for half in (0, 1):
        for d in (1, -1):
            send(("p", half, d), torus.rows(half, 0, 0, 0), torus.first(half, d))
    for half in (0, 1):
        cross(half, 0)
        spread(half, 0, 0)
    for half in (0, 1):
        for d in (1, -1):
            part = 0 if d == 1 else 1
            arrive(("p", half, d), torus.rows(half, 0, -d, 0))
            send(("pf", half, d), torus.rows(half, 0, -d, 0, part), torus.first(half, d))
            cross(half, -d)
    for half in (0, 1):
        for d in (1, -1):
            spread(half, 0, -d)
    for half in (0, 1):
        crossed(half, 0)
        for d in (1, -1):
            part = 0 if d == 1 else 1
            arrive(("pf", half, d), torus.rows(half, 0, -2 * d, 0, part))
        cross(half, 2)
        spread(half, 0, 2)
    for half in (0, 1):
        pass_on(half, 0, 0)
    for half in (0, 1):
        for d in (1, -1):
            crossed(half, -d)
    for half in (0, 1):
        for d in (1, -1):
            pass_on(half, 0, -d)
    for half in (0, 1):
        crossed(half, 2)
    for half in (0, 1):
        pass_on(half, 1, 0)
    for half in (0, 1):
        for d in (1, -1):
            part = 0 if d == 1 else 1
            arrive(("qf", half, 0, 0, d), torus.rows(half, 0, 0, -2 * d, part))
        send(("zq", half), torus.rows(half, 0, 0, 2), torus.other())
    for half in (0, 1):
        pass_on(half, 0, 2)
    for half in (0, 1):
        for d in (1, -1):
            pass_on(half, 1, -d)
    for half in (0, 1):
        pass_on(half, 1, 2)
    for half in (0, 1):
        for plane in (0, 1):
            for dp in (2, -1, 1):
                for d in (1, -1):
                    part = 0 if d == 1 else 1
                    arrive(
                        ("qf", half, plane, dp, d), torus.rows(half, plane, dp, -2 * d, part)
                    )
        arrive(("zq", half), torus.rows(half, 1, 0, 2))
    for copy in started:
        copy.wait_send()


def exchange_values(torus, assigned_ref, estimates, moved, send_sems, recv_sems):
    lane = lax.broadcasted_iota(jnp.int32, (STEPS, 128), 1)
    phases = (
        (0, torus.y, 2, 4, lambda d: torus.device(0, 0, d)),
        (4, torus.x, 8, 4, lambda d: torus.device(0, d, 0)),
        (8, torus.z, 32, 2, lambda d: torus.device(d, 0, 0)),
    )

    def copies(phase):
        first, _, _, size, device = phases[phase]
        return [
            pltpu.make_async_remote_copy(
                src_ref=moved.at[first],
                dst_ref=moved.at[first + d],
                send_sem=send_sems.at[first + d],
                recv_sem=recv_sems.at[first + d],
                device_id=device(d),
                device_id_type=MESH,
            )
            for d in range(1, size)
        ]

    def start(phase):
        for copy in copies(phase):
            copy.start()

    def finish(phase):
        first, place, stride, size, _ = phases[phase]
        for copy in copies(phase):
            copy.wait()
        field = lax.rem(lane // stride, size)
        result = jnp.zeros((STEPS, 128), F32)
        for d in range(size):
            source = lax.rem(place - d + size, size)
            shift = lax.rem((source - place) * stride + 128, 128)
            turned = pltpu.roll(moved[first + d], shift, 1)
            result = jnp.where(field == source, turned, result)
        return result

    def run(stage):
        if stage == 0:
            row = jnp.broadcast_to(assigned_ref[...].astype(F32), (BATCH, BATCH))
            row = jnp.concatenate([row, jnp.full((BATCH, 128 - BATCH), -1.0, F32)], axis=1)
            tall = jnp.concatenate([row, row], axis=0).T
            column = tall[0:BATCH, :]
            across = lax.broadcasted_iota(jnp.int32, (BATCH, 128), 1)
            down = lax.broadcasted_iota(jnp.int32, (BATCH, 128), 0)
            earlier = jnp.where((row == column) & (across < down), 1.0, 0.0)
            target = 2.0 * column + jnp.sum(earlier, axis=1, keepdims=True)
            spread = jnp.where(across.astype(F32) == target, 1.0, 0.0)
            moved[0] = jnp.dot(
                estimates,
                spread,
                preferred_element_type=F32,
                precision=lax.Precision.HIGHEST,
            )
            start(0)
        elif stage < 3:
            moved[phases[stage][0]] = finish(stage - 1)
            start(stage)
        else:
            moved[6] = finish(2)

    return run


def reduce_blocks(
    torus,
    hidden,
    grads,
    exchange,
    out_ref,
    own,
    arena,
    send_sems,
    recv_sems,
):
    started = []
    where = {}
    counts = {16: 0, 32: 0}
    for key in KEYS:
        size = 16 if key[0] in ("qf", "pf") else 32
        where[key] = counts[size]
        counts[size] += 1

    def landing(key):
        size = 16 if key[0] in ("qf", "pf") else 32
        base = 0 if size == 32 else counts[32] * 32
        return arena.at[pl.ds(base + where[key] * size, size)]

    def send(key, source, device):
        index = KEYS[key]
        copy = pltpu.make_async_remote_copy(
            src_ref=source,
            dst_ref=landing(key),
            send_sem=send_sems.at[index],
            recv_sem=recv_sems.at[index],
            device_id=device,
            device_id_type=MESH,
        )
        copy.start()
        started.append(copy)

    def arrived(key):
        index = KEYS[key]
        ref = landing(key)
        pltpu.make_async_remote_copy(
            src_ref=ref,
            dst_ref=ref,
            send_sem=send_sems.at[index],
            recv_sem=recv_sems.at[index],
            device_id=torus.other(),
            device_id_type=MESH,
        ).wait_recv()
        return ref[...].astype(F32)

    def multiply(plane, dx):
        first = torus.device(plane, dx, 0)["learn"] // 4
        spot = pl.ds(pl.multiple_of(first * 256, 256), 256)
        kept = hidden[0:STEPS, :, spot].reshape(STEPS * BATCH, 256)
        for k in range(4):
            part = pl.ds(k * QUARTER, QUARTER)
            own[spot, part] = lax.dot_general(
                kept,
                grads[:, :, part].reshape(STEPS * BATCH, QUARTER),
                (((0,), (0,)), ((), ())),
                preferred_element_type=F32,
            ).astype(BF)

    def far(half, plane, dp):
        for d in (1, -1):
            part = 0 if d == 1 else 1
            send(
                ("qf", half, plane, dp, d),
                own.at[torus.rows(half, plane, dp, -2 * d, part)],
                torus.second(half, -d),
            )

    def near(half, plane, dp, d):
        part = 0 if d == 1 else 1
        extra = arrived(("qf", half, plane, dp, d))
        rows = torus.rows(half, plane, dp, -d, part)
        own[rows, :] = (own[rows, :].astype(F32) + extra).astype(BF)
        block = own.at[torus.rows(half, plane, dp, -d)]
        send(("q", half, plane, dp, d), block, torus.second(half, -d))

    def line(half, plane, dp):
        total = own[torus.rows(half, plane, dp, 0), :].astype(F32)
        for d in (1, -1):
            total = total + arrived(("q", half, plane, dp, d))
        return total

    def cross(half, dp):
        rows = torus.rows(half, 1, dp, 0)
        own[rows, :] = line(half, 1, dp).astype(BF)
        send(("z", half, dp), own.at[rows], torus.other())

    def plane_sum(half, dp):
        return line(half, 0, dp) + arrived(("z", half, dp))

    def product(plane, dp):
        multiply(plane, dp)
        if dp == 2:
            for other in OFFSETS:
                far(1, plane, other)
        far(0, plane, dp)

    for dp in OFFSETS:
        product(1, dp)
        if dp == 2:
            exchange(0)
    for dp in OFFSETS:
        for half in (0, 1):
            for d in (1, -1):
                near(half, 1, dp, d)
    exchange(1)
    for dp in OFFSETS:
        product(0, dp)
        for half in (0, 1):
            cross(half, dp)
    exchange(2)
    for dp in OFFSETS:
        for half in (0, 1):
            for d in (1, -1):
                near(half, 0, dp, d)
    exchange(3)
    for half in (0, 1):
        own[torus.rows(half, 0, 2, 0), :] = plane_sum(half, 2).astype(BF)
        for d in (1, -1):
            part = 0 if d == 1 else 1
            block = own.at[torus.rows(half, 0, 2, 0, part)]
            send(("pf", half, d), block, torus.first(half, -d))
    for half in (0, 1):
        for d in (1, -1):
            part = 0 if d == 1 else 1
            rows = torus.rows(half, 0, -d, 0)
            own[rows, :] = plane_sum(half, -d).astype(BF)
            extra = arrived(("pf", half, d))
            some = torus.rows(half, 0, -d, 0, part)
            own[some, :] = (own[some, :].astype(F32) + extra).astype(BF)
            send(("p", half, d), own.at[rows], torus.first(half, -d))
    for half in (0, 1):
        total = plane_sum(half, 0)
        for d in (1, -1):
            total = total + arrived(("p", half, d))
        rows = pl.ds(32 * half, 32)
        for k in range(4):
            out_ref[rows, k, :] = total[:, k * QUARTER : (k + 1) * QUARTER]
    for copy in started:
        copy.wait_send()


class Heads:
    def __init__(self, torus, held, partial, along_x, along_y, along_z, sems):
        self.torus, self.held, self.partial = torus, held, partial
        self.along = (along_z, along_y, along_x)
        self.sems = sems

    def group(self, plane, dx):
        first = self.torus.device(plane, dx, 0)["learn"] // 4
        return pl.ds(pl.multiple_of(first * 256, 256), 256)

    def block(self, plane, dx, dy):
        return pl.ds(pl.multiple_of(self.torus.device(plane, dx, dy)["learn"] * 64, 64), 64)

    def copy(self, way, index, source, target, device):
        return pltpu.make_async_remote_copy(
            src_ref=source,
            dst_ref=target,
            send_sem=self.sems[2 * way].at[index],
            recv_sem=self.sems[2 * way + 1].at[index],
            device_id=device,
            device_id_type=MESH,
        )

    def gather_copies(self, stage, arrivals):
        held, torus, result = self.held, self.torus, []
        if stage == 0:
            rows = self.block(1 if arrivals else 0, 0, 0)
            result.append(self.copy(0, 0, held.at[rows], held.at[rows], torus.other()))
        for d in (1, 2, 3):
            for plane in (0, 1):
                index = 1 + (stage - 1) * 6 + (d - 1) * 2 + plane
                shift = 4 - d if arrivals else 0
                if stage == 1:
                    rows = self.block(plane, 0, shift)
                    device = torus.device(0, 0, d)
                elif stage == 2:
                    rows = self.group(plane, shift)
                    device = torus.device(0, d, 0)
                else:
                    continue
                result.append(self.copy(0, index, held.at[rows], held.at[rows], device))
        return result

    def gather(self, stage):
        if stage > 0:
            for copy in self.gather_copies(stage - 1, True):
                copy.wait_recv()
            for copy in self.gather_copies(stage - 1, False):
                copy.wait_send()
        if stage < 3:
            for copy in self.gather_copies(stage, False):
                copy.start()

    def reduce_copies(self, stage):
        partial, torus, result = self.partial, self.torus, []
        along_z, along_y, along_x = self.along
        if stage == 2:
            rows = self.block(1, 0, 0)
            result.append(self.copy(1, 12, partial.at[rows], along_z, torus.other()))
        for d in (1, 2, 3):
            for plane in (0, 1):
                slot = (d - 1) * 2 + plane
                if stage == 0:
                    rows, target = self.group(plane, d), along_x.at[slot]
                    device = torus.device(0, d, 0)
                elif stage == 1:
                    rows, target = self.block(plane, 0, d), along_y.at[slot]
                    device = torus.device(0, 0, d)
                else:
                    continue
                result.append(self.copy(1, stage * 6 + slot, partial.at[rows], target, device))
        return result

    def reduce(self, stage):
        along_z, along_y, along_x = self.along
        if stage > 0:
            for copy in self.reduce_copies(stage - 1):
                copy.wait()
        if stage in (1, 2):
            for plane in (0, 1):
                rows = self.group(plane, 0) if stage == 1 else self.block(plane, 0, 0)
                arrived = along_x if stage == 1 else along_y
                total = self.partial[rows, :].astype(F32)
                for d in (1, 2, 3):
                    total = total + arrived[(d - 1) * 2 + plane].astype(F32)
                self.partial[rows, :] = total.astype(BF)
        if stage < 3:
            for copy in self.reduce_copies(stage):
                copy.start()
            return None
        return self.partial[self.block(0, 0, 0), :].astype(F32) + along_z[...].astype(F32)


def actor_peers():
    me = lax.axis_index("actor")
    core = me + 1 - 2 * lax.rem(me, 2)
    across = lax.rem(me + 2, 4)
    return me, (core, across, 3 - me)


def columns(quarter, start=0, size=QUARTER):
    return pl.ds(pl.multiple_of(quarter * QUARTER + start, 128), size)


def sigmoid(value):
    return 0.5 * jnp.tanh(0.5 * value) + 0.5


HALF = QUARTER // 2


def train_kernel(
    block_ref,
    head_ref,
    value_ref,
    gate_source,
    state_ref,
    counts_ref,
    start_ref,
    advantage_ref,
    return_ref,
    logprob_ref,
    action_ref,
    assigned_ref,
    out_ref,
    policy_ref,
    value_out_ref,
    values_ref,
    hidden,
    grads,
    scores,
    values,
    heads_held,
    heads_partial,
    heads_x,
    heads_y,
    heads_z,
    moved,
    held,
    arena,
    factors,
    head_grad,
    gates,
    aux,
    preact,
    cell,
    carry_hidden,
    carry_cell,
    sent,
    got,
    gather_send,
    gather_recv,
    step_send,
    step_recv,
    back_send,
    back_recv,
    reduce_send,
    reduce_recv,
    value_send,
    value_recv,
    ready,
    gate_ref,
    gate_sem,
    *heads_sems,
):
    gate_copy = pltpu.make_async_copy(gate_source, gate_ref, gate_sem)
    gate_copy.start()
    torus = Torus()
    me, peers = actor_peers()
    core, across, diagonal = peers
    far_devices = [torus.device(0, 2, 0), torus.device(0, 0, 2)]
    meet(torus.neighbours() + far_devices + [{"actor": peer} for peer in peers])
    place = lax.axis_index("learn")
    mine = pl.ds(pl.multiple_of(place * 64, 64), 64)
    held[mine, :] = block_ref[...].reshape(64, UNITS)
    heads_held[mine, 0:CHOICES] = head_ref[...]
    line = jnp.concatenate([value_ref[...].astype(F32), jnp.zeros((1, 64), F32)], axis=1)
    heads_held[mine, CHOICES:PAIR] = jnp.broadcast_to(line, (128, 128)).T[0:64].astype(BF)
    heads_moves = Heads(torus, heads_held, heads_partial, heads_x, heads_y, heads_z, heads_sems)

    def pieces(t):
        return (
            (hidden.at[t, :, columns(me)], core),
            (hidden.at[t, :, columns(me, 0, HALF)], across),
            (hidden.at[t, :, columns(me, HALF, HALF)], across),
            (hidden.at[t, :, columns(me, HALF, HALF)], diagonal),
            (hidden.at[t, :, columns(across, 0, HALF)], core),
        )

    def landed(t):
        return (
            hidden.at[t, :, columns(core)],
            hidden.at[t, :, columns(across, 0, HALF)],
            hidden.at[t, :, columns(across, HALF, HALF)],
            hidden.at[t, :, columns(diagonal, HALF, HALF)],
            hidden.at[t, :, columns(diagonal, 0, HALF)],
        )

    def step_copy(t, index):
        part, peer = pieces(t)[index]
        return pltpu.make_async_remote_copy(
            src_ref=part,
            dst_ref=part,
            send_sem=step_send.at[t, index],
            recv_sem=step_recv.at[t, index],
            device_id={"actor": peer},
            device_id_type=MESH,
        )

    def arrive(t, index):
        part = landed(t)[index]
        pltpu.make_async_remote_copy(
            src_ref=part,
            dst_ref=part,
            send_sem=step_send.at[t, index],
            recv_sem=step_recv.at[t, index],
            device_id={"actor": core},
            device_id_type=MESH,
        ).wait_recv()

    def multiply(t, spot, first=False):
        part = hidden[t, :, spot]
        for k in range(4):
            wide = pl.ds(k * QUARTER, QUARTER)
            product = jnp.dot(part, held[spot, wide], preferred_element_type=F32)
            if first:
                preact[:, wide] = product
            else:
                preact[:, wide] += product

    def column(t, kind):
        lane = lax.broadcasted_iota(jnp.int32, (BATCH, 128), 1)
        return jnp.sum(jnp.where(lane == t + 16 * kind, aux[...], 0.0), axis=1, keepdims=True)

    def heads(index):
        t = index - 1
        result = jnp.dot(hidden[index], heads_held[...], preferred_element_type=F32)
        logits = result[:, 0:CHOICES]
        estimate = result[:, CHOICES : CHOICES + 1]
        share = aux[:, 80:81]
        lane = lax.broadcasted_iota(jnp.int32, (BATCH, CHOICES), 1)
        onehot = (lane.astype(F32) == column(t, 4)).astype(F32)
        shifted = logits - jnp.max(logits, axis=1, keepdims=True)
        powers = jnp.exp(shifted)
        total = jnp.sum(powers, axis=1, keepdims=True)
        chosen = jnp.sum(shifted * onehot, axis=1, keepdims=True) - jnp.log(total)
        ratio = jnp.exp(chosen - column(t, 3))
        slope = (0.5 * (ratio - 1.0) - ratio * column(t, 1)) * share
        grad_logits = slope * (onehot - powers / total)
        grad_estimate = (estimate - column(t, 2)) * share
        scores[index, :, 0:CHOICES] = grad_logits.astype(BF)
        scores[index, :, CHOICES : 2 * CHOICES] = jnp.where(lane == 0, grad_estimate, 0.0).astype(BF)
        live = (share > 0.0).astype(F32)
        values[...] = jnp.where(lane == t, estimate * live, values[...])
        head_grad[index] = lax.dot_general(
            scores[index],
            heads_held[columns(me), :],
            (((1,), (1,)), ((), ())),
            preferred_element_type=F32,
        )

    def cells(t, half):
        keep = column(t, 0)
        for chunk in range(2 * half, 2 * half + 2):
            spot = pl.ds(chunk * 128, 128)
            kept = keep * cell[:, spot]
            inputs = []
            for k in range(4):
                wide = pl.ds(k * QUARTER + chunk * 128, 128)
                inputs.append(gates[t, :, wide].astype(F32) + keep * preact[:, wide])
            inp = sigmoid(inputs[0])
            forget = sigmoid(inputs[1])
            cand = jnp.tanh(inputs[2])
            outg = sigmoid(inputs[3])
            new_cell = forget * kept + inp * cand
            squash = jnp.tanh(new_cell)
            cell[:, spot] = new_cell
            part = pl.ds(pl.multiple_of(me * QUARTER + chunk * 128, 128), 128)
            hidden[t + 1, :, part] = (outg * squash).astype(BF)
            kept_factors = (
                outg * (1.0 - squash * squash),
                keep * cand * inp * (1.0 - inp),
                kept * forget * (1.0 - forget),
                keep * inp * (1.0 - cand * cand),
                keep * squash * outg * (1.0 - outg),
                keep * forget,
            )
            for index, value in enumerate(kept_factors):
                factors[t, index, :, spot] = value.astype(BF)

    hidden[0, :, columns(me)] = state_ref[:, 0, :]
    for index in (1, 2, 3, 0):
        step_copy(0, index).start()
    cell[...] = state_ref[:, 1, :].astype(F32)
    values[...] = jnp.zeros_like(values)
    row = lax.broadcasted_iota(jnp.int32, (BATCH, 128), 0)
    live = jnp.where(row < counts_ref[place], 1.0 / STEPS, 0.0)
    table = jnp.concatenate(
        [
            1.0 - start_ref[...].astype(F32),
            advantage_ref[...].astype(F32),
            return_ref[...].astype(F32),
            logprob_ref[...].astype(F32),
            action_ref[...].astype(F32),
            jnp.zeros((48, BATCH), F32),
        ],
        axis=0,
    )
    table = jnp.concatenate([table, jnp.zeros((128, 128 - BATCH), F32)], axis=1)
    lane = lax.broadcasted_iota(jnp.int32, (BATCH, 128), 1)
    aux[...] = jnp.where(lane < 80, table.T[0:BATCH], live)

    def unpack(t):
        if t == 0:
            gate_copy.wait()
        gates[t] = gate_ref[:, t].reshape(BATCH, UNITS)

    gather_blocks(held, gather_send, gather_recv, unpack)

    def step(t, carry):
        multiply(t, columns(me), True)
        stripe = pl.ds(pl.multiple_of(t * 128, 128), 128)
        arena[:, stripe] = held[stripe, :].T
        arrive(t, 0)
        multiply(t, columns(core))

        for stage, when in enumerate(GATHER_AT):

            @pl.when(t == when)
            def _(stage=stage):
                heads_moves.gather(stage)

        @pl.when(t > GATHER_AT[3])
        def _():
            heads(2 * (t - GATHER_AT[3]) - 1)
            heads(2 * (t - GATHER_AT[3]))

        arrive(t, 1)
        step_copy(t, 4).start()
        multiply(t, columns(across, 0, HALF))
        arrive(t, 2)
        multiply(t, columns(across, HALF, HALF))
        arrive(t, 3)
        multiply(t, columns(diagonal, HALF, HALF))
        arrive(t, 4)
        multiply(t, columns(diagonal, 0, HALF))
        cells(t, 0)
        step_copy(t + 1, 1).start()
        cells(t, 1)
        for index in (2, 3, 0):
            step_copy(t + 1, index).start()
        for index in range(5):
            step_copy(t, index).wait_send()
        return carry

    lax.fori_loop(0, STEPS, step, 0)
    heads(STEPS - 1)
    arrive(STEPS, 1)
    step_copy(STEPS, 4).start()
    for index in (0, 2, 3, 4):
        arrive(STEPS, index)
    for index in range(5):
        step_copy(STEPS, index).wait_send()
    heads(STEPS)

    carry_hidden[...] = jnp.zeros_like(carry_hidden)
    carry_cell[...] = jnp.zeros_like(carry_cell)

    targets = (diagonal, diagonal, across, across, core)
    spans = ((0, HALF), (HALF, HALF), (0, HALF), (HALF, HALF), (0, QUARTER))

    def back_copy(t, index):
        return pltpu.make_async_remote_copy(
            src_ref=sent.at[t, index // 2, :, pl.ds(*spans[index])],
            dst_ref=got.at[t, index // 2, :, pl.ds(*spans[index])],
            send_sem=back_send.at[t, index],
            recv_sem=back_recv.at[t, index],
            device_id={"actor": targets[index]},
            device_id_type=MESH,
        )

    def cell_back(t):
        for chunk in range(QUARTER // 128):
            spot = pl.ds(chunk * 128, 128)
            factor = [factors[t, index, :, spot].astype(F32) for index in range(6)]
            total = head_grad[t + 1, :, spot] + carry_hidden[:, spot]
            dcell = carry_cell[:, spot] + total * factor[0]
            carry_cell[:, spot] = dcell * factor[5]
            parts = (dcell * factor[1], dcell * factor[2], dcell * factor[3], total * factor[4])
            for k, part in enumerate(parts):
                grads[t, :, pl.ds(k * QUARTER + chunk * 128, 128)] = part.astype(BF)

    def product(t, spot):
        return jnp.dot(grads[t], arena[:, spot], preferred_element_type=F32)

    def back(i, carry):
        t = STEPS - 1 - i
        cell_back(t)
        for index, (first, size) in enumerate(spans):
            part = product(t, columns(targets[index], first, size)).astype(BF)
            sent[t, index // 2, :, pl.ds(first, size)] = part
            back_copy(t, index).start()
        carry_hidden[...] = product(t, columns(me))

        @pl.when(i < 8)
        def _():
            spot = pl.ds(pl.multiple_of(i * 256, 256), 256)
            heads_partial[spot, :] = lax.dot_general(
                hidden[1 : STEPS + 1, :, spot].reshape(STEPS * BATCH, 256),
                scores[1 : STEPS + 1].reshape(STEPS * BATCH, PAIR),
                (((0,), (0,)), ((), ())),
                preferred_element_type=F32,
            ).astype(BF)

        for stage, when in enumerate(REDUCE_AT):

            @pl.when(i == when)
            def _(stage=stage):
                heads_moves.reduce(stage)

        for index in (4, 0, 1, 2, 3):
            back_copy(t, index).wait_recv()
            spot = pl.ds(*spans[index])
            carry_hidden[:, spot] += got[t, index // 2, :, spot].astype(F32)
        for index in range(5):
            back_copy(t, index).wait_send()
        return carry

    lax.fori_loop(0, STEPS - 1, back, 0)
    for device in torus.neighbours():
        pl.semaphore_signal(ready, inc=1, device_id=device, device_id_type=MESH)
    cell_back(0)
    heads_total = heads_moves.reduce(3)
    policy_ref[...] = heads_total[:, 0:CHOICES]
    value_out_ref[...] = heads_total[:, CHOICES:PAIR].T[0:1, 0:64]
    pl.semaphore_wait(ready, 5)
    estimates = jnp.concatenate([values[...], values[...]], axis=0).T[0:STEPS, 0:BATCH]
    exchange = exchange_values(torus, assigned_ref, estimates, moved, value_send, value_recv)
    reduce_blocks(
        torus,
        hidden,
        grads,
        exchange,
        out_ref,
        held,
        arena,
        reduce_send,
        reduce_recv,
    )
    values_ref[...] = moved[6, :, 0:BATCH]


RESULTS = (
    jax.ShapeDtypeStruct((64, 4, QUARTER), F32),
    jax.ShapeDtypeStruct((64, CHOICES), F32),
    jax.ShapeDtypeStruct((1, 64), F32),
    jax.ShapeDtypeStruct((STEPS, BATCH), F32),
)


def hand_on_kernel(*refs):
    for source, target in zip(refs[:4], refs[4:]):
        target[...] = source[...]


def hand_on(*results):
    return pl.pallas_call(
        hand_on_kernel,
        out_shape=RESULTS,
        in_specs=[VMEM] * 4,
        out_specs=(VMEM,) * 4,
        name="hand_on",
    )(*results)


def train(*operands):
    specs = [VMEM] * len(operands)
    specs[5] = pl.BlockSpec(memory_space=pltpu.SMEM)
    specs[3] = pl.BlockSpec(memory_space=pl.ANY)
    return pl.pallas_call(
        train_kernel,
        out_shape=RESULTS,
        in_specs=specs,
        out_specs=(VMEM,) * 4,
        scratch_shapes=[
            pltpu.VMEM((STEPS + 1, BATCH, UNITS), BF),
            pltpu.VMEM((STEPS, BATCH, UNITS), BF),
            pltpu.VMEM((STEPS + 1, BATCH, 2 * CHOICES), BF),
            pltpu.VMEM((BATCH, 128), F32),
            pltpu.VMEM((UNITS, PAIR), BF),
            pltpu.VMEM((UNITS, PAIR), BF),
            pltpu.VMEM((6, 256, PAIR), BF),
            pltpu.VMEM((6, 64, PAIR), BF),
            pltpu.VMEM((64, PAIR), BF),
            pltpu.VMEM((10, STEPS, 128), F32),
            pltpu.VMEM((UNITS, UNITS), BF),
            pltpu.VMEM((UNITS, UNITS), BF),
            pltpu.VMEM((STEPS, 6, BATCH, QUARTER), BF),
            pltpu.VMEM((STEPS + 1, BATCH, QUARTER), F32),
            pltpu.VMEM((STEPS, BATCH, UNITS), BF),
            pltpu.VMEM((BATCH, 128), F32),
            pltpu.VMEM((BATCH, UNITS), F32),
            pltpu.VMEM((BATCH, QUARTER), F32),
            pltpu.VMEM((BATCH, QUARTER), F32),
            pltpu.VMEM((BATCH, QUARTER), F32),
            pltpu.VMEM((STEPS, 3, BATCH, QUARTER), BF),
            pltpu.VMEM((STEPS, 3, BATCH, QUARTER), BF),
            pltpu.SemaphoreType.DMA((len(KEYS),)),
            pltpu.SemaphoreType.DMA((len(KEYS),)),
            pltpu.SemaphoreType.DMA((STEPS + 1, 5)),
            pltpu.SemaphoreType.DMA((STEPS + 1, 5)),
            pltpu.SemaphoreType.DMA((STEPS, 5)),
            pltpu.SemaphoreType.DMA((STEPS, 5)),
            pltpu.SemaphoreType.DMA((len(KEYS),)),
            pltpu.SemaphoreType.DMA((len(KEYS),)),
            pltpu.SemaphoreType.DMA((10,)),
            pltpu.SemaphoreType.DMA((10,)),
            pltpu.SemaphoreType.REGULAR,
            pltpu.VMEM((BATCH, STEPS, 4, QUARTER), BF),
            pltpu.SemaphoreType.DMA(()),
            pltpu.SemaphoreType.DMA((13,)),
            pltpu.SemaphoreType.DMA((13,)),
            pltpu.SemaphoreType.DMA((13,)),
            pltpu.SemaphoreType.DMA((13,)),
        ],
        compiler_params=params(1),
        name="train",
    )(*operands)


def shards(
    rec_weight,
    head_weight,
    value_head,
    gate_inputs,
    start_state,
    advantages,
    returns,
    old_logprob,
    taken_action,
    episode_start,
    segment_counts,
    assignment,
):
    results = train(
        rec_weight,
        head_weight,
        value_head[None],
        gate_inputs[0],
        start_state[0],
        segment_counts,
        episode_start[0].T,
        advantages[0].T,
        returns[0].T,
        old_logprob[0].T,
        taken_action[0].T,
        assignment,
    )
    rec_share, policy_share, value_share, values = hand_on(*results)
    return (rec_share, policy_share, value_share[0], values.T[None])


def solution(mesh):
    placed = (
        P("learn", None, "actor"),
        P("learn", None),
        P("learn"),
        P("learn", None, None, None, "actor"),
        P("learn", None, None, "actor"),
        P("learn", None, None),
        P("learn", None, None),
        P("learn", None, None),
        P("learn", None, None),
        P("learn", None, None),
        P(),
        P("learn", None),
    )
    return jax.shard_map(
        shards,
        mesh=mesh,
        in_specs=placed,
        out_specs=(P("learn", None, "actor"), P("learn", None), P("learn"), P("learn", None, None)),
        check_vma=False,
    )
```
